256 devices in a mesh: grp: 8 (over y, core), dev: 32 (over x, z).
Axes of the slice: x: 4, y: 4, z: 8, core: 2. Of those that a mesh axis runs over, the one named last changes fastest.
Arguments:
- velocity: float32 [3, 512, 65536], P(None, None, ('grp', 'dev'))
- density: float32 [512, 65536], P(None, ('grp', 'dev')), may hold values from 0.1 to 3
- inverse_density: float32 [512, 65536], P(None, ('grp', 'dev')), may hold values from 0.25 to 4
- neighbours: int32 [6, 65536], P(None, ('grp', 'dev')), may hold values from -1 to 65535, as said below
- leaf_layer: int32 [65536], P(('grp', 'dev')), may hold values from 0 to 63, as said below
- leaf_tile: int32 [65536, 1], P(('grp', 'dev')), may hold values from 0 to 31; in each aligned block of 256 rows (0 to 255, 256 to 511, ...) at most 16 rows name the same one
- leaf_block: int32 [65536], P(('grp', 'dev')), may hold values from 0 to 255
- samples: int32 [32], replicated, may hold values from 1 to 64
Outputs:
- projected_velocity: float32 [3, 512, 65536], P(None, None, ('grp', 'dev'))
- rendered: float32 [32, 16384], P('dev', 'grp')
The draws below stay inside these ranges and needn't reach their ends.
Inputs may be any that keep to these rules, and one draw needn't show every extreme that they name: `neighbours`: A neighbour in direction -x or +x lies on the same device or on the device with dev index one lower or higher in the same group; one in -y or +y on the same device or on the device with the same dev index in the group one lower or higher; one in -z or +z on the same device. The relation is symmetric: leaf m is beside l in direction f exactly when l is beside m in the opposite direction. A device's leaves are distinct places of a brick of 8 x 8 x 8 leaf places. `leaf_layer`: the layer of a leaf of group g lies in g * 8 to g * 8 + 7. `leaf_tile`: among the 256 leaves of one device, no tile is named by more than 16, a bound that some block reaches.
All inputs are finite; a program needn't handle non-finite values.
Results may differ from the reference program's by a relative error of at most 0.0001.
Values sent between devices are 32-bit elements; how exact they have to be, the bound alone decides.
A program may use at most 64 MiB of HBM per device.

```python
import math
import jax
import jax.numpy as jnp
import numpy as np

LEAF_DEV = 256
BX = 8
BY = 8
BZ = 8
LEAF_VOX = 512
ITERS = 3
BLOCKS = 256
TILES = 32
CAP = 16
LEAVES = 65536
NLAYERS = 64
N_GRP = 8
N_DEV = 32


def leaf_geometry(key):
    device_count = N_GRP * N_DEV
    places = BX * BY * BZ
    key_list = jax.random.split(key, device_count)
    shuffled = jax.vmap(lambda sub_key: jax.random.permutation(sub_key, places))(key_list)
    chosen = jnp.sort(shuffled[:, :LEAF_DEV], axis=1).astype(jnp.int32)
    device_ids = jnp.broadcast_to(jnp.arange(device_count, dtype=jnp.int32)[:, None], chosen.shape)
    slot_ids = jnp.broadcast_to(jnp.arange(LEAF_DEV, dtype=jnp.int32)[None, :], chosen.shape)
    slot_map = jnp.full((device_count, places), -1, jnp.int32).at[device_ids, chosen].set(slot_ids)
    leaf_x = chosen // (BY * BZ)
    leaf_y = chosen // BZ % BY
    leaf_z = chosen % BZ
    group_of = device_ids // N_DEV
    member_of = device_ids % N_DEV
    neighbour_rows = []
    for axis_id, offset in ((0, -1), (0, 1), (1, -1), (1, 1), (2, -1), (2, 1)):
        next_x = leaf_x + offset * int(axis_id == 0)
        next_y = leaf_y + offset * int(axis_id == 1)
        next_z = leaf_z + offset * int(axis_id == 2)
        member_next = member_of + jnp.where(next_x < 0, -1, 0) + jnp.where(next_x >= BX, 1, 0)
        group_next = group_of + jnp.where(next_y < 0, -1, 0) + jnp.where(next_y >= BY, 1, 0)
        inside = (member_next >= 0) & (member_next < N_DEV) & (group_next >= 0) & (group_next < N_GRP)
        inside = inside & (next_z >= 0) & (next_z < BZ)
        target = jnp.clip(group_next, 0, N_GRP - 1) * N_DEV + jnp.clip(member_next, 0, N_DEV - 1)
        place = next_x % BX * (BY * BZ) + next_y % BY * BZ + jnp.clip(next_z, 0, BZ - 1)
        found = slot_map[target, place]
        linked = inside & (found >= 0)
        neighbour_rows.append(jnp.where(linked, target * LEAF_DEV + found, -1).reshape(-1).astype(jnp.int32))
    layers = (group_of * BY + leaf_y).reshape(-1).astype(jnp.int32)
    return (jnp.stack(neighbour_rows), layers)


def draw_neighbours(key, part):
    neighbour_table, layer_list = leaf_geometry(key)
    return neighbour_table


def draw_leaf_layer(key, part):
    neighbour_table, layer_list = leaf_geometry(key)
    return layer_list


def draw_velocity(key, part):
    key = jax.random.fold_in(key, 7)
    column_count = LEAF_DEV * N_GRP * N_DEV
    device_rank = (jnp.arange(column_count) // LEAF_DEV).astype(jnp.float32)
    ramp_share = device_rank / max(N_GRP * N_DEV - 1, 1)
    leaf_scale = 10.0 ** jax.random.uniform(jax.random.fold_in(key, 1), (column_count,), jnp.float32)
    noise_part = jax.random.normal(jax.random.fold_in(key, 2), (3, LEAF_VOX, column_count), jnp.float32)
    return noise_part * 0.15 * leaf_scale * 3.0 ** ramp_share


def set_ends(result, stream_key, least, largest):
    shape = result.shape
    spot = [jax.random.randint(jax.random.fold_in(stream_key, axis), (), 0, shape[axis]) for axis in range(len(shape))]
    result = result.at[tuple(spot)].set(least)
    longest = shape.index(max(shape))
    spot[longest] = (spot[longest] + 1) % shape[longest]
    return result.at[tuple(spot)].set(largest)


def levels(stream_key, shape, pieces, least, largest):
    level, own = 1.0, jax.random.fold_in(stream_key, 6)
    for position, shards_of in pieces:
        steps = jnp.exp(jax.random.uniform(jax.random.fold_in(own, position), (shards_of,), jnp.float32, least / len(pieces), largest / len(pieces)))
        level = level * jnp.repeat(steps, shape[position] // shards_of).reshape([-1 if axis == position else 1 for axis in range(len(shape))])
    return level


def assign_block(key, own, number, rows, number_of, top, bound, skew):
    sequence = jax.random.permutation(key, number_of)
    crowded, ordinary = shares(number_of, rows * top, bound, skew, True), shares(number_of, rows * top, bound, skew, False)
    places = jnp.arange(number_of)

    def named(sizes, rotation):
        used = int((sizes > 0).sum())
        fixed = max(1, used // 4)
        passed = fixed + (places - fixed + rotation * (used - fixed)) % max(1, number_of - fixed)
        return jnp.zeros((number_of,), jnp.int32).at[sequence[jnp.where(places < fixed, places, passed)]].set(jnp.asarray(sizes, jnp.int32))

    sizes = jnp.where(number % 4 == 0, named(crowded, number // 4), named(ordinary, number - number // 4 - 1))
    mixed = jax.random.permutation(jax.random.fold_in(own, 3), number_of)
    source_of, taker = mixed[0:number_of // 2 * 2:2], mixed[1:number_of // 2 * 2:2]
    slack = jnp.minimum(sizes[source_of] - 1, bound - sizes[taker]) // 2
    slack = jnp.where((source_of == sequence[0]) | (taker == sequence[0]) | (sizes[taker] == 0), 0, jnp.maximum(slack, 0))
    passed = jax.random.randint(jax.random.fold_in(own, 4), (number_of // 2,), 0, 1 << 20) % (slack + 1)
    sizes = sizes.at[source_of].add(-passed).at[taker].add(passed)
    members = jnp.searchsorted(jnp.cumsum(sizes), jnp.arange(rows * top), side="right").astype(jnp.int32)
    table = members.reshape(top, rows).T
    table = table[jax.random.permutation(jax.random.fold_in(own, 1), rows)]
    rotation = jax.random.randint(jax.random.fold_in(own, 2), (rows, 1), 0, top)
    return jnp.take_along_axis(table, (jnp.arange(top)[None, :] + rotation) % top, axis=1)


def shares(count, total, bound, skew, full):
    loads = [(1 << 20) // math.isqrt(grade ** skew) + 1 for grade in range(1, count + 1)]
    largest = bound if full else min(bound, max(-(-total // count), total * loads[0] // sum(loads)))
    least = 1 if total - largest >= count - 1 else 0
    given, rest = [largest] + [least] * (count - 1), total - largest - least * (count - 1)
    while rest > 0:
        movable = [i for i in range(1, count) if given[i] < largest] or [i for i in range(1, count) if given[i] < bound]
        pool, left = sum([loads[i] for i in movable]), rest
        for i in movable:
            extra = min(bound - given[i], max(1, left * loads[i] // pool), rest)
            given[i] = given[i] + extra
            rest = rest - extra
    return np.array(given)


def setup_inputs(seed: int = 0) -> dict:
    streams_of = jax.random.split(jax.random.key(seed), 9)
    velocity = draw_velocity(jax.random.fold_in(streams_of[8], 71), 0)
    density = jnp.clip(jnp.exp(math.log(3.0) - 3.4011974 * jax.random.uniform(streams_of[1], (LEAF_VOX, LEAVES), jnp.float32) ** levels(streams_of[1], (LEAF_VOX, LEAVES), ((1, 256),), -0.2, 0.2)), 0.1, 3.0)
    inverse_density = jnp.clip(jnp.exp(math.log(4.0) - 2.7725887 * jax.random.uniform(streams_of[2], (LEAF_VOX, LEAVES), jnp.float32) ** levels(streams_of[2], (LEAF_VOX, LEAVES), ((1, 256),), -0.2, 0.2)), 0.25, 4.0)
    neighbours = draw_neighbours(jax.random.fold_in(streams_of[8], 71), 0)
    leaf_layer = draw_leaf_layer(jax.random.fold_in(streams_of[8], 71), 0)
    leaf_tile_keys = jax.random.split(jax.random.fold_in(streams_of[5], 1), LEAVES // LEAF_DEV)
    leaf_tile_turns = jax.random.permutation(jax.random.fold_in(streams_of[5], 3), LEAVES // LEAF_DEV)
    leaf_tile = jax.vmap(lambda own, number: assign_block(jax.random.fold_in(streams_of[5], 2), own, number, LEAF_DEV, TILES, 1, CAP, 2))(leaf_tile_keys, leaf_tile_turns).reshape((LEAVES, 1))
    leaf_block = set_ends(jax.random.randint(streams_of[6], (LEAVES,), 0, BLOCKS), jax.random.fold_in(streams_of[6], 1), 0, BLOCKS - 1).astype(jnp.int32)
    samples = set_ends(jax.random.randint(streams_of[7], (TILES,), 1, NLAYERS + 1), jax.random.fold_in(streams_of[7], 1), 1, NLAYERS).astype(jnp.int32)
    return dict(velocity=velocity, density=density, inverse_density=inverse_density, neighbours=neighbours, leaf_layer=leaf_layer, leaf_tile=leaf_tile, leaf_block=leaf_block, samples=samples)


advect_step = 0.2
ray_step = 0.03


def neighbour_faces(first, second, third, neighbours):
    leaf_count = first.shape[-1]
    safe_index = jnp.maximum(neighbours, 0)
    present = neighbours >= 0
    tables = [first[7].reshape(64, leaf_count), first[0].reshape(64, leaf_count),
              second[:, 7].reshape(64, leaf_count), second[:, 0].reshape(64, leaf_count),
              third[:, :, 7].reshape(64, leaf_count), third[:, :, 0].reshape(64, leaf_count)]
    return [jnp.where(present[face_id][None, :], jnp.take(tables[face_id], safe_index[face_id], axis=1), 0.0)
            for face_id in range(6)]


def shifted(first, second, third, face_list):
    leaf_count = first.shape[-1]
    minus_x = jnp.concatenate([face_list[0].reshape(1, 8, 8, leaf_count), first[:-1]], axis=0)
    plus_x = jnp.concatenate([first[1:], face_list[1].reshape(1, 8, 8, leaf_count)], axis=0)
    minus_y = jnp.concatenate([face_list[2].reshape(8, 1, 8, leaf_count), second[:, :-1]], axis=1)
    plus_y = jnp.concatenate([second[:, 1:], face_list[3].reshape(8, 1, 8, leaf_count)], axis=1)
    minus_z = jnp.concatenate([face_list[4].reshape(8, 8, 1, leaf_count), third[:, :, :-1]], axis=2)
    plus_z = jnp.concatenate([third[:, :, 1:], face_list[5].reshape(8, 8, 1, leaf_count)], axis=2)
    return [minus_x, plus_x, minus_y, plus_y, minus_z, plus_z]


def beside_all(first, second, third, neighbours):
    return shifted(first, second, third, neighbour_faces(first, second, third, neighbours))


def reference(velocity, density, inverse_density, neighbours, leaf_layer, leaf_tile, leaf_block, samples):
    grid_shape = (8, 8, 8, LEAVES)
    inverse = inverse_density.reshape(grid_shape)
    dens_grid = density.reshape(grid_shape)
    velocity_grid = velocity.reshape((3,) + grid_shape)
    present = neighbours >= 0
    ones_grid = jnp.ones(grid_shape, jnp.float32)
    presence_faces = [jnp.broadcast_to(present[face_id][None, :].astype(jnp.float32), (64, LEAVES)) for face_id in range(6)]
    presence = shifted(ones_grid, ones_grid, ones_grid, presence_faces)
    inverse_near = beside_all(inverse, inverse, inverse, neighbours)
    coupling = [0.5 * (inverse + inverse_near[face_id]) + 0.5 * inverse * (1.0 - presence[face_id]) for face_id in range(6)]
    diagonal = coupling[0] + coupling[1] + coupling[2] + coupling[3] + coupling[4] + coupling[5]

    def operate(values):
        near_list = beside_all(values, values, values, neighbours)
        total = diagonal * values
        for face_id in range(6):
            total = total - coupling[face_id] * near_list[face_id]
        return total

    vel_near = beside_all(velocity_grid[0], velocity_grid[1], velocity_grid[2], neighbours)
    source = -0.5 * ((vel_near[1] - vel_near[0]) + (vel_near[3] - vel_near[2]) + (vel_near[5] - vel_near[4]))
    pressure = jnp.zeros(grid_shape, jnp.float32)
    residual = source
    precond = residual / diagonal
    energy = jnp.sum(residual * precond)
    direction = precond
    for iteration in range(ITERS):
        image_dir = operate(direction)
        step_size = energy / jnp.sum(direction * image_dir)
        pressure = pressure + step_size * direction
        residual = residual - step_size * image_dir
        if iteration + 1 < ITERS:
            precond = residual / diagonal
            fresh = jnp.sum(residual * precond)
            direction = precond + (fresh / energy) * direction
            energy = fresh
    press_near = beside_all(pressure, pressure, pressure, neighbours)
    gradient = jnp.stack([press_near[1] - press_near[0], press_near[3] - press_near[2], press_near[5] - press_near[4]]) * 0.5
    new_velocity = velocity_grid - inverse[None] * gradient
    flux = dens_grid[None] * new_velocity
    flux_near = beside_all(flux[0], flux[1], flux[2], neighbours)
    change = 0.5 * ((flux_near[1] - flux_near[0]) + (flux_near[3] - flux_near[2]) + (flux_near[5] - flux_near[4]))
    advected = dens_grid - advect_step * change
    column = ray_step * jnp.sum(advected, axis=1).reshape(64, LEAVES)
    tile_ids = leaf_tile[:, 0]
    marched = (leaf_layer < jnp.take(samples, tile_ids)).astype(jnp.float32)
    column = column * marched[None, :]
    segment_ids = tile_ids * BLOCKS + leaf_block
    summed = jax.ops.segment_sum(column.T, segment_ids, num_segments=TILES * BLOCKS)
    optical = summed.reshape(TILES, BLOCKS, 64).transpose(0, 2, 1).reshape(TILES, 64 * BLOCKS)
    rendered = 1.0 - jnp.exp(-optical)
    return new_velocity.reshape(3, LEAF_VOX, LEAVES), rendered
```

```python
import functools

import jax
import jax.numpy as jnp
from jax import lax
from jax.experimental import pallas as pl
from jax.experimental.pallas import tpu as pltpu
from jax.sharding import PartitionSpec as P

BLOCKS = 256
advect_step = 0.2
ray_step = 0.03
L = 256
FACE = 64
CAP = 16
F32 = jnp.float32
BF16 = jnp.bfloat16
MESH = pl.DeviceIdType.MESH


def parts(x):
    hi = x.astype(BF16)
    rest = x - hi.astype(F32)
    mid = rest.astype(BF16)
    low = (rest - mid.astype(F32)).astype(BF16)
    return jnp.concatenate([hi, mid, low], axis=0)


def joined(y):
    rows = y.shape[0] // 3
    return y[:rows] + y[rows : 2 * rows] + y[2 * rows :]


def pick(x, hot):
    return joined(jnp.dot(parts(x), hot, preferred_element_type=F32))


def pick_t(x, hot):
    return joined(
        lax.dot_general(parts(x), hot, (((1,), (1,)), ((), ())), preferred_element_type=F32)
    )


def spread(row, rows):
    return jnp.broadcast_to(row, (rows, row.shape[1]))


def hot_of(condition):
    return jnp.where(condition, 1.0, 0.0).astype(BF16)


def kernel(
    n_grp,
    n_dev,
    vel,
    dens,
    inv,
    nbr,
    layer,
    tile,
    block,
    samples,
    newv,
    rendered,
    wp,
    vx,
    vy,
    vz,
    dn,
    q,
    zf,
    zt,
    cs,
    dg,
    pp,
    gl,
    gr,
    cp,
    er,
    r1,
    rf,
    sb,
    rb,
    a1s,
    a1r,
    a2s,
    a2r,
    ids,
    idr,
    das,
    dar,
    ims,
    imr,
    sx,
    fy,
    sz,
    sd,
    col,
    in_sem,
    hs_sem,
    hr_sem,
    gs_sem,
    gr_sem,
    ds_sem,
    dr_sem,
):
    g = lax.axis_index("grp")
    d = lax.axis_index("dev")
    me = g * n_dev + d

    def grp_at(step):
        return (lax.rem(g + step, n_grp), d)

    def dev_at(step):
        return (g, lax.rem(d + step, n_dev))

    barrier = pltpu.get_barrier_semaphore()

    @pl.loop(1, n_dev)
    def _(i):
        pl.semaphore_signal(barrier, inc=1, device_id=dev_at(i), device_id_type=MESH)

    @pl.loop(1, n_grp)
    def _(i):
        pl.semaphore_signal(barrier, inc=1, device_id=grp_at(i), device_id_type=MESH)

    loads = [
        pltpu.make_async_copy(inv, wp.at[pl.ds(1, 8), pl.ds(1, 8)], in_sem.at[0]),
        pltpu.make_async_copy(vel.at[0], vx.at[pl.ds(1, 8)], in_sem.at[1]),
        pltpu.make_async_copy(vel.at[1], vy.at[:, pl.ds(1, 8)], in_sem.at[2]),
        pltpu.make_async_copy(vel.at[2], vz, in_sem.at[3]),
        pltpu.make_async_copy(dens, dn, in_sem.at[4]),
    ]
    for load in loads:
        load.start()

    pl.semaphore_wait(barrier, n_dev - 1 + n_grp - 1)

    to = [dev_at(1), dev_at(n_dev - 1), grp_at(1), grp_at(n_grp - 1)]

    def halo(number, face, src, dst):
        return pltpu.make_async_remote_copy(
            src_ref=src,
            dst_ref=dst,
            send_sem=hs_sem.at[number, face],
            recv_sem=hr_sem.at[number, face],
            device_id=to[face],
            device_id_type=MESH,
        )

    raw = []
    for which, field in enumerate((inv, vel, dens)):
        x_field = vel.at[0] if which == 1 else field
        y_field = vel.at[1] if which == 1 else field
        raw.append(
            [
                halo(which, 0, x_field.at[7], r1.at[0, which]),
                halo(which, 1, x_field.at[0], r1.at[1, which]),
                halo(which, 2, y_field.at[:, 7], r1.at[2, which]),
                halo(which, 3, y_field.at[:, 0], r1.at[3, which]),
            ]
        )
        for copy in raw[-1]:
            copy.start()

    table = nbr[...]
    present = table >= 0
    local = present & ((table // L) == me)
    remote = present & ((table // L) != me)
    slot = table % L
    local_slot = jnp.where(local, slot, -1)
    remote_slot = jnp.where(remote, slot, -1)
    sub = lax.broadcasted_iota(jnp.int32, (L, L), 0)
    lane = lax.broadcasted_iota(jnp.int32, (L, L), 1)
    upper = hot_of(sub < lane)
    sub128 = lax.broadcasted_iota(jnp.int32, (2 * FACE, L), 0)
    for face in range(6):
        gl[face] = hot_of(sub == spread(local_slot[face : face + 1], L))
    tile_row = tile[...]
    tile_hot = hot_of(
        lax.broadcasted_iota(jnp.int32, (n_dev, L), 0) == spread(tile_row, n_dev)
    )
    remote_hot = hot_of(remote)
    before = jnp.dot(
        jnp.concatenate([tile_hot, remote_hot, jnp.zeros((10, L), BF16)], axis=0),
        upper,
        preferred_element_type=F32,
    )
    for face in range(4):
        mine = remote_slot[face : face + 1]
        hot = jnp.where(sub == spread(mine, L), 1.0, 0.0)
        gr[face] = hot.astype(BF16)
        occupied = jnp.sum(hot, axis=1, keepdims=True)
        rank = jnp.sum(
            jnp.where(sub < spread(mine, L), occupied, 0.0), axis=0, keepdims=True
        ).astype(jnp.int32)
        rank = jnp.where(mine >= 0, rank, -1000)
        er[face, 0] = hot_of(sub128 == spread(rank, 2 * FACE))
        er[face, 1] = hot_of(sub128 == spread(rank + FACE, 2 * FACE))
        out_face = face ^ 1
        place = before[n_dev + out_face : n_dev + out_face + 1].astype(jnp.int32)
        place = jnp.where(remote_slot[out_face : out_face + 1] >= 0, place, -1000)
        cp[face, 0] = hot_of(sub128 == spread(place, 2 * FACE))
        cp[face, 1] = hot_of(sub128 == spread(place + FACE, 2 * FACE))

    rank = jnp.sum(
        jnp.where(tile_hot > 0, before[:n_dev], 0.0), axis=0, keepdims=True
    ).astype(jnp.int32)
    rows = n_dev * 8
    sub_key = lax.broadcasted_iota(jnp.int32, (rows, L), 0)
    first_key = jnp.where(rank < 8, tile_row * 8 + rank, -1)
    second_key = jnp.where(rank >= 8, tile_row * 8 + rank - 8, -1)
    slot_hot = jnp.concatenate(
        [hot_of(sub_key == spread(first_key, rows)), hot_of(sub_key == spread(second_key, rows))],
        axis=1,
    )

    def packed(values):
        zero = jnp.zeros_like(values)
        return jnp.concatenate(
            [
                jnp.concatenate([values, zero], axis=1),
                jnp.concatenate([zero, values], axis=1),
            ],
            axis=0,
        )

    def into_slots(values):
        return lax.dot_general(
            slot_hot, packed(values), (((1,), (1,)), ((), ())), preferred_element_type=F32
        )

    ids[...] = into_slots(spread(block[...], 64).astype(F32).astype(BF16)).reshape(n_dev, 8, 128)

    def to_dev(number, src, dst, i):
        return pltpu.make_async_remote_copy(
            src_ref=src,
            dst_ref=dst,
            send_sem=ds_sem.at[number, i],
            recv_sem=dr_sem.at[number, i],
            device_id=dev_at(i),
            device_id_type=MESH,
        )

    def to_grp(number, src, dst, i):
        return pltpu.make_async_remote_copy(
            src_ref=src,
            dst_ref=dst,
            send_sem=gs_sem.at[number, i],
            recv_sem=gr_sem.at[number, i],
            device_id=grp_at(i),
            device_id_type=MESH,
        )

    def ids_copy(i):
        return to_dev(0, ids.at[lax.rem(d + i, n_dev)], idr.at[i], i)

    @pl.loop(1, n_dev)
    def _(i):
        ids_copy(i).start()

    idr[0] = ids[d]
    limit = jnp.zeros((1, L), jnp.int32)
    for t in range(n_dev):
        limit = jnp.where(tile_row == t, samples[t], limit)
    marched = jnp.where(layer[...] < limit, ray_step, 0.0)

    for load in loads:
        load.wait()

    def flat(x):
        return x.reshape(FACE, L)

    def cube(x):
        return x.reshape(8, 8, L)

    def fill_z_tables(read):
        @pl.loop(0, 8)
        def _(i):
            for j in range(8):
                c = read(i, j)
                zt[0, i, j : j + 1, :] = c[7:8]
                zt[1, i, j : j + 1, :] = c[0:1]

    def local_faces(k):
        q[k, 0, 1:9] = cube(pick(flat(q[k, 8, 1:9]), gl[0]))
        q[k, 9, 1:9] = cube(pick(flat(q[k, 1, 1:9]), gl[1]))
        q[k, 1:9, 0] = cube(pick(flat(q[k, 1:9, 8]), gl[2]))
        q[k, 1:9, 9] = cube(pick(flat(q[k, 1:9, 1]), gl[3]))
        zf[2 * k] = cube(pick(flat(zt[0]), gl[4]))
        zf[2 * k + 1] = cube(pick(flat(zt[1]), gl[5]))

    fill_z_tables(lambda i, j: vz[i, j])
    zf[2] = cube(pick(flat(zt[0]), gl[4]))
    zf[3] = cube(pick(flat(zt[1]), gl[5]))
    fill_z_tables(lambda i, j: wp[i + 1, j + 1])
    absent = [jnp.where(present[face : face + 1], 0.0, 1.0) for face in range(6)]

    def both(first, second, face):
        return pick(jnp.concatenate([flat(first), flat(second)], axis=0), gl[face])

    near_local = [
        both(wp[8, 1:9], vx[8], 0),
        both(wp[1, 1:9], vx[1], 1),
        both(wp[1:9, 8], vy[:, 8], 2),
        both(wp[1:9, 1], vy[:, 1], 3),
    ]
    zf[0] = cube(pick(flat(zt[0]), gl[4]))
    zf[1] = cube(pick(flat(zt[1]), gl[5]))
    for which in range(3):
        for copy in raw[which]:
            copy.wait_recv()
    for face in range(4):
        got = pick(r1[face].reshape(3 * FACE, L), gr[face])
        rf[face] = got.reshape(3, 8, 8, L)
        near = near_local[face] + got[: 2 * FACE]
        w_near = cube(near[:FACE])
        v_near = cube(near[FACE:])
        if face == 0:
            wp[0, 1:9] = w_near + absent[face] * wp[1, 1:9]
            vx[0] = v_near
        elif face == 1:
            wp[9, 1:9] = w_near + absent[face] * wp[8, 1:9]
            vx[9] = v_near
        elif face == 2:
            wp[1:9, 0] = w_near + absent[face] * wp[1:9, 1]
            vy[:, 0] = v_near
        else:
            wp[1:9, 9] = w_near + absent[face] * wp[1:9, 8]
            vy[:, 9] = v_near

    k_id = lax.broadcasted_iota(jnp.int32, (8, L), 0)
    at_low = k_id == 0
    at_high = k_id == 7

    def beside_z(c, low, high):
        return (
            jnp.where(at_low, low, pltpu.roll(c, 1, 0)),
            jnp.where(at_high, high, pltpu.roll(c, 7, 0)),
        )

    def start_body(i, total):
        for j in range(8):
            c = wp[i + 1, j + 1]
            low, high = beside_z(
                c,
                zf[0, i, j : j + 1] + absent[4] * c[0:1],
                zf[1, i, j : j + 1] + absent[5] * c[7:8],
            )
            near = [wp[i, j + 1], wp[i + 2, j + 1], wp[i + 1, j], wp[i + 1, j + 2], low, high]
            coupling = [0.5 * (c + value) for value in near]
            diagonal = (
                coupling[0] + coupling[1] + coupling[2] + coupling[3] + coupling[4] + coupling[5]
            )
            inverse = 1.0 / diagonal
            dg[i, j] = diagonal
            for face in range(6):
                cs[face, i, j] = coupling[face] * inverse
            v = vz[i, j]
            low, high = beside_z(v, zf[2, i, j : j + 1], zf[3, i, j : j + 1])
            source = -0.5 * (
                (vx[i + 2, j] - vx[i, j]) + (vy[i, j + 2] - vy[i, j]) + (high - low)
            )
            value = source * inverse
            q[0, i + 1, j + 1] = value
            zt[0, i, j : j + 1, :] = value[7:8]
            zt[1, i, j : j + 1, :] = value[0:1]
            total = total + source * value
        return total

    zero = jnp.zeros((8, L), F32)
    moments = [lax.fori_loop(0, 8, start_body, zero)]

    def exchange(k):
        tables = [
            (flat(q[k, 8, 1:9]), flat(q[k, 7, 1:9])),
            (flat(q[k, 1, 1:9]), flat(q[k, 2, 1:9])),
            (flat(q[k, 1:9, 8]), flat(q[k, 1:9, 7])),
            (flat(q[k, 1:9, 1]), flat(q[k, 1:9, 2])),
        ]
        copies = []
        for face in range(4):
            sb[k, face] = pick_t(tables[face][0], cp[face, 0]) + pick_t(
                tables[face][1], cp[face, 1]
            )
            copies.append(halo(3 + k, face, sb.at[k, face], rb.at[k, face]))
            copies[-1].start()
        local_faces(k)
        for copy in copies:
            copy.wait_recv()
        q[k, 0, 1:9] += cube(pick(rb[k, 0], er[0, 0]))
        q[k, 9, 1:9] += cube(pick(rb[k, 1], er[1, 0]))
        q[k, 1:9, 0] += cube(pick(rb[k, 2], er[2, 0]))
        q[k, 1:9, 9] += cube(pick(rb[k, 3], er[3, 0]))
        return copies

    def apply(k):
        def body(i, totals):
            odd, even = totals
            for j in range(8):
                c = q[k, i + 1, j + 1]
                low, high = beside_z(c, zf[2 * k, i, j : j + 1], zf[2 * k + 1, i, j : j + 1])
                near = [
                    q[k, i, j + 1],
                    q[k, i + 2, j + 1],
                    q[k, i + 1, j],
                    q[k, i + 1, j + 2],
                    low,
                    high,
                ]
                value = c
                for face in range(6):
                    value = value - cs[face, i, j] * near[face]
                scaled = dg[i, j] * value
                odd = odd + c * scaled
                if k < 2:
                    even = even + value * scaled
                    q[k + 1, i + 1, j + 1] = value
                    zt[0, i, j : j + 1, :] = value[7:8]
                    zt[1, i, j : j + 1, :] = value[0:1]
            return odd, even

        return lax.fori_loop(0, 8, body, (zero, zero))

    sent = []
    for k in range(3):
        sent += exchange(k)
        odd, even = apply(k)
        moments += [odd, even]
    moments = moments[:6]

    a1s[...] = jnp.zeros((8, 128), F32)
    for k in range(6):
        line = jnp.sum(moments[k], axis=0, keepdims=True)
        a1s[k : k + 1, :] = line[:, :128] + line[:, 128:]

    for i in range(1, n_grp):
        to_grp(0, a1s, a1r.at[i], i).start()
    partial = a1s[...]
    for i in range(1, n_grp):
        to_grp(0, a1s, a1r.at[i], i).wait_recv()
        partial = partial + a1r[i]
    a2s[...] = partial

    @pl.loop(1, n_dev)
    def _(i):
        to_dev(1, a2s, a2r.at[i], i).start()

    @pl.loop(1, n_dev)
    def _(i):
        to_dev(1, a2s, a2r.at[i], i).wait_recv()

    whole = partial
    for i in range(1, n_dev):
        whole = whole + a2r[i]
    m = jnp.broadcast_to(jnp.sum(whole, axis=1, keepdims=True), (8, 128))
    m = [m[k : k + 1] for k in range(6)]
    l10 = m[2] / m[1]
    l20 = m[3] / m[1]
    d1 = m[3] - l10 * m[2]
    t21 = m[4] - l20 * m[2]
    l21 = t21 / d1
    d2 = m[5] - l20 * m[3] - l21 * t21
    y1 = m[1] - l10 * m[0]
    y2 = m[2] - l20 * m[0] - l21 * y1
    c2 = y2 / d2
    c1 = y1 / d1 - l21 * c2
    c0 = m[0] / m[1] - l10 * c1 - l20 * c2
    coefs = [jnp.concatenate([spread(c, 8), spread(c, 8)], axis=1) for c in (c0, c1, c2)]
    narrow = [spread(c, 8) for c in (c0, c1, c2)]

    def mixed(read):
        return coefs[0] * read(0) + coefs[1] * read(1) + coefs[2] * read(2)

    @pl.loop(0, 8)
    def _(i):
        pp[0, i + 1] = mixed(lambda k: q[k, 0, i + 1])
        pp[9, i + 1] = mixed(lambda k: q[k, 9, i + 1])
        zf[0, i] = mixed(lambda k: zf[2 * k, i])
        zf[1, i] = mixed(lambda k: zf[2 * k + 1, i])
        for j in range(10):
            pp[i + 1, j] = mixed(lambda k: q[k, i + 1, j])

    def far(face):
        deep = jnp.zeros((FACE, 128), F32)
        for k in range(3):
            deep = deep + jnp.broadcast_to(narrow[k][0:1], (FACE, 128)) * rb[k, face]
        deep = cube(pick(deep, er[face, 1]))
        if face == 0:
            change = pp[1, 1:9] - deep
        elif face == 1:
            change = deep - pp[8, 1:9]
        elif face == 2:
            change = pp[1:9, 1] - deep
        else:
            change = deep - pp[1:9, 8]
        return rf[face, 2] * (rf[face, 1] - 0.5 * rf[face, 0] * change)

    sx[0] = jnp.sum(far(0), axis=0)
    sx[9] = jnp.sum(far(1), axis=0)
    fy[0] = far(2)
    fy[3] = far(3)

    @pl.loop(0, 8)
    def _(i):
        sum_x = zero
        sum_z = zero
        sum_d = zero
        for j in range(8):
            c = pp[i + 1, j + 1]
            low, high = beside_z(c, zf[0, i, j : j + 1], zf[1, i, j : j + 1])
            half = 0.5 * wp[i + 1, j + 1]
            n_x = vx[i + 1, j] - half * (pp[i + 2, j + 1] - pp[i, j + 1])
            n_y = vy[i, j + 1] - half * (pp[i + 1, j + 2] - pp[i + 1, j])
            n_z = vz[i, j] - half * (high - low)
            newv[0, i, j] = n_x
            newv[1, i, j] = n_y
            newv[2, i, j] = n_z
            smoke = dn[i, j]
            sum_x = sum_x + smoke * n_x
            sum_z = sum_z + smoke * n_z
            sum_d = sum_d + smoke
            if j == 0:
                fy[1, i] = smoke * n_y
            if j == 7:
                fy[2, i] = smoke * n_y
        sx[i + 1] = sum_x
        sz[i] = sum_z
        sd[i] = sum_d
        zt[0, 0, pl.ds(i, 1), :] = sum_z[7:8]
        zt[1, 0, pl.ds(i, 1), :] = sum_z[0:1]

    fy[0] += cube(pick(flat(fy[2]), gl[2]))
    fy[3] += cube(pick(flat(fy[1]), gl[3]))
    both_x = jnp.concatenate([sx[8], sx[8]], axis=0)
    sx[0] += pick(both_x, gl[0])[:8]
    both_x = jnp.concatenate([sx[1], sx[1]], axis=0)
    sx[9] += pick(both_x, gl[1])[:8]
    z_low = pick(jnp.concatenate([zt[0, 0], zt[0, 0]], axis=0), gl[4])[:8]
    z_high = pick(jnp.concatenate([zt[1, 0], zt[1, 0]], axis=0), gl[5])[:8]
    for i in range(8):
        low, high = beside_z(sz[i], z_low[i : i + 1], z_high[i : i + 1])
        change = (
            (sx[i + 2] - sx[i]) + ((fy[3, i] + fy[2, i]) - (fy[1, i] + fy[0, i])) + (high - low)
        )
        col[8 * i : 8 * i + 8] = marched * (sd[i] - (0.5 * advect_step) * change)

    columns = parts(col[...])
    total = into_slots(columns[:64]) + into_slots(columns[64:128]) + into_slots(columns[128:])
    das[...] = total.reshape(n_dev, 8, 128)

    def data_copy(i):
        return to_dev(2, das.at[lax.rem(d + i, n_dev)], dar.at[i], i)

    @pl.loop(1, n_dev)
    def _(i):
        data_copy(i).start()

    dar[0] = das[d]

    @pl.loop(1, n_dev)
    def _(i):
        ids_copy(i).wait_recv()

    marks = idr[...].reshape(rows, 128)
    lane_b = lax.broadcasted_iota(jnp.int32, (rows, BLOCKS), 1).astype(F32)
    first_hot = hot_of(marks[:, 0:1] == lane_b)
    second_hot = hot_of(marks[:, 64:65] == lane_b)

    @pl.loop(1, n_dev)
    def _(i):
        data_copy(i).wait_recv()

    got = parts(dar[...].reshape(rows, 128).T)
    image = joined(jnp.dot(got, first_hot, preferred_element_type=F32))[:64]
    image = image + joined(jnp.dot(got, second_hot, preferred_element_type=F32))[64:]
    ims[...] = image.reshape(8, 8, BLOCKS)

    def image_copy(i):
        return to_grp(1, ims.at[lax.rem(g + i, n_grp)], imr.at[i], i)

    for i in range(1, n_grp):
        image_copy(i).start()
    optical = ims[g]
    for i in range(1, n_grp):
        image_copy(i).wait_recv()
        optical = optical + imr[i]
    shade = 1.0 - jnp.exp(-optical)
    for row in range(8):
        rendered[:, BLOCKS * row : BLOCKS * (row + 1)] = shade[row : row + 1]

    for which in range(3):
        for copy in raw[which]:
            copy.wait_send()
    for copy in sent:
        copy.wait_send()
    for i in range(1, n_grp):
        to_grp(0, a1s, a1r.at[i], i).wait_send()
        image_copy(i).wait_send()

    @pl.loop(1, n_dev)
    def _(i):
        ids_copy(i).wait_send()
        to_dev(1, a2s, a2r.at[i], i).wait_send()
        data_copy(i).wait_send()


def solution(mesh):
    n_grp, n_dev = mesh.shape["grp"], mesh.shape["dev"]

    def step(
        velocity, density, inverse_density, neighbours, leaf_layer, leaf_tile, leaf_block, samples
    ):
        vmem = pl.BlockSpec(memory_space=pltpu.VMEM)
        anywhere = pl.BlockSpec(memory_space=pl.ANY)
        smem = pl.BlockSpec(memory_space=pltpu.SMEM)
        new_velocity, rendered = pl.pallas_call(
            functools.partial(kernel, n_grp, n_dev),
            out_shape=(
                jax.ShapeDtypeStruct((3, 8, 8, 8, L), F32),
                jax.ShapeDtypeStruct((1, 8 * BLOCKS), F32),
            ),
            in_specs=[anywhere] * 3 + [vmem] * 4 + [smem],
            out_specs=(vmem, vmem),
            scratch_shapes=[
                pltpu.VMEM((10, 10, 8, L), F32),
                pltpu.VMEM((10, 8, 8, L), F32),
                pltpu.VMEM((8, 10, 8, L), F32),
                pltpu.VMEM((8, 8, 8, L), F32),
                pltpu.VMEM((8, 8, 8, L), F32),
                pltpu.VMEM((3, 10, 10, 8, L), F32),
                pltpu.VMEM((6, 8, 8, L), F32),
                pltpu.VMEM((2, 8, 8, L), F32),
                pltpu.VMEM((6, 8, 8, 8, L), F32),
                pltpu.VMEM((8, 8, 8, L), F32),
                pltpu.VMEM((10, 10, 8, L), F32),
                pltpu.VMEM((6, L, L), BF16),
                pltpu.VMEM((4, L, L), BF16),
                pltpu.VMEM((4, 2, 2 * FACE, L), BF16),
                pltpu.VMEM((4, 2, 2 * FACE, L), BF16),
                pltpu.VMEM((4, 3, 8, 8, L), F32),
                pltpu.VMEM((4, 3, 8, 8, L), F32),
                pltpu.VMEM((3, 4, FACE, 128), F32),
                pltpu.VMEM((3, 4, FACE, 128), F32),
                pltpu.VMEM((8, 128), F32),
                pltpu.VMEM((n_grp, 8, 128), F32),
                pltpu.VMEM((8, 128), F32),
                pltpu.VMEM((n_dev, 8, 128), F32),
                pltpu.VMEM((n_dev, 8, 128), F32),
                pltpu.VMEM((n_dev, 8, 128), F32),
                pltpu.VMEM((n_dev, 8, 128), F32),
                pltpu.VMEM((n_dev, 8, 128), F32),
                pltpu.VMEM((8, 8, BLOCKS), F32),
                pltpu.VMEM((n_grp, 8, BLOCKS), F32),
                pltpu.VMEM((10, 8, L), F32),
                pltpu.VMEM((4, 8, 8, L), F32),
                pltpu.VMEM((8, 8, L), F32),
                pltpu.VMEM((8, 8, L), F32),
                pltpu.VMEM((64, L), F32),
                pltpu.SemaphoreType.DMA((5,)),
                pltpu.SemaphoreType.DMA((6, 4)),
                pltpu.SemaphoreType.DMA((6, 4)),
                pltpu.SemaphoreType.DMA((2, n_grp)),
                pltpu.SemaphoreType.DMA((2, n_grp)),
                pltpu.SemaphoreType.DMA((3, n_dev)),
                pltpu.SemaphoreType.DMA((3, n_dev)),
            ],
            compiler_params=pltpu.CompilerParams(
                collective_id=0, has_side_effects=True, vmem_limit_bytes=48 * 1024 * 1024
            ),
        )(
            velocity.reshape(3, 8, 8, 8, L),
            density.reshape(8, 8, 8, L),
            inverse_density.reshape(8, 8, 8, L),
            neighbours,
            leaf_layer.reshape(1, L),
            leaf_tile.reshape(1, L),
            leaf_block.reshape(1, L),
            samples,
        )
        return new_velocity.reshape(3, 512, L), rendered

    return jax.shard_map(
        step,
        mesh=mesh,
        in_specs=(
            P(None, None, ("grp", "dev")),
            P(None, ("grp", "dev")),
            P(None, ("grp", "dev")),
            P(None, ("grp", "dev")),
            P(("grp", "dev")),
            P(("grp", "dev"), None),
            P(("grp", "dev")),
            P(),
        ),
        out_specs=(P(None, None, ("grp", "dev")), P("dev", "grp")),
        check_vma=False,
    )
```

```python
import functools

import jax
import jax.numpy as jnp
from jax import lax
from jax.experimental import pallas as pl
from jax.experimental.pallas import tpu as pltpu
from jax.sharding import PartitionSpec as P

BLOCKS = 256
advect_step = 0.2
ray_step = 0.03
L = 256
FACE = 64
CAP = 16
F32 = jnp.float32
BF16 = jnp.bfloat16
MESH = pl.DeviceIdType.MESH


def parts(x):
    hi = x.astype(BF16)
    rest = x - hi.astype(F32)
    mid = rest.astype(BF16)
    low = (rest - mid.astype(F32)).astype(BF16)
    return jnp.concatenate([hi, mid, low], axis=0)


def joined(y):
    rows = y.shape[0] // 3
    return y[:rows] + y[rows : 2 * rows] + y[2 * rows :]


def pick(x, hot):
    return joined(jnp.dot(parts(x), hot, preferred_element_type=F32))


def pick_t(x, hot):
    return joined(
        lax.dot_general(parts(x), hot, (((1,), (1,)), ((), ())), preferred_element_type=F32)
    )


def spread(row, rows):
    return jnp.broadcast_to(row, (rows, row.shape[1]))


def hot_of(condition):
    return jnp.where(condition, 1.0, 0.0).astype(BF16)


def kernel(
    n_grp,
    n_dev,
    vel,
    dens,
    inv,
    nbr_any,
    layer_any,
    tile_any,
    block_any,
    samples,
    newv,
    rendered,
    nbr,
    rows_in,
    wp,
    vx,
    vy,
    vz,
    dn,
    hd,
    q,
    zf,
    zt,
    cs,
    dg,
    pp,
    gl,
    cp,
    er,
    rf,
    sb,
    rb,
    a1s,
    a1r,
    a2s,
    a2r,
    ids,
    idr,
    das,
    dar,
    ims,
    imr,
    sx,
    fy,
    sz,
    sd,
    col,
    in_sem,
    hs_sem,
    hr_sem,
    gs_sem,
    gr_sem,
    ds_sem,
    dr_sem,
):
    g = lax.axis_index("grp")
    d = lax.axis_index("dev")
    me = g * n_dev + d

    def grp_at(step):
        return (lax.rem(g + step, n_grp), d)

    def dev_at(step):
        return (g, lax.rem(d + step, n_dev))

    small = [
        pltpu.make_async_copy(nbr_any, nbr, in_sem.at[5]),
        pltpu.make_async_copy(tile_any, rows_in.at[0], in_sem.at[6]),
        pltpu.make_async_copy(block_any, rows_in.at[1], in_sem.at[7]),
        pltpu.make_async_copy(layer_any, rows_in.at[2], in_sem.at[8]),
    ]
    loads = [
        pltpu.make_async_copy(inv, wp.at[pl.ds(1, 8), pl.ds(1, 8)], in_sem.at[0]),
        pltpu.make_async_copy(vel.at[0], vx.at[pl.ds(1, 8)], in_sem.at[1]),
        pltpu.make_async_copy(vel.at[1], vy.at[:, pl.ds(1, 8)], in_sem.at[2]),
        pltpu.make_async_copy(dens, dn, in_sem.at[3]),
        pltpu.make_async_copy(vel.at[2], vz, in_sem.at[4]),
    ]
    for load in small + loads:
        load.start()

    to = [dev_at(1), dev_at(n_dev - 1), grp_at(1), grp_at(n_grp - 1)]
    sends = [d < n_dev - 1, d > 0, g < n_grp - 1, g > 0]
    takes = [d > 0, d < n_dev - 1, g > 0, g < n_grp - 1]

    for face in range(4):

        @pl.when(jnp.logical_not(takes[face]))
        def _():
            rb[:, face] = jnp.zeros((5, FACE, 128), F32)

    barrier = pltpu.get_barrier_semaphore()

    @pl.loop(1, n_grp)
    def _(i):
        pl.semaphore_signal(barrier, inc=1, device_id=grp_at(i), device_id_type=MESH)

    @pl.loop(1, n_dev)
    def _(i):
        pl.semaphore_signal(barrier, inc=1, device_id=dev_at(i), device_id_type=MESH)

    for load in small:
        load.wait()

    table = nbr[...]
    present = table >= 0
    local = present & ((table // L) == me)
    remote = present & ((table // L) != me)
    slot = table % L
    local_slot = jnp.where(local, slot, -1)
    remote_slot = jnp.where(remote, slot, -1)
    sub = lax.broadcasted_iota(jnp.int32, (L, L), 0)
    lane = lax.broadcasted_iota(jnp.int32, (L, L), 1)
    upper = hot_of(sub < lane)
    sub128 = lax.broadcasted_iota(jnp.int32, (2 * FACE, L), 0)
    tile_row = rows_in[0]
    tile_hot = hot_of(
        lax.broadcasted_iota(jnp.int32, (n_dev, L), 0) == spread(tile_row, n_dev)
    )
    before = jnp.dot(
        jnp.concatenate([tile_hot, hot_of(remote), jnp.zeros((10, L), BF16)], axis=0),
        upper,
        preferred_element_type=F32,
    )
    for face in range(4):
        out_face = face ^ 1
        place = before[n_dev + out_face : n_dev + out_face + 1].astype(jnp.int32)
        place = jnp.where(remote_slot[out_face : out_face + 1] >= 0, place, -1000)
        cp[face, 0] = hot_of(sub128 == spread(place, 2 * FACE))
        cp[face, 1] = hot_of(sub128 == spread(place + FACE, 2 * FACE))

    for load in loads[:4]:
        load.wait()

    def flat(x):
        return x.reshape(FACE, L)

    def cube(x):
        return x.reshape(8, 8, L)

    def halo(number, face):
        return pltpu.make_async_remote_copy(
            src_ref=sb.at[number, face],
            dst_ref=rb.at[number, face],
            send_sem=hs_sem.at[number, face],
            recv_sem=hr_sem.at[number, face],
            device_id=to[face],
            device_id_type=MESH,
        )

    def send_faces(number, first, second):
        for face in range(4):
            sb[number, face] = pick_t(flat(first[face]), cp[face, 0]) + pick_t(
                flat(second[face]), cp[face, 1]
            )

            @pl.when(sends[face])
            def _():
                halo(number, face).start()

    def take_faces(number):
        for face in range(4):

            @pl.when(takes[face])
            def _():
                halo(number, face).wait_recv()

    pl.semaphore_wait(barrier, n_dev - 1 + n_grp - 1)

    send_faces(
        3,
        [wp[8, 1:9], wp[1, 1:9], wp[1:9, 8], wp[1:9, 1]],
        [vx[8], vx[1], vy[:, 8], vy[:, 1]],
    )
    smoke_faces = [dn[7], dn[0], dn[:, 7], dn[:, 0]]
    send_faces(4, smoke_faces, smoke_faces)

    for face in range(6):
        gl[face] = hot_of(sub == spread(local_slot[face : face + 1], L))
    for face in range(4):
        mine = remote_slot[face : face + 1]
        occupied = jnp.sum(
            jnp.where(sub == spread(mine, L), 1.0, 0.0), axis=1, keepdims=True
        )
        rank = jnp.sum(
            jnp.where(sub < spread(mine, L), occupied, 0.0), axis=0, keepdims=True
        ).astype(jnp.int32)
        rank = jnp.where(mine >= 0, rank, -1000)
        er[face, 0] = hot_of(sub128 == spread(rank, 2 * FACE))
        er[face, 1] = hot_of(sub128 == spread(rank + FACE, 2 * FACE))

    rank = jnp.sum(
        jnp.where(tile_hot > 0, before[:n_dev], 0.0), axis=0, keepdims=True
    ).astype(jnp.int32)
    rows = n_dev * 8
    sub_key = lax.broadcasted_iota(jnp.int32, (rows, L), 0)
    first_key = jnp.where(rank < 8, tile_row * 8 + rank, -1)
    second_key = jnp.where(rank >= 8, tile_row * 8 + rank - 8, -1)
    slot_hot = jnp.concatenate(
        [hot_of(sub_key == spread(first_key, rows)), hot_of(sub_key == spread(second_key, rows))],
        axis=1,
    )

    def into_slots(values):
        empty = jnp.zeros_like(values)
        packed = jnp.concatenate(
            [
                jnp.concatenate([values, empty], axis=1),
                jnp.concatenate([empty, values], axis=1),
            ],
            axis=0,
        )
        return lax.dot_general(
            slot_hot, packed, (((1,), (1,)), ((), ())), preferred_element_type=F32
        )

    def to_dev(number, src, dst, i):
        return pltpu.make_async_remote_copy(
            src_ref=src,
            dst_ref=dst,
            send_sem=ds_sem.at[number, i],
            recv_sem=dr_sem.at[number, i],
            device_id=dev_at(i),
            device_id_type=MESH,
        )

    def to_grp(number, src, dst, i):
        return pltpu.make_async_remote_copy(
            src_ref=src,
            dst_ref=dst,
            send_sem=gs_sem.at[number, i],
            recv_sem=gr_sem.at[number, i],
            device_id=grp_at(i),
            device_id_type=MESH,
        )

    def ids_copy(i):
        return to_dev(0, ids.at[lax.rem(d + i, n_dev)], idr.at[i], i)

    def sum_copy(i):
        return to_dev(1, a2s, a2r.at[i], i)

    def data_copy(which, i):
        return to_dev(2 + which, das.at[which, lax.rem(d + i, n_dev)], dar.at[which, i], i)

    ids[...] = into_slots(spread(rows_in[1], 64).astype(F32).astype(BF16)).reshape(n_dev, 8, 128)

    @pl.loop(1, n_dev)
    def _(i):
        ids_copy(i).start()

    idr[0] = ids[d]
    limit = jnp.zeros((1, L), jnp.int32)
    for t in range(n_dev):
        limit = jnp.where(tile_row == t, samples[t], limit)
    marched = jnp.where(rows_in[2] < limit, ray_step, 0.0)

    loads[4].wait()

    def fill_z_tables(read):
        @pl.loop(0, 8)
        def _(i):
            for j in range(8):
                c = read(i, j)
                zt[0, i, j : j + 1, :] = c[7:8]
                zt[1, i, j : j + 1, :] = c[0:1]

    def local_faces(k):
        q[k, 0, 1:9] = cube(pick(flat(q[k, 8, 1:9]), gl[0]))
        q[k, 9, 1:9] = cube(pick(flat(q[k, 1, 1:9]), gl[1]))
        q[k, 1:9, 0] = cube(pick(flat(q[k, 1:9, 8]), gl[2]))
        q[k, 1:9, 9] = cube(pick(flat(q[k, 1:9, 1]), gl[3]))
        zf[2 * k] = cube(pick(flat(zt[0]), gl[4]))
        zf[2 * k + 1] = cube(pick(flat(zt[1]), gl[5]))

    fill_z_tables(lambda i, j: vz[i, j])
    zf[2] = cube(pick(flat(zt[0]), gl[4]))
    zf[3] = cube(pick(flat(zt[1]), gl[5]))
    fill_z_tables(lambda i, j: wp[i + 1, j + 1])
    absent = [jnp.where(present[face : face + 1], 0.0, 1.0) for face in range(6)]
    zf[0] = cube(pick(flat(zt[0]), gl[4]))
    zf[1] = cube(pick(flat(zt[1]), gl[5]))

    def both(first, second, face):
        return pick(jnp.concatenate([flat(first), flat(second)], axis=0), gl[face])

    near_local = [
        both(wp[8, 1:9], vx[8], 0),
        both(wp[1, 1:9], vx[1], 1),
        both(wp[1:9, 8], vy[:, 8], 2),
        both(wp[1:9, 1], vy[:, 1], 3),
    ]
    take_faces(3)
    for face in range(4):
        got = parts(rb[3, face])
        w_far = joined(jnp.dot(got, er[face, 0], preferred_element_type=F32))
        v_far = joined(jnp.dot(got, er[face, 1], preferred_element_type=F32))
        rf[face, 0] = cube(w_far)
        rf[face, 1] = cube(v_far)
        w_near = cube(near_local[face][:FACE] + w_far)
        v_near = cube(near_local[face][FACE:] + v_far)
        if face == 0:
            wp[0, 1:9] = w_near + absent[face] * wp[1, 1:9]
            vx[0] = v_near
        elif face == 1:
            wp[9, 1:9] = w_near + absent[face] * wp[8, 1:9]
            vx[9] = v_near
        elif face == 2:
            wp[1:9, 0] = w_near + absent[face] * wp[1:9, 1]
            vy[:, 0] = v_near
        else:
            wp[1:9, 9] = w_near + absent[face] * wp[1:9, 8]
            vy[:, 9] = v_near

    k_id = lax.broadcasted_iota(jnp.int32, (8, L), 0)
    at_low = k_id == 0
    at_high = k_id == 7
    zero = jnp.zeros((8, L), F32)

    def beside_z(c, low, high):
        return (
            jnp.where(at_low, low, pltpu.roll(c, 1, 0)),
            jnp.where(at_high, high, pltpu.roll(c, 7, 0)),
        )

    @pl.loop(0, 8)
    def _(i):
        for j in range(8):
            c = wp[i + 1, j + 1]
            low, high = beside_z(
                c,
                zf[0, i, j : j + 1] + absent[4] * c[0:1],
                zf[1, i, j : j + 1] + absent[5] * c[7:8],
            )
            near = [wp[i, j + 1], wp[i + 2, j + 1], wp[i + 1, j], wp[i + 1, j + 2], low, high]
            coupling = [0.5 * (c + value) for value in near]
            diagonal = (
                coupling[0] + coupling[1] + coupling[2] + coupling[3] + coupling[4] + coupling[5]
            )
            inverse = 1.0 / diagonal
            dg[i, j] = diagonal
            for face in range(6):
                cs[face, i, j] = coupling[face] * inverse
            v = vz[i, j]
            low, high = beside_z(v, zf[2, i, j : j + 1], zf[3, i, j : j + 1])
            source = -0.5 * (
                (vx[i + 2, j] - vx[i, j]) + (vy[i, j + 2] - vy[i, j]) + (high - low)
            )
            q[0, i + 1, j + 1] = source * inverse

    def send_field(k):
        send_faces(
            k,
            [q[k, 8, 1:9], q[k, 1, 1:9], q[k, 1:9, 8], q[k, 1:9, 1]],
            [q[k, 7, 1:9], q[k, 2, 1:9], q[k, 1:9, 7], q[k, 1:9, 2]],
        )

    send_field(0)

    def apply_local(k):
        @pl.loop(0, 8)
        def _(i):
            for j in range(8):
                c = q[k, i + 1, j + 1]
                low, high = beside_z(c, zf[2 * k, i, j : j + 1], zf[2 * k + 1, i, j : j + 1])
                near = [
                    q[k, i, j + 1],
                    q[k, i + 2, j + 1],
                    q[k, i + 1, j],
                    q[k, i + 1, j + 2],
                    low,
                    high,
                ]
                value = c
                for face in range(6):
                    value = value - cs[face, i, j] * near[face]
                q[k + 1, i + 1, j + 1] = value

    def add_far(k):
        far = [cube(pick(rb[k, face], er[face, 0])) for face in range(4)]
        q[k, 0, 1:9] += far[0]
        q[k, 9, 1:9] += far[1]
        q[k, 1:9, 0] += far[2]
        q[k, 1:9, 9] += far[3]
        q[k + 1, 1, 1:9] -= cs[0, 0] * far[0]
        q[k + 1, 8, 1:9] -= cs[1, 7] * far[1]
        q[k + 1, 1:9, 1] -= cs[2, :, 0] * far[2]
        q[k + 1, 1:9, 8] -= cs[3, :, 7] * far[3]

    def products(k):
        def body(i, totals):
            even, odd = totals
            for j in range(8):
                c = q[k, i + 1, j + 1]
                scaled = dg[i, j] * c
                even = even + c * scaled
                odd = odd + q[k + 1, i + 1, j + 1] * scaled
            return even, odd

        return lax.fori_loop(0, 8, body, (zero, zero))

    def read_z(k):
        return lambda i, j: q[k, i + 1, j + 1]

    def flux_columns(which):
        base = which == 0
        k = which - 1

        def far(face):
            if base:
                return rf[face, 2] * rf[face, 1]
            deep = cube(pick(rb[k, face], er[face, 1]))
            change = [
                lambda: q[k, 1, 1:9] - deep,
                lambda: deep - q[k, 8, 1:9],
                lambda: q[k, 1:9, 1] - deep,
                lambda: deep - q[k, 1:9, 8],
            ][face]()
            return rf[face, 3] * change

        sx[0] = jnp.sum(far(0), axis=0)
        sx[9] = jnp.sum(far(1), axis=0)
        fy[0] = far(2)
        fy[3] = far(3)

        @pl.loop(0, 8)
        def _(i):
            sum_x = zero
            sum_z = zero
            sum_d = zero
            for j in range(8):
                if base:
                    smoke = dn[i, j]
                    sum_x = sum_x + smoke * vx[i + 1, j]
                    sum_z = sum_z + smoke * vz[i, j]
                    sum_d = sum_d + smoke
                    if j == 0:
                        fy[1, i] = smoke * vy[i, 1]
                    if j == 7:
                        fy[2, i] = smoke * vy[i, 8]
                else:
                    half = hd[i, j]
                    low, high = beside_z(
                        q[k, i + 1, j + 1], zf[2 * k, i, j : j + 1], zf[2 * k + 1, i, j : j + 1]
                    )
                    sum_x = sum_x + half * (q[k, i + 2, j + 1] - q[k, i, j + 1])
                    sum_z = sum_z + half * (high - low)
                    if j == 0:
                        fy[1, i] = half * (q[k, i + 1, 2] - q[k, i + 1, 0])
                    if j == 7:
                        fy[2, i] = half * (q[k, i + 1, 9] - q[k, i + 1, 7])
            sx[i + 1] = sum_x
            sz[i] = sum_z
            if base:
                sd[i] = sum_d
            zt[0, 0, pl.ds(i, 1), :] = sum_z[7:8]
            zt[1, 0, pl.ds(i, 1), :] = sum_z[0:1]

        fy[0] += cube(pick(flat(fy[2]), gl[2]))
        fy[3] += cube(pick(flat(fy[1]), gl[3]))

        def pick_8(x, hot):
            return pick(jnp.concatenate([x, x], axis=0), hot)[:8]

        sx[0] += pick_8(sx[8], gl[0])
        sx[9] += pick_8(sx[1], gl[1])
        z_low = pick_8(zt[0, 0], gl[4])
        z_high = pick_8(zt[1, 0], gl[5])
        for i in range(8):
            low, high = beside_z(sz[i], z_low[i : i + 1], z_high[i : i + 1])
            change = (
                (sx[i + 2] - sx[i])
                + ((fy[3, i] + fy[2, i]) - (fy[1, i] + fy[0, i]))
                + (high - low)
            )
            change = (0.5 * advect_step) * change
            col[8 * i : 8 * i + 8] = marched * (sd[i] - change if base else change)
        columns = parts(col[...])
        total = into_slots(columns[:64]) + into_slots(columns[64:128]) + into_slots(columns[128:])
        das[which] = total.reshape(n_dev, 8, 128)

        @pl.loop(1, n_dev)
        def _(i):
            data_copy(which, i).start()

        dar[which, 0] = das[which, d]

    fill_z_tables(read_z(0))
    local_faces(0)
    apply_local(0)
    take_faces(4)
    for face in range(4):
        smoke_far = cube(pick(rb[4, face], er[face, 0]))
        rf[face, 2] = smoke_far
        rf[face, 3] = 0.5 * smoke_far * rf[face, 0]

    @pl.loop(0, 8)
    def _(i):
        for j in range(8):
            hd[i, j] = 0.5 * dn[i, j] * wp[i + 1, j + 1]

    flux_columns(0)
    take_faces(0)
    add_far(0)
    send_field(1)

    fill_z_tables(read_z(1))
    local_faces(1)
    apply_local(1)
    flux_columns(1)
    m0, m1 = products(0)
    take_faces(1)
    add_far(1)
    send_field(2)

    fill_z_tables(read_z(2))
    local_faces(2)
    apply_local(2)
    flux_columns(2)
    m2, m3 = products(1)
    m4, m5 = products(2)

    take_faces(2)
    far = [cube(pick(rb[2, face], er[face, 0])) for face in range(4)]
    m5_far = zero
    for j in range(8):
        m5_far = m5_far + dg[0, j] * cs[0, 0, j] * far[0][j] * q[2, 1, j + 1]
        m5_far = m5_far + dg[7, j] * cs[1, 7, j] * far[1][j] * q[2, 8, j + 1]
        m5_far = m5_far + dg[j, 0] * cs[2, j, 0] * far[2][j] * q[2, j + 1, 1]
        m5_far = m5_far + dg[j, 7] * cs[3, j, 7] * far[3][j] * q[2, j + 1, 8]

    moments = [m0, m1, m2, m3, m4, m5 - m5_far]
    a1s[...] = jnp.zeros((8, 128), F32)
    for k in range(6):
        line = jnp.sum(moments[k], axis=0, keepdims=True)
        a1s[k : k + 1, :] = line[:, :128] + line[:, 128:]
    for i in range(1, n_grp):
        to_grp(0, a1s, a1r.at[i], i).start()

    q[2, 0, 1:9] += far[0]
    q[2, 9, 1:9] += far[1]
    q[2, 1:9, 0] += far[2]
    q[2, 1:9, 9] += far[3]
    flux_columns(3)

    partial = a1s[...]
    for i in range(1, n_grp):
        to_grp(0, a1s, a1r.at[i], i).wait_recv()
        partial = partial + a1r[i]
    a2s[...] = partial

    @pl.loop(1, n_dev)
    def _(i):
        sum_copy(i).start()

    @pl.loop(1, n_dev)
    def _(i):
        ids_copy(i).wait_recv()

    marks = idr[...].reshape(rows, 128)
    lane_b = lax.broadcasted_iota(jnp.int32, (rows, BLOCKS), 1).astype(F32)
    first_hot = hot_of(marks[:, 0:1] == lane_b)
    second_hot = hot_of(marks[:, 64:65] == lane_b)

    @pl.loop(1, n_dev)
    def _(i):
        ids_copy(i).wait_send()
        for which in range(2):
            data_copy(which, i).wait_send()
            data_copy(which, i).wait_recv()

    @pl.loop(1, n_dev)
    def _(i):
        sum_copy(i).wait_recv()

    whole = partial
    for i in range(1, n_dev):
        whole = whole + a2r[i]
    m = jnp.broadcast_to(jnp.sum(whole, axis=1, keepdims=True), (8, 128))
    m = [m[k : k + 1] for k in range(6)]
    l10 = m[2] / m[1]
    l20 = m[3] / m[1]
    d1 = m[3] - l10 * m[2]
    t21 = m[4] - l20 * m[2]
    l21 = t21 / d1
    d2 = m[5] - l20 * m[3] - l21 * t21
    y1 = m[1] - l10 * m[0]
    y2 = m[2] - l20 * m[0] - l21 * y1
    c2 = y2 / d2
    c1 = y1 / d1 - l21 * c2
    c0 = m[0] / m[1] - l10 * c1 - l20 * c2
    coefs = [jnp.concatenate([spread(c, 8), spread(c, 8)], axis=1) for c in (c0, c1, c2)]

    @pl.loop(1, n_dev)
    def _(i):
        for which in range(2, 4):
            data_copy(which, i).wait_recv()

    columns = dar[0].reshape(rows, 128)
    for k, c in enumerate((c0, c1, c2)):
        columns = columns + spread(c, rows) * dar[k + 1].reshape(rows, 128)
    got = parts(columns.T)
    image = joined(jnp.dot(got, first_hot, preferred_element_type=F32))[:64]
    image = image + joined(jnp.dot(got, second_hot, preferred_element_type=F32))[64:]
    ims[...] = image.reshape(8, 8, BLOCKS)

    def image_copy(i):
        return to_grp(1, ims.at[lax.rem(g + i, n_grp)], imr.at[i], i)

    for i in range(1, n_grp):
        image_copy(i).start()

    def mixed(read):
        return coefs[0] * read(0) + coefs[1] * read(1) + coefs[2] * read(2)

    @pl.loop(0, 8)
    def _(i):
        pp[0, i + 1] = mixed(lambda k: q[k, 0, i + 1])
        pp[9, i + 1] = mixed(lambda k: q[k, 9, i + 1])
        zf[0, i] = mixed(lambda k: zf[2 * k, i])
        zf[1, i] = mixed(lambda k: zf[2 * k + 1, i])
        for j in range(10):
            pp[i + 1, j] = mixed(lambda k: q[k, i + 1, j])

    @pl.loop(0, 8)
    def _(i):
        for j in range(8):
            c = pp[i + 1, j + 1]
            low, high = beside_z(c, zf[0, i, j : j + 1], zf[1, i, j : j + 1])
            half = 0.5 * wp[i + 1, j + 1]
            newv[0, i, j] = vx[i + 1, j] - half * (pp[i + 2, j + 1] - pp[i, j + 1])
            newv[1, i, j] = vy[i, j + 1] - half * (pp[i + 1, j + 2] - pp[i + 1, j])
            newv[2, i, j] = vz[i, j] - half * (high - low)

    for number in range(5):
        for face in range(4):

            @pl.when(sends[face])
            def _():
                halo(number, face).wait_send()

    for i in range(1, n_grp):
        to_grp(0, a1s, a1r.at[i], i).wait_send()

    @pl.loop(1, n_dev)
    def _(i):
        sum_copy(i).wait_send()
        for which in range(2, 4):
            data_copy(which, i).wait_send()

    optical = ims[g]
    for i in range(1, n_grp):
        image_copy(i).wait_recv()
        optical = optical + imr[i]
    shade = 1.0 - jnp.exp(-optical)
    for row in range(8):
        rendered[:, BLOCKS * row : BLOCKS * (row + 1)] = shade[row : row + 1]
    for i in range(1, n_grp):
        image_copy(i).wait_send()


def solution(mesh):
    n_grp, n_dev = mesh.shape["grp"], mesh.shape["dev"]

    def step(
        velocity, density, inverse_density, neighbours, leaf_layer, leaf_tile, leaf_block, samples
    ):
        vmem = pl.BlockSpec(memory_space=pltpu.VMEM)
        anywhere = pl.BlockSpec(memory_space=pl.ANY)
        smem = pl.BlockSpec(memory_space=pltpu.SMEM)
        new_velocity, rendered = pl.pallas_call(
            functools.partial(kernel, n_grp, n_dev),
            out_shape=(
                pltpu.VMEM((3, 8, 8, 8, L), F32),
                pltpu.VMEM((1, 8 * BLOCKS), F32),
            ),
            in_specs=[anywhere] * 7 + [smem],
            out_specs=(vmem, vmem),
            scratch_shapes=[
                pltpu.VMEM((6, L), jnp.int32),
                pltpu.VMEM((3, 1, L), jnp.int32),
                pltpu.VMEM((10, 10, 8, L), F32),
                pltpu.VMEM((10, 8, 8, L), F32),
                pltpu.VMEM((8, 10, 8, L), F32),
                pltpu.VMEM((8, 8, 8, L), F32),
                pltpu.VMEM((8, 8, 8, L), F32),
                pltpu.VMEM((8, 8, 8, L), F32),
                pltpu.VMEM((4, 10, 10, 8, L), F32),
                pltpu.VMEM((6, 8, 8, L), F32),
                pltpu.VMEM((2, 8, 8, L), F32),
                pltpu.VMEM((6, 8, 8, 8, L), F32),
                pltpu.VMEM((8, 8, 8, L), F32),
                pltpu.VMEM((10, 10, 8, L), F32),
                pltpu.VMEM((6, L, L), BF16),
                pltpu.VMEM((4, 2, 2 * FACE, L), BF16),
                pltpu.VMEM((4, 2, 2 * FACE, L), BF16),
                pltpu.VMEM((4, 4, 8, 8, L), F32),
                pltpu.VMEM((5, 4, FACE, 128), F32),
                pltpu.VMEM((5, 4, FACE, 128), F32),
                pltpu.VMEM((8, 128), F32),
                pltpu.VMEM((n_grp, 8, 128), F32),
                pltpu.VMEM((8, 128), F32),
                pltpu.VMEM((n_dev, 8, 128), F32),
                pltpu.VMEM((n_dev, 8, 128), F32),
                pltpu.VMEM((n_dev, 8, 128), F32),
                pltpu.VMEM((4, n_dev, 8, 128), F32),
                pltpu.VMEM((4, n_dev, 8, 128), F32),
                pltpu.VMEM((8, 8, BLOCKS), F32),
                pltpu.VMEM((n_grp, 8, BLOCKS), F32),
                pltpu.VMEM((10, 8, L), F32),
                pltpu.VMEM((4, 8, 8, L), F32),
                pltpu.VMEM((8, 8, L), F32),
                pltpu.VMEM((8, 8, L), F32),
                pltpu.VMEM((64, L), F32),
                pltpu.SemaphoreType.DMA((9,)),
                pltpu.SemaphoreType.DMA((5, 4)),
                pltpu.SemaphoreType.DMA((5, 4)),
                pltpu.SemaphoreType.DMA((2, n_grp)),
                pltpu.SemaphoreType.DMA((2, n_grp)),
                pltpu.SemaphoreType.DMA((6, n_dev)),
                pltpu.SemaphoreType.DMA((6, n_dev)),
            ],
            compiler_params=pltpu.CompilerParams(
                collective_id=0, has_side_effects=True, vmem_limit_bytes=(64 * 1024 - 2048) * 1024
            ),
        )(
            velocity.reshape(3, 8, 8, 8, L),
            density.reshape(8, 8, 8, L),
            inverse_density.reshape(8, 8, 8, L),
            neighbours,
            leaf_layer.reshape(1, L),
            leaf_tile.reshape(1, L),
            leaf_block.reshape(1, L),
            samples,
        )
        return new_velocity.reshape(3, 512, L), rendered

    return jax.shard_map(
        step,
        mesh=mesh,
        in_specs=(
            P(None, None, ("grp", "dev")),
            P(None, ("grp", "dev")),
            P(None, ("grp", "dev")),
            P(None, ("grp", "dev")),
            P(("grp", "dev")),
            P(("grp", "dev"), None),
            P(("grp", "dev")),
            P(),
        ),
        out_specs=(P(None, None, ("grp", "dev")), P("dev", "grp")),
        check_vma=False,
    )
```

```python
import functools

import jax
import jax.numpy as jnp
from jax import lax
from jax.experimental import pallas as pl
from jax.experimental.pallas import tpu as pltpu
from jax.sharding import PartitionSpec as P

BLOCKS = 256
advect_step = 0.2
ray_step = 0.03
L = 256
FACE = 64
CAP = 16
F32 = jnp.float32
BF16 = jnp.bfloat16
MESH = pl.DeviceIdType.MESH


def parts(x):
    hi = x.astype(BF16)
    rest = x - hi.astype(F32)
    mid = rest.astype(BF16)
    low = (rest - mid.astype(F32)).astype(BF16)
    return jnp.concatenate([hi, mid, low], axis=0)


def joined(y):
    rows = y.shape[0] // 3
    return y[:rows] + y[rows : 2 * rows] + y[2 * rows :]


def pick(x, hot):
    return joined(jnp.dot(parts(x), hot, preferred_element_type=F32))


def pick_t(x, hot):
    return joined(
        lax.dot_general(parts(x), hot, (((1,), (1,)), ((), ())), preferred_element_type=F32)
    )


def spread(row, rows):
    return jnp.broadcast_to(row, (rows, row.shape[1]))


def hot_of(condition):
    return jnp.where(condition, 1.0, 0.0).astype(BF16)


def kernel(
    n_grp,
    n_dev,
    vel,
    dens,
    inv,
    nbr_any,
    layer_any,
    tile_any,
    block_any,
    samples,
    newv,
    rendered,
    nbr,
    rows_in,
    wp,
    vx,
    vy,
    vz,
    dn,
    hd,
    q,
    zf,
    zt,
    cs,
    dg,
    pp,
    gl,
    cp,
    er,
    rf,
    sb,
    rb,
    sbw,
    rbw,
    a1s,
    a1r,
    a2s,
    a2r,
    ids,
    idr,
    das,
    dar,
    pix,
    ims,
    imr,
    sx,
    fy,
    sz,
    sd,
    col,
    in_sem,
    hs_sem,
    hr_sem,
    gs_sem,
    gr_sem,
    ds_sem,
    dr_sem,
):
    g = lax.axis_index("grp")
    d = lax.axis_index("dev")
    me = g * n_dev + d

    def grp_at(step):
        return (lax.rem(g + step, n_grp), d)

    def dev_at(step):
        return (g, lax.rem(d + step, n_dev))

    barrier = pltpu.get_barrier_semaphore()

    @pl.loop(1, n_grp)
    def _(i):
        pl.semaphore_signal(barrier, inc=1, device_id=grp_at(i), device_id_type=MESH)

    @pl.loop(1, n_dev)
    def _(i):
        pl.semaphore_signal(barrier, inc=1, device_id=dev_at(i), device_id_type=MESH)

    small = [
        pltpu.make_async_copy(nbr_any, nbr, in_sem.at[5]),
        pltpu.make_async_copy(tile_any, rows_in.at[0], in_sem.at[6]),
        pltpu.make_async_copy(block_any, rows_in.at[1], in_sem.at[7]),
        pltpu.make_async_copy(layer_any, rows_in.at[2], in_sem.at[8]),
    ]
    loads = [
        pltpu.make_async_copy(inv, wp.at[pl.ds(1, 8), pl.ds(1, 8)], in_sem.at[0]),
        pltpu.make_async_copy(vel.at[0], vx.at[pl.ds(1, 8)], in_sem.at[1]),
        pltpu.make_async_copy(vel.at[1], vy.at[:, pl.ds(1, 8)], in_sem.at[2]),
        pltpu.make_async_copy(dens, dn, in_sem.at[3]),
        pltpu.make_async_copy(vel.at[2], vz, in_sem.at[4]),
    ]
    for load in small + loads:
        load.start()

    to = [dev_at(1), dev_at(n_dev - 1), grp_at(1), grp_at(n_grp - 1)]
    sends = [d < n_dev - 1, d > 0, g < n_grp - 1, g > 0]
    takes = [d > 0, d < n_dev - 1, g > 0, g < n_grp - 1]

    for face in range(4):

        @pl.when(jnp.logical_not(takes[face]))
        def _():
            rb[:, face] = jnp.zeros((7, FACE // 2, 128), F32)
            rbw[face] = jnp.zeros((FACE, 128), F32)

    for load in small:
        load.wait()

    table = nbr[...]
    present = table >= 0
    local = present & ((table // L) == me)
    remote = present & ((table // L) != me)
    slot = table % L
    local_slot = jnp.where(local, slot, -1)
    remote_slot = jnp.where(remote, slot, -1)
    sub = lax.broadcasted_iota(jnp.int32, (L, L), 0)
    lane = lax.broadcasted_iota(jnp.int32, (L, L), 1)
    upper = hot_of(sub < lane)
    sub128 = lax.broadcasted_iota(jnp.int32, (2 * FACE, L), 0)
    tile_row = rows_in[0]
    tile_hot = hot_of(
        lax.broadcasted_iota(jnp.int32, (n_dev, L), 0) == spread(tile_row, n_dev)
    )
    before = jnp.dot(
        jnp.concatenate([tile_hot, hot_of(remote), jnp.zeros((10, L), BF16)], axis=0),
        upper,
        preferred_element_type=F32,
    )
    for face in range(4):
        out_face = face ^ 1
        place = before[n_dev + out_face : n_dev + out_face + 1].astype(jnp.int32)
        place = jnp.where(remote_slot[out_face : out_face + 1] >= 0, place, -1000)
        cp[face, 0] = hot_of(sub128 == spread(place, 2 * FACE))
        cp[face, 1] = hot_of(sub128 == spread(place + FACE, 2 * FACE))

    for load in loads[:4]:
        load.wait()

    def flat(x):
        return x.reshape(FACE, L)

    def cube(x):
        return x.reshape(8, 8, L)

    def halo(number, face):
        wide = number == 7
        return pltpu.make_async_remote_copy(
            src_ref=sbw.at[face] if wide else sb.at[number, face],
            dst_ref=rbw.at[face] if wide else rb.at[number, face],
            send_sem=hs_sem.at[number, face],
            recv_sem=hr_sem.at[number, face],
            device_id=to[face],
            device_id_type=MESH,
        )

    def start_faces(number):
        for face in range(4):

            @pl.when(sends[face])
            def _():
                halo(number, face).start()

    def pack_faces(number, layers):
        for face in range(4):
            rows_64 = flat(layers[face])
            sb[number, face] = pick_t(rows_64[:32], cp[face, 0]) + pick_t(
                rows_64[32:], cp[face, 1]
            )

    def take_faces(number):
        for face in range(4):

            @pl.when(takes[face])
            def _():
                halo(number, face).wait_recv()

    def unpacked(number, face):
        got = parts(rb[number, face])
        top = joined(jnp.dot(got, er[face, 0], preferred_element_type=F32))
        bottom = joined(jnp.dot(got, er[face, 1], preferred_element_type=F32))
        return cube(jnp.concatenate([top, bottom], axis=0))

    first = [wp[8, 1:9], wp[1, 1:9], wp[1:9, 8], wp[1:9, 1]]
    second = [vx[8], vx[1], vy[:, 8], vy[:, 1]]
    for face in range(4):
        sbw[face] = pick_t(flat(first[face]), cp[face, 0]) + pick_t(
            flat(second[face]), cp[face, 1]
        )

    pl.semaphore_wait(barrier, n_dev - 1 + n_grp - 1)
    start_faces(7)
    pack_faces(6, [dn[7], dn[0], dn[:, 7], dn[:, 0]])
    start_faces(6)

    for face in range(6):
        gl[face] = hot_of(sub == spread(local_slot[face : face + 1], L))
    for face in range(4):
        mine = remote_slot[face : face + 1]
        occupied = jnp.sum(
            jnp.where(sub == spread(mine, L), 1.0, 0.0), axis=1, keepdims=True
        )
        rank = jnp.sum(
            jnp.where(sub < spread(mine, L), occupied, 0.0), axis=0, keepdims=True
        ).astype(jnp.int32)
        rank = jnp.where(mine >= 0, rank, -1000)
        er[face, 0] = hot_of(sub128 == spread(rank, 2 * FACE))
        er[face, 1] = hot_of(sub128 == spread(rank + FACE, 2 * FACE))

    rank = jnp.sum(
        jnp.where(tile_hot > 0, before[:n_dev], 0.0), axis=0, keepdims=True
    ).astype(jnp.int32)
    rows = n_dev * 8
    sub_key = lax.broadcasted_iota(jnp.int32, (rows, L), 0)
    first_key = jnp.where(rank < 8, tile_row * 8 + rank, -1)
    second_key = jnp.where(rank >= 8, tile_row * 8 + rank - 8, -1)
    slot_hot = jnp.concatenate(
        [hot_of(sub_key == spread(first_key, rows)), hot_of(sub_key == spread(second_key, rows))],
        axis=1,
    )

    def into_slots(values):
        empty = jnp.zeros_like(values)
        packed = jnp.concatenate(
            [
                jnp.concatenate([values, empty], axis=1),
                jnp.concatenate([empty, values], axis=1),
            ],
            axis=0,
        )
        return lax.dot_general(
            slot_hot, packed, (((1,), (1,)), ((), ())), preferred_element_type=F32
        )

    def to_dev(number, src, dst, i):
        return pltpu.make_async_remote_copy(
            src_ref=src,
            dst_ref=dst,
            send_sem=ds_sem.at[number, i],
            recv_sem=dr_sem.at[number, i],
            device_id=dev_at(i),
            device_id_type=MESH,
        )

    def to_grp(number, src, dst, i):
        return pltpu.make_async_remote_copy(
            src_ref=src,
            dst_ref=dst,
            send_sem=gs_sem.at[number, i],
            recv_sem=gr_sem.at[number, i],
            device_id=grp_at(i),
            device_id_type=MESH,
        )

    def ids_copy(i):
        return to_dev(0, ids.at[lax.rem(d + i, n_dev)], idr.at[i], i)

    def sum_copy(i):
        return to_dev(1, a2s, a2r.at[i], i)

    def data_copy(which, i):
        return to_dev(2 + which, das.at[which, lax.rem(d + i, n_dev)], dar.at[which, i], i)

    ids[...] = into_slots(spread(rows_in[1], 64).astype(F32).astype(BF16)).reshape(n_dev, 8, 128)

    @pl.loop(1, n_dev)
    def _(i):
        ids_copy(i).start()

    idr[0] = ids[d]
    limit = jnp.zeros((1, L), jnp.int32)
    for t in range(n_dev):
        limit = jnp.where(tile_row == t, samples[t], limit)
    marched = jnp.where(rows_in[2] < limit, ray_step, 0.0)

    loads[4].wait()

    def fill_z_tables(read):
        @pl.loop(0, 8)
        def _(i):
            for j in range(8):
                c = read(i, j)
                zt[0, i, j : j + 1, :] = c[7:8]
                zt[1, i, j : j + 1, :] = c[0:1]

    def local_faces(k):
        q[k, 0, 1:9] = cube(pick(flat(q[k, 8, 1:9]), gl[0]))
        q[k, 9, 1:9] = cube(pick(flat(q[k, 1, 1:9]), gl[1]))
        q[k, 1:9, 0] = cube(pick(flat(q[k, 1:9, 8]), gl[2]))
        q[k, 1:9, 9] = cube(pick(flat(q[k, 1:9, 1]), gl[3]))
        zf[2 * k] = cube(pick(flat(zt[0]), gl[4]))
        zf[2 * k + 1] = cube(pick(flat(zt[1]), gl[5]))

    fill_z_tables(lambda i, j: vz[i, j])
    zf[2] = cube(pick(flat(zt[0]), gl[4]))
    zf[3] = cube(pick(flat(zt[1]), gl[5]))
    fill_z_tables(lambda i, j: wp[i + 1, j + 1])
    absent = [jnp.where(present[face : face + 1], 0.0, 1.0) for face in range(6)]
    zf[0] = cube(pick(flat(zt[0]), gl[4]))
    zf[1] = cube(pick(flat(zt[1]), gl[5]))

    def both(first, second, face):
        return pick(jnp.concatenate([flat(first), flat(second)], axis=0), gl[face])

    near_local = [
        both(wp[8, 1:9], vx[8], 0),
        both(wp[1, 1:9], vx[1], 1),
        both(wp[1:9, 8], vy[:, 8], 2),
        both(wp[1:9, 1], vy[:, 1], 3),
    ]
    k_id = lax.broadcasted_iota(jnp.int32, (8, L), 0)
    at_low = k_id == 0
    at_high = k_id == 7
    zero = jnp.zeros((8, L), F32)

    def beside_z(c, low, high):
        return (
            jnp.where(at_low, low, pltpu.roll(c, 1, 0)),
            jnp.where(at_high, high, pltpu.roll(c, 7, 0)),
        )

    def start(i, columns):
        for j in columns:
            c = wp[i + 1, j + 1]
            low, high = beside_z(
                c,
                zf[0, i, j : j + 1] + absent[4] * c[0:1],
                zf[1, i, j : j + 1] + absent[5] * c[7:8],
            )
            near = [wp[i, j + 1], wp[i + 2, j + 1], wp[i + 1, j], wp[i + 1, j + 2], low, high]
            coupling = [0.5 * (c + value) for value in near]
            diagonal = (
                coupling[0] + coupling[1] + coupling[2] + coupling[3] + coupling[4] + coupling[5]
            )
            inverse = 1.0 / diagonal
            dg[i, j] = diagonal
            for face in range(6):
                cs[face, i, j] = coupling[face] * inverse
            v = vz[i, j]
            low, high = beside_z(v, zf[2, i, j : j + 1], zf[3, i, j : j + 1])
            source = -0.5 * (
                (vx[i + 2, j] - vx[i, j]) + (vy[i, j + 2] - vy[i, j]) + (high - low)
            )
            q[0, i + 1, j + 1] = source * inverse

    @pl.loop(1, 7)
    def _(i):
        start(i, range(1, 7))

    take_faces(7)
    for face in range(4):
        got = parts(rbw[face])
        w_far = joined(jnp.dot(got, er[face, 0], preferred_element_type=F32))
        v_far = joined(jnp.dot(got, er[face, 1], preferred_element_type=F32))
        rf[face, 0] = cube(w_far)
        rf[face, 1] = cube(v_far)
        w_near = cube(near_local[face][:FACE] + w_far)
        v_near = cube(near_local[face][FACE:] + v_far)
        if face == 0:
            wp[0, 1:9] = w_near + absent[face] * wp[1, 1:9]
            vx[0] = v_near
        elif face == 1:
            wp[9, 1:9] = w_near + absent[face] * wp[8, 1:9]
            vx[9] = v_near
        elif face == 2:
            wp[1:9, 0] = w_near + absent[face] * wp[1:9, 1]
            vy[:, 0] = v_near
        else:
            wp[1:9, 9] = w_near + absent[face] * wp[1:9, 8]
            vy[:, 9] = v_near

    for i in (0, 7):
        start(i, range(8))

    @pl.loop(1, 7)
    def _(i):
        start(i, (0, 7))

    def send_field(k):
        pack_faces(k, [q[k, 8, 1:9], q[k, 1, 1:9], q[k, 1:9, 8], q[k, 1:9, 1]])
        start_faces(k)

    def send_deep(k):
        pack_faces(3 + k, [q[k, 7, 1:9], q[k, 2, 1:9], q[k, 1:9, 7], q[k, 1:9, 2]])
        start_faces(3 + k)

    send_field(0)

    def apply_local(k):
        @pl.loop(0, 8)
        def _(i):
            for j in range(8):
                c = q[k, i + 1, j + 1]
                low, high = beside_z(c, zf[2 * k, i, j : j + 1], zf[2 * k + 1, i, j : j + 1])
                near = [
                    q[k, i, j + 1],
                    q[k, i + 2, j + 1],
                    q[k, i + 1, j],
                    q[k, i + 1, j + 2],
                    low,
                    high,
                ]
                value = c
                for face in range(6):
                    value = value - cs[face, i, j] * near[face]
                q[k + 1, i + 1, j + 1] = value

    def add_far(k):
        far = [unpacked(k, face) for face in range(4)]
        q[k, 0, 1:9] += far[0]
        q[k, 9, 1:9] += far[1]
        q[k, 1:9, 0] += far[2]
        q[k, 1:9, 9] += far[3]
        q[k + 1, 1, 1:9] -= cs[0, 0] * far[0]
        q[k + 1, 8, 1:9] -= cs[1, 7] * far[1]
        q[k + 1, 1:9, 1] -= cs[2, :, 0] * far[2]
        q[k + 1, 1:9, 8] -= cs[3, :, 7] * far[3]

    def products(k):
        def body(i, totals):
            even, odd = totals
            for j in range(8):
                c = q[k, i + 1, j + 1]
                scaled = dg[i, j] * c
                even = even + c * scaled
                odd = odd + q[k + 1, i + 1, j + 1] * scaled
            return even, odd

        return lax.fori_loop(0, 8, body, (zero, zero))

    def read_z(k):
        return lambda i, j: q[k, i + 1, j + 1]

    def flux_columns(which):
        base = which == 0
        k = which - 1

        def far(face):
            if base:
                return rf[face, 2] * rf[face, 1]
            deep = unpacked(3 + k, face)
            change = [
                lambda: q[k, 1, 1:9] - deep,
                lambda: deep - q[k, 8, 1:9],
                lambda: q[k, 1:9, 1] - deep,
                lambda: deep - q[k, 1:9, 8],
            ][face]()
            return rf[face, 3] * change

        if not base:
            take_faces(3 + k)
        sx[0] = jnp.sum(far(0), axis=0)
        sx[9] = jnp.sum(far(1), axis=0)
        fy[0] = far(2)
        fy[3] = far(3)

        @pl.loop(0, 8)
        def _(i):
            sum_x = zero
            sum_z = zero
            sum_d = zero
            for j in range(8):
                if base:
                    smoke = dn[i, j]
                    sum_x = sum_x + smoke * vx[i + 1, j]
                    sum_z = sum_z + smoke * vz[i, j]
                    sum_d = sum_d + smoke
                    if j == 0:
                        fy[1, i] = smoke * vy[i, 1]
                    if j == 7:
                        fy[2, i] = smoke * vy[i, 8]
                else:
                    half = hd[i, j]
                    low, high = beside_z(
                        q[k, i + 1, j + 1], zf[2 * k, i, j : j + 1], zf[2 * k + 1, i, j : j + 1]
                    )
                    sum_x = sum_x + half * (q[k, i + 2, j + 1] - q[k, i, j + 1])
                    sum_z = sum_z + half * (high - low)
                    if j == 0:
                        fy[1, i] = half * (q[k, i + 1, 2] - q[k, i + 1, 0])
                    if j == 7:
                        fy[2, i] = half * (q[k, i + 1, 9] - q[k, i + 1, 7])
            sx[i + 1] = sum_x
            sz[i] = sum_z
            if base:
                sd[i] = sum_d
            zt[0, 0, pl.ds(i, 1), :] = sum_z[7:8]
            zt[1, 0, pl.ds(i, 1), :] = sum_z[0:1]

        fy[0] += cube(pick(flat(fy[2]), gl[2]))
        fy[3] += cube(pick(flat(fy[1]), gl[3]))

        def pick_8(x, hot):
            return pick(jnp.concatenate([x, x], axis=0), hot)[:8]

        sx[0] += pick_8(sx[8], gl[0])
        sx[9] += pick_8(sx[1], gl[1])
        z_low = pick_8(zt[0, 0], gl[4])
        z_high = pick_8(zt[1, 0], gl[5])
        for i in range(8):
            low, high = beside_z(sz[i], z_low[i : i + 1], z_high[i : i + 1])
            change = (
                (sx[i + 2] - sx[i])
                + ((fy[3, i] + fy[2, i]) - (fy[1, i] + fy[0, i]))
                + (high - low)
            )
            change = (0.5 * advect_step) * change
            col[8 * i : 8 * i + 8] = marched * (sd[i] - change if base else change)
        columns = parts(col[...])
        total = into_slots(columns[:64]) + into_slots(columns[64:128]) + into_slots(columns[128:])
        das[which] = total.reshape(n_dev, 8, 128)

        @pl.loop(1, n_dev)
        def _(i):
            data_copy(which, i).start()

        dar[which, 0] = das[which, d]

    send_deep(0)
    fill_z_tables(read_z(0))
    local_faces(0)
    apply_local(0)
    take_faces(6)
    for face in range(4):
        smoke_far = unpacked(6, face)
        rf[face, 2] = smoke_far
        rf[face, 3] = 0.5 * smoke_far * rf[face, 0]

    @pl.loop(0, 8)
    def _(i):
        for j in range(8):
            hd[i, j] = 0.5 * dn[i, j] * wp[i + 1, j + 1]

    flux_columns(0)
    take_faces(0)
    add_far(0)
    send_field(1)

    send_deep(1)
    fill_z_tables(read_z(1))
    local_faces(1)
    apply_local(1)
    flux_columns(1)
    m0, m1 = products(0)
    take_faces(1)
    add_far(1)
    send_field(2)

    send_deep(2)
    fill_z_tables(read_z(2))
    local_faces(2)
    apply_local(2)
    flux_columns(2)
    m2, m3 = products(1)
    m4, m5 = products(2)

    take_faces(2)
    far = [unpacked(2, face) for face in range(4)]
    m5_far = zero
    for j in range(8):
        m5_far = m5_far + dg[0, j] * cs[0, 0, j] * far[0][j] * q[2, 1, j + 1]
        m5_far = m5_far + dg[7, j] * cs[1, 7, j] * far[1][j] * q[2, 8, j + 1]
        m5_far = m5_far + dg[j, 0] * cs[2, j, 0] * far[2][j] * q[2, j + 1, 1]
        m5_far = m5_far + dg[j, 7] * cs[3, j, 7] * far[3][j] * q[2, j + 1, 8]

    moments = [m0, m1, m2, m3, m4, m5 - m5_far]
    lanes = lax.broadcasted_iota(jnp.int32, (1, 128), 1)
    row = jnp.zeros((1, 128), F32)
    for k in range(6):
        line = jnp.sum(moments[k], axis=0, keepdims=True)
        line = jnp.sum(line[:, :128] + line[:, 128:], axis=1, keepdims=True)
        row = jnp.where(lanes == k, line, row)
    a1s[...] = row
    for i in range(1, n_grp):
        to_grp(0, a1s, a1r.at[i], i).start()

    q[2, 0, 1:9] += far[0]
    q[2, 9, 1:9] += far[1]
    q[2, 1:9, 0] += far[2]
    q[2, 1:9, 9] += far[3]
    flux_columns(3)

    partial = a1s[...]
    for i in range(1, n_grp):
        to_grp(0, a1s, a1r.at[i], i).wait_recv()
        partial = partial + a1r[i]
    a2s[...] = partial

    @pl.loop(1, n_dev)
    def _(i):
        sum_copy(i).start()

    @pl.loop(1, n_dev)
    def _(i):
        ids_copy(i).wait_recv()

    marks = idr[...].reshape(rows, 128)
    lane_b = lax.broadcasted_iota(jnp.int32, (rows, BLOCKS), 1).astype(F32)
    first_hot = hot_of(marks[:, 0:1] == lane_b)
    second_hot = hot_of(marks[:, 64:65] == lane_b)

    def pixels(which):
        got = parts(dar[which].reshape(rows, 128).T)
        image = joined(jnp.dot(got, first_hot, preferred_element_type=F32))[:64]
        return image + joined(jnp.dot(got, second_hot, preferred_element_type=F32))[64:]

    @pl.loop(1, n_dev)
    def _(i):
        ids_copy(i).wait_send()
        for which in range(3):
            data_copy(which, i).wait_send()
            data_copy(which, i).wait_recv()

    for which in range(3):
        pix[which] = pixels(which)

    @pl.loop(1, n_dev)
    def _(i):
        data_copy(3, i).wait_recv()

    pix[3] = pixels(3)

    @pl.loop(1, n_dev)
    def _(i):
        sum_copy(i).wait_recv()

    whole = partial
    for i in range(1, n_dev):
        whole = whole + a2r[i]
    m = [
        jnp.broadcast_to(
            jnp.sum(jnp.where(lanes == k, whole, 0.0), axis=1, keepdims=True), (1, 128)
        )
        for k in range(6)
    ]
    l10 = m[2] / m[1]
    l20 = m[3] / m[1]
    d1 = m[3] - l10 * m[2]
    t21 = m[4] - l20 * m[2]
    l21 = t21 / d1
    d2 = m[5] - l20 * m[3] - l21 * t21
    y1 = m[1] - l10 * m[0]
    y2 = m[2] - l20 * m[0] - l21 * y1
    c2 = y2 / d2
    c1 = y1 / d1 - l21 * c2
    c0 = m[0] / m[1] - l10 * c1 - l20 * c2
    coefs = [jnp.concatenate([spread(c, 8), spread(c, 8)], axis=1) for c in (c0, c1, c2)]
    for row_id in range(8):
        part = slice(8 * row_id, 8 * row_id + 8)
        ims[row_id] = (
            pix[0, part] + coefs[0] * pix[1, part] + coefs[1] * pix[2, part] + coefs[2] * pix[3, part]
        )

    def image_copy(i):
        return to_grp(1, ims.at[lax.rem(g + i, n_grp)], imr.at[i], i)

    for i in range(1, n_grp):
        image_copy(i).start()

    def mixed(read):
        return coefs[0] * read(0) + coefs[1] * read(1) + coefs[2] * read(2)

    @pl.loop(0, 8)
    def _(i):
        pp[0, i + 1] = mixed(lambda k: q[k, 0, i + 1])
        pp[9, i + 1] = mixed(lambda k: q[k, 9, i + 1])
        zf[0, i] = mixed(lambda k: zf[2 * k, i])
        zf[1, i] = mixed(lambda k: zf[2 * k + 1, i])
        for j in range(10):
            pp[i + 1, j] = mixed(lambda k: q[k, i + 1, j])

    @pl.loop(0, 8)
    def _(i):
        for j in range(8):
            c = pp[i + 1, j + 1]
            low, high = beside_z(c, zf[0, i, j : j + 1], zf[1, i, j : j + 1])
            half = 0.5 * wp[i + 1, j + 1]
            newv[0, i, j] = vx[i + 1, j] - half * (pp[i + 2, j + 1] - pp[i, j + 1])
            newv[1, i, j] = vy[i, j + 1] - half * (pp[i + 1, j + 2] - pp[i + 1, j])
            newv[2, i, j] = vz[i, j] - half * (high - low)

    for number in range(8):
        for face in range(4):

            @pl.when(sends[face])
            def _():
                halo(number, face).wait_send()

    for i in range(1, n_grp):
        to_grp(0, a1s, a1r.at[i], i).wait_send()

    @pl.loop(1, n_dev)
    def _(i):
        sum_copy(i).wait_send()
        data_copy(3, i).wait_send()

    optical = ims[g]
    for i in range(1, n_grp):
        image_copy(i).wait_recv()
        optical = optical + imr[i]
    shade = 1.0 - jnp.exp(-optical)
    for row in range(8):
        rendered[:, BLOCKS * row : BLOCKS * (row + 1)] = shade[row : row + 1]
    for i in range(1, n_grp):
        image_copy(i).wait_send()


def solution(mesh):
    n_grp, n_dev = mesh.shape["grp"], mesh.shape["dev"]

    def step(
        velocity, density, inverse_density, neighbours, leaf_layer, leaf_tile, leaf_block, samples
    ):
        vmem = pl.BlockSpec(memory_space=pltpu.VMEM)
        anywhere = pl.BlockSpec(memory_space=pl.ANY)
        smem = pl.BlockSpec(memory_space=pltpu.SMEM)
        new_velocity, rendered = pl.pallas_call(
            functools.partial(kernel, n_grp, n_dev),
            out_shape=(
                pltpu.VMEM((3, 8, 8, 8, L), F32),
                pltpu.VMEM((1, 8 * BLOCKS), F32),
            ),
            in_specs=[anywhere] * 7 + [smem],
            out_specs=(vmem, vmem),
            scratch_shapes=[
                pltpu.VMEM((6, L), jnp.int32),
                pltpu.VMEM((3, 1, L), jnp.int32),
                pltpu.VMEM((10, 10, 8, L), F32),
                pltpu.VMEM((10, 8, 8, L), F32),
                pltpu.VMEM((8, 10, 8, L), F32),
                pltpu.VMEM((8, 8, 8, L), F32),
                pltpu.VMEM((8, 8, 8, L), F32),
                pltpu.VMEM((8, 8, 8, L), F32),
                pltpu.VMEM((4, 10, 10, 8, L), F32),
                pltpu.VMEM((6, 8, 8, L), F32),
                pltpu.VMEM((2, 8, 8, L), F32),
                pltpu.VMEM((6, 8, 8, 8, L), F32),
                pltpu.VMEM((8, 8, 8, L), F32),
                pltpu.VMEM((10, 10, 8, L), F32),
                pltpu.VMEM((6, L, L), BF16),
                pltpu.VMEM((4, 2, 2 * FACE, L), BF16),
                pltpu.VMEM((4, 2, 2 * FACE, L), BF16),
                pltpu.VMEM((4, 4, 8, 8, L), F32),
                pltpu.VMEM((7, 4, FACE // 2, 128), F32),
                pltpu.VMEM((7, 4, FACE // 2, 128), F32),
                pltpu.VMEM((4, FACE, 128), F32),
                pltpu.VMEM((4, FACE, 128), F32),
                pltpu.VMEM((1, 128), F32),
                pltpu.VMEM((n_grp, 1, 128), F32),
                pltpu.VMEM((1, 128), F32),
                pltpu.VMEM((n_dev, 1, 128), F32),
                pltpu.VMEM((n_dev, 8, 128), F32),
                pltpu.VMEM((n_dev, 8, 128), F32),
                pltpu.VMEM((4, n_dev, 8, 128), F32),
                pltpu.VMEM((4, n_dev, 8, 128), F32),
                pltpu.VMEM((4, 64, BLOCKS), F32),
                pltpu.VMEM((8, 8, BLOCKS), F32),
                pltpu.VMEM((n_grp, 8, BLOCKS), F32),
                pltpu.VMEM((10, 8, L), F32),
                pltpu.VMEM((4, 8, 8, L), F32),
                pltpu.VMEM((8, 8, L), F32),
                pltpu.VMEM((8, 8, L), F32),
                pltpu.VMEM((64, L), F32),
                pltpu.SemaphoreType.DMA((9,)),
                pltpu.SemaphoreType.DMA((8, 4)),
                pltpu.SemaphoreType.DMA((8, 4)),
                pltpu.SemaphoreType.DMA((2, n_grp)),
                pltpu.SemaphoreType.DMA((2, n_grp)),
                pltpu.SemaphoreType.DMA((6, n_dev)),
                pltpu.SemaphoreType.DMA((6, n_dev)),
            ],
            compiler_params=pltpu.CompilerParams(
                collective_id=0, has_side_effects=True, vmem_limit_bytes=(64 * 1024 - 2048) * 1024
            ),
        )(
            velocity.reshape(3, 8, 8, 8, L),
            density.reshape(8, 8, 8, L),
            inverse_density.reshape(8, 8, 8, L),
            neighbours,
            leaf_layer.reshape(1, L),
            leaf_tile.reshape(1, L),
            leaf_block.reshape(1, L),
            samples,
        )
        return new_velocity.reshape(3, 512, L), rendered

    return jax.shard_map(
        step,
        mesh=mesh,
        in_specs=(
            P(None, None, ("grp", "dev")),
            P(None, ("grp", "dev")),
            P(None, ("grp", "dev")),
            P(None, ("grp", "dev")),
            P(("grp", "dev")),
            P(("grp", "dev"), None),
            P(("grp", "dev")),
            P(),
        ),
        out_specs=(P(None, None, ("grp", "dev")), P("dev", "grp")),
        check_vma=False,
    )
```

```python
import functools

import jax
import jax.numpy as jnp
from jax import lax
from jax.experimental import pallas as pl
from jax.experimental.pallas import tpu as pltpu
from jax.sharding import PartitionSpec as P

BLOCKS = 256
advect_step = 0.2
ray_step = 0.03
L = 256
FACE = 64
CAP = 16
F32 = jnp.float32
BF16 = jnp.bfloat16
MESH = pl.DeviceIdType.MESH


def parts(x):
    hi = x.astype(BF16)
    rest = x - hi.astype(F32)
    mid = rest.astype(BF16)
    low = (rest - mid.astype(F32)).astype(BF16)
    return jnp.concatenate([hi, mid, low], axis=0)


def joined(y):
    rows = y.shape[0] // 3
    return y[:rows] + y[rows : 2 * rows] + y[2 * rows :]


def pick(x, hot):
    return joined(jnp.dot(parts(x), hot, preferred_element_type=F32))


def pick_t(x, hot):
    return joined(
        lax.dot_general(parts(x), hot, (((1,), (1,)), ((), ())), preferred_element_type=F32)
    )


def spread(row, rows):
    return jnp.broadcast_to(row, (rows, row.shape[1]))


def hot_of(condition):
    return jnp.where(condition, 1.0, 0.0).astype(BF16)


def kernel(
    n_grp,
    n_dev,
    vel,
    dens,
    inv,
    nbr_any,
    layer_any,
    tile_any,
    block_any,
    samples,
    newv,
    rendered,
    nbr,
    rows_in,
    wp,
    vx,
    vy,
    vz,
    dn,
    hd,
    q,
    zf,
    zt,
    cs,
    dg,
    pp,
    gl,
    cp,
    er,
    rf,
    sb,
    rb,
    sbw,
    rbw,
    a1s,
    a1r,
    a2s,
    a2r,
    ids,
    idr,
    das,
    dar,
    pix,
    imr,
    sx,
    fy,
    sz,
    sd,
    col,
    in_sem,
    hs_sem,
    hr_sem,
    gs_sem,
    gr_sem,
    ds_sem,
    dr_sem,
    relay_sem,
):
    g = lax.axis_index("grp")
    d = lax.axis_index("dev")
    me = g * n_dev + d

    def grp_at(step):
        return (lax.rem(g + step, n_grp), d)

    def dev_at(step):
        return (g, lax.rem(d + step, n_dev))

    def torus_at(step_x, step_z):
        x = lax.rem(d // 8 + step_x, n_dev // 8)
        return (g, x * 8 + lax.rem(lax.rem(d, 8) + step_z, 8))

    two_away = [torus_at(0, 2), torus_at(0, 6), torus_at(2, 0)] + [
        torus_at(x, z) for x in (1, n_dev // 8 - 1) for z in (1, 7)
    ]
    greeted = [torus_at(0, 1), torus_at(0, 7), torus_at(1, 0), torus_at(n_dev // 8 - 1, 0)]
    greeted = [grp_at(i) for i in range(1, n_grp)] + greeted + two_away
    barrier = pltpu.get_barrier_semaphore()
    for who in greeted:
        pl.semaphore_signal(barrier, inc=1, device_id=who, device_id_type=MESH)

    def relay(number):
        for who in two_away:
            pl.semaphore_signal(
                relay_sem.at[number], inc=1, device_id=who, device_id_type=MESH
            )

    small = [
        pltpu.make_async_copy(nbr_any, nbr, in_sem.at[5]),
        pltpu.make_async_copy(tile_any, rows_in.at[0], in_sem.at[6]),
        pltpu.make_async_copy(block_any, rows_in.at[1], in_sem.at[7]),
        pltpu.make_async_copy(layer_any, rows_in.at[2], in_sem.at[8]),
    ]
    loads = [
        pltpu.make_async_copy(inv, wp.at[pl.ds(1, 8), pl.ds(1, 8)], in_sem.at[0]),
        pltpu.make_async_copy(vel.at[0], vx.at[pl.ds(1, 8)], in_sem.at[1]),
        pltpu.make_async_copy(vel.at[1], vy.at[:, pl.ds(1, 8)], in_sem.at[2]),
        pltpu.make_async_copy(dens, dn, in_sem.at[3]),
        pltpu.make_async_copy(vel.at[2], vz, in_sem.at[4]),
    ]
    for load in small + loads:
        load.start()

    to = [dev_at(1), dev_at(n_dev - 1), grp_at(1), grp_at(n_grp - 1)]
    sends = [d < n_dev - 1, d > 0, g < n_grp - 1, g > 0]
    takes = [d > 0, d < n_dev - 1, g > 0, g < n_grp - 1]

    for face in range(4):

        @pl.when(jnp.logical_not(takes[face]))
        def _():
            rb[:, face] = jnp.zeros((7, FACE // 2, 128), F32)
            rbw[face] = jnp.zeros((FACE, 128), F32)

    for load in small:
        load.wait()

    table = nbr[...]
    present = table >= 0
    local = present & ((table // L) == me)
    remote = present & ((table // L) != me)
    slot = table % L
    local_slot = jnp.where(local, slot, -1)
    remote_slot = jnp.where(remote, slot, -1)
    sub = lax.broadcasted_iota(jnp.int32, (L, L), 0)
    lane = lax.broadcasted_iota(jnp.int32, (L, L), 1)
    upper = hot_of(sub < lane)
    sub128 = lax.broadcasted_iota(jnp.int32, (2 * FACE, L), 0)
    tile_row = rows_in[0]
    tile_hot = hot_of(
        lax.broadcasted_iota(jnp.int32, (n_dev, L), 0) == spread(tile_row, n_dev)
    )
    before = jnp.dot(
        jnp.concatenate([tile_hot, hot_of(remote), jnp.zeros((10, L), BF16)], axis=0),
        upper,
        preferred_element_type=F32,
    )
    for face in range(4):
        out_face = face ^ 1
        place = before[n_dev + out_face : n_dev + out_face + 1].astype(jnp.int32)
        place = jnp.where(remote_slot[out_face : out_face + 1] >= 0, place, -1000)
        cp[face, 0] = hot_of(sub128 == spread(place, 2 * FACE))
        cp[face, 1] = hot_of(sub128 == spread(place + FACE, 2 * FACE))

    for load in loads[:4]:
        load.wait()

    def flat(x):
        return x.reshape(FACE, L)

    def cube(x):
        return x.reshape(8, 8, L)

    def halo(number, face):
        wide = number == 7
        return pltpu.make_async_remote_copy(
            src_ref=sbw.at[face] if wide else sb.at[number, face],
            dst_ref=rbw.at[face] if wide else rb.at[number, face],
            send_sem=hs_sem.at[number, face],
            recv_sem=hr_sem.at[number, face],
            device_id=to[face],
            device_id_type=MESH,
        )

    def start_faces(number):
        for face in range(4):

            @pl.when(sends[face])
            def _():
                halo(number, face).start()

    def pack_faces(number, layers):
        for face in range(4):
            rows_64 = flat(layers[face])
            sb[number, face] = pick_t(rows_64[:32], cp[face, 0]) + pick_t(
                rows_64[32:], cp[face, 1]
            )

    def take_faces(number):
        for face in range(4):

            @pl.when(takes[face])
            def _():
                halo(number, face).wait_recv()

    def unpacked(number, face):
        got = parts(rb[number, face])
        top = joined(jnp.dot(got, er[face, 0], preferred_element_type=F32))
        bottom = joined(jnp.dot(got, er[face, 1], preferred_element_type=F32))
        return cube(jnp.concatenate([top, bottom], axis=0))

    first = [wp[8, 1:9], wp[1, 1:9], wp[1:9, 8], wp[1:9, 1]]
    second = [vx[8], vx[1], vy[:, 8], vy[:, 1]]
    for face in range(4):
        sbw[face] = pick_t(flat(first[face]), cp[face, 0]) + pick_t(
            flat(second[face]), cp[face, 1]
        )

    pl.semaphore_wait(barrier, len(greeted))
    start_faces(7)
    relay(0)
    pack_faces(6, [dn[7], dn[0], dn[:, 7], dn[:, 0]])
    start_faces(6)

    for face in range(6):
        gl[face] = hot_of(sub == spread(local_slot[face : face + 1], L))
    for face in range(4):
        mine = remote_slot[face : face + 1]
        occupied = jnp.sum(
            jnp.where(sub == spread(mine, L), 1.0, 0.0), axis=1, keepdims=True
        )
        rank = jnp.sum(
            jnp.where(sub < spread(mine, L), occupied, 0.0), axis=0, keepdims=True
        ).astype(jnp.int32)
        rank = jnp.where(mine >= 0, rank, -1000)
        er[face, 0] = hot_of(sub128 == spread(rank, 2 * FACE))
        er[face, 1] = hot_of(sub128 == spread(rank + FACE, 2 * FACE))

    rank = jnp.sum(
        jnp.where(tile_hot > 0, before[:n_dev], 0.0), axis=0, keepdims=True
    ).astype(jnp.int32)
    rows = n_dev * 8
    sub_key = lax.broadcasted_iota(jnp.int32, (rows, L), 0)
    first_key = jnp.where(rank < 8, tile_row * 8 + rank, -1)
    second_key = jnp.where(rank >= 8, tile_row * 8 + rank - 8, -1)
    slot_hot = jnp.concatenate(
        [hot_of(sub_key == spread(first_key, rows)), hot_of(sub_key == spread(second_key, rows))],
        axis=1,
    )

    def into_slots(values):
        empty = jnp.zeros_like(values)
        packed = jnp.concatenate(
            [
                jnp.concatenate([values, empty], axis=1),
                jnp.concatenate([empty, values], axis=1),
            ],
            axis=0,
        )
        return lax.dot_general(
            slot_hot, packed, (((1,), (1,)), ((), ())), preferred_element_type=F32
        )

    def to_dev(number, src, dst, i):
        return pltpu.make_async_remote_copy(
            src_ref=src,
            dst_ref=dst,
            send_sem=ds_sem.at[number, i],
            recv_sem=dr_sem.at[number, i],
            device_id=dev_at(i),
            device_id_type=MESH,
        )

    def to_grp(number, src, dst, i):
        return pltpu.make_async_remote_copy(
            src_ref=src,
            dst_ref=dst,
            send_sem=gs_sem.at[number, i],
            recv_sem=gr_sem.at[number, i],
            device_id=grp_at(i),
            device_id_type=MESH,
        )

    def ids_copy(i):
        return to_dev(0, ids.at[lax.rem(d + i, n_dev)], idr.at[i], i)

    def sum_copy(i):
        return to_dev(1, a2s, a2r.at[i], i)

    def data_copy(which, i):
        return to_dev(2 + which, das.at[which, lax.rem(d + i, n_dev)], dar.at[which, i], i)

    marked = jnp.where(
        lax.broadcasted_iota(jnp.int32, (128, L), 0) == spread(rank, 128),
        spread(rows_in[1], 128),
        0,
    )
    marked = lax.dot_general(
        tile_hot,
        marked.astype(F32).astype(BF16),
        (((1,), (1,)), ((), ())),
        preferred_element_type=F32,
    )
    for t in range(n_dev):
        ids[t] = marked[t : t + 1]

    idr[0] = ids[d]
    limit = jnp.zeros((1, L), jnp.int32)
    for t in range(n_dev):
        limit = jnp.where(tile_row == t, samples[t], limit)
    marched = jnp.where(rows_in[2] < limit, ray_step, 0.0)

    loads[4].wait()

    def fill_z_tables(read):
        @pl.loop(0, 8)
        def _(i):
            for j in range(8):
                c = read(i, j)
                zt[0, i, j : j + 1, :] = c[7:8]
                zt[1, i, j : j + 1, :] = c[0:1]

    def local_faces(k):
        q[k, 0, 1:9] = cube(pick(flat(q[k, 8, 1:9]), gl[0]))
        q[k, 9, 1:9] = cube(pick(flat(q[k, 1, 1:9]), gl[1]))
        q[k, 1:9, 0] = cube(pick(flat(q[k, 1:9, 8]), gl[2]))
        q[k, 1:9, 9] = cube(pick(flat(q[k, 1:9, 1]), gl[3]))
        zf[2 * k] = cube(pick(flat(zt[0]), gl[4]))
        zf[2 * k + 1] = cube(pick(flat(zt[1]), gl[5]))

    fill_z_tables(lambda i, j: vz[i, j])
    zf[2] = cube(pick(flat(zt[0]), gl[4]))
    zf[3] = cube(pick(flat(zt[1]), gl[5]))
    fill_z_tables(lambda i, j: wp[i + 1, j + 1])
    absent = [jnp.where(present[face : face + 1], 0.0, 1.0) for face in range(6)]
    zf[0] = cube(pick(flat(zt[0]), gl[4]))
    zf[1] = cube(pick(flat(zt[1]), gl[5]))

    def both(first, second, face):
        return pick(jnp.concatenate([flat(first), flat(second)], axis=0), gl[face])

    near_local = [
        both(wp[8, 1:9], vx[8], 0),
        both(wp[1, 1:9], vx[1], 1),
        both(wp[1:9, 8], vy[:, 8], 2),
        both(wp[1:9, 1], vy[:, 1], 3),
    ]
    k_id = lax.broadcasted_iota(jnp.int32, (8, L), 0)
    at_low = k_id == 0
    at_high = k_id == 7
    zero = jnp.zeros((8, L), F32)

    def beside_z(c, low, high):
        return (
            jnp.where(at_low, low, pltpu.roll(c, 1, 0)),
            jnp.where(at_high, high, pltpu.roll(c, 7, 0)),
        )

    def start(i, columns):
        for j in columns:
            c = wp[i + 1, j + 1]
            low, high = beside_z(
                c,
                zf[0, i, j : j + 1] + absent[4] * c[0:1],
                zf[1, i, j : j + 1] + absent[5] * c[7:8],
            )
            near = [wp[i, j + 1], wp[i + 2, j + 1], wp[i + 1, j], wp[i + 1, j + 2], low, high]
            coupling = [0.5 * (c + value) for value in near]
            diagonal = (
                coupling[0] + coupling[1] + coupling[2] + coupling[3] + coupling[4] + coupling[5]
            )
            inverse = 1.0 / diagonal
            dg[i, j] = diagonal
            for face in range(6):
                cs[face, i, j] = coupling[face] * inverse
            v = vz[i, j]
            low, high = beside_z(v, zf[2, i, j : j + 1], zf[3, i, j : j + 1])
            source = -0.5 * (
                (vx[i + 2, j] - vx[i, j]) + (vy[i, j + 2] - vy[i, j]) + (high - low)
            )
            q[0, i + 1, j + 1] = source * inverse

    @pl.loop(1, 7)
    def _(i):
        start(i, range(1, 7))

    take_faces(7)
    pl.semaphore_wait(relay_sem.at[0], len(two_away))
    relay(1)
    for face in range(4):
        got = parts(rbw[face])
        w_far = joined(jnp.dot(got, er[face, 0], preferred_element_type=F32))
        v_far = joined(jnp.dot(got, er[face, 1], preferred_element_type=F32))
        rf[face, 0] = cube(w_far)
        rf[face, 1] = cube(v_far)
        w_near = cube(near_local[face][:FACE] + w_far)
        v_near = cube(near_local[face][FACE:] + v_far)
        if face == 0:
            wp[0, 1:9] = w_near + absent[face] * wp[1, 1:9]
            vx[0] = v_near
        elif face == 1:
            wp[9, 1:9] = w_near + absent[face] * wp[8, 1:9]
            vx[9] = v_near
        elif face == 2:
            wp[1:9, 0] = w_near + absent[face] * wp[1:9, 1]
            vy[:, 0] = v_near
        else:
            wp[1:9, 9] = w_near + absent[face] * wp[1:9, 8]
            vy[:, 9] = v_near

    for i in (0, 7):
        start(i, range(8))

    @pl.loop(1, 7)
    def _(i):
        start(i, (0, 7))

    def send_field(k):
        pack_faces(k, [q[k, 8, 1:9], q[k, 1, 1:9], q[k, 1:9, 8], q[k, 1:9, 1]])
        start_faces(k)

    def send_deep(k):
        pack_faces(3 + k, [q[k, 7, 1:9], q[k, 2, 1:9], q[k, 1:9, 7], q[k, 1:9, 2]])
        start_faces(3 + k)

    send_field(0)

    def apply_local(k):
        @pl.loop(0, 8)
        def _(i):
            for j in range(8):
                c = q[k, i + 1, j + 1]
                low, high = beside_z(c, zf[2 * k, i, j : j + 1], zf[2 * k + 1, i, j : j + 1])
                near = [
                    q[k, i, j + 1],
                    q[k, i + 2, j + 1],
                    q[k, i + 1, j],
                    q[k, i + 1, j + 2],
                    low,
                    high,
                ]
                value = c
                for face in range(6):
                    value = value - cs[face, i, j] * near[face]
                q[k + 1, i + 1, j + 1] = value

    def add_far(k):
        far = [unpacked(k, face) for face in range(4)]
        q[k, 0, 1:9] += far[0]
        q[k, 9, 1:9] += far[1]
        q[k, 1:9, 0] += far[2]
        q[k, 1:9, 9] += far[3]
        q[k + 1, 1, 1:9] -= cs[0, 0] * far[0]
        q[k + 1, 8, 1:9] -= cs[1, 7] * far[1]
        q[k + 1, 1:9, 1] -= cs[2, :, 0] * far[2]
        q[k + 1, 1:9, 8] -= cs[3, :, 7] * far[3]

    def products(k):
        def body(i, totals):
            even, odd = totals
            for j in range(8):
                c = q[k, i + 1, j + 1]
                scaled = dg[i, j] * c
                even = even + c * scaled
                odd = odd + q[k + 1, i + 1, j + 1] * scaled
            return even, odd

        return lax.fori_loop(0, 8, body, (zero, zero))

    def read_z(k):
        return lambda i, j: q[k, i + 1, j + 1]

    def flux_local(which):
        base = which == 0
        k = which - 1

        @pl.loop(0, 8)
        def _(i):
            sum_x = zero
            sum_z = zero
            sum_d = zero
            for j in range(8):
                if base:
                    smoke = dn[i, j]
                    sum_x = sum_x + smoke * vx[i + 1, j]
                    sum_z = sum_z + smoke * vz[i, j]
                    sum_d = sum_d + smoke
                    if j == 0:
                        fy[1, i] = smoke * vy[i, 1]
                    if j == 7:
                        fy[2, i] = smoke * vy[i, 8]
                else:
                    half = hd[i, j]
                    low, high = beside_z(
                        q[k, i + 1, j + 1], zf[2 * k, i, j : j + 1], zf[2 * k + 1, i, j : j + 1]
                    )
                    sum_x = sum_x + half * (q[k, i + 2, j + 1] - q[k, i, j + 1])
                    sum_z = sum_z + half * (high - low)
                    if j == 0:
                        fy[1, i] = half * (q[k, i + 1, 2] - q[k, i + 1, 0])
                    if j == 7:
                        fy[2, i] = half * (q[k, i + 1, 9] - q[k, i + 1, 7])
            sx[i + 1] = sum_x
            sz[i] = sum_z
            if base:
                sd[i] = sum_d
            zt[0, 0, pl.ds(i, 1), :] = sum_z[7:8]
            zt[1, 0, pl.ds(i, 1), :] = sum_z[0:1]

    def flux_finish(which):
        base = which == 0
        k = which - 1

        def far(face):
            if base:
                return rf[face, 2] * rf[face, 1]
            deep = unpacked(3 + k, face)
            change = [
                lambda: q[k, 1, 1:9] - deep,
                lambda: deep - q[k, 8, 1:9],
                lambda: q[k, 1:9, 1] - deep,
                lambda: deep - q[k, 1:9, 8],
            ][face]()
            return rf[face, 3] * change

        if not base:
            take_faces(3 + k)
        sx[0] = jnp.sum(far(0), axis=0)
        sx[9] = jnp.sum(far(1), axis=0)
        fy[0] = far(2)
        fy[3] = far(3)

        fy[0] += cube(pick(flat(fy[2]), gl[2]))
        fy[3] += cube(pick(flat(fy[1]), gl[3]))

        def pick_8(x, hot):
            return pick(jnp.concatenate([x, x], axis=0), hot)[:8]

        sx[0] += pick_8(sx[8], gl[0])
        sx[9] += pick_8(sx[1], gl[1])
        z_low = pick_8(zt[0, 0], gl[4])
        z_high = pick_8(zt[1, 0], gl[5])
        for i in range(8):
            low, high = beside_z(sz[i], z_low[i : i + 1], z_high[i : i + 1])
            change = (
                (sx[i + 2] - sx[i])
                + ((fy[3, i] + fy[2, i]) - (fy[1, i] + fy[0, i]))
                + (high - low)
            )
            change = (0.5 * advect_step) * change
            col[8 * i : 8 * i + 8] = marched * (sd[i] - change if base else change)
        columns = parts(col[...])
        total = into_slots(columns[:64]) + into_slots(columns[64:128]) + into_slots(columns[128:])
        das[which] = total.reshape(n_dev, 8, 128)
        dar[which, 0] = das[which, d]

    def send_columns(which):
        @pl.loop(1, n_dev)
        def _(i):
            data_copy(which, i).start()

    def flux_columns(which):
        flux_local(which)
        flux_finish(which)

    send_deep(0)
    fill_z_tables(read_z(0))
    local_faces(0)
    apply_local(0)
    take_faces(6)
    for face in range(4):
        smoke_far = unpacked(6, face)
        rf[face, 2] = smoke_far
        rf[face, 3] = 0.5 * smoke_far * rf[face, 0]

    @pl.loop(0, 8)
    def _(i):
        for j in range(8):
            hd[i, j] = 0.5 * dn[i, j] * wp[i + 1, j + 1]

    flux_columns(0)
    pl.semaphore_wait(relay_sem.at[1], len(two_away))

    @pl.loop(1, n_dev)
    def _(i):
        ids_copy(i).start()

    send_columns(0)
    take_faces(0)
    add_far(0)
    send_field(1)

    send_deep(1)
    fill_z_tables(read_z(1))
    local_faces(1)
    apply_local(1)
    flux_columns(1)
    send_columns(1)
    m0, m1 = products(0)
    take_faces(1)
    add_far(1)
    send_field(2)

    send_deep(2)
    fill_z_tables(read_z(2))
    local_faces(2)
    apply_local(2)
    flux_columns(2)
    send_columns(2)
    m2, m3 = products(1)
    m4, m5 = products(2)
    flux_local(3)

    take_faces(2)
    far = [unpacked(2, face) for face in range(4)]
    m5_far = zero
    for j in range(8):
        m5_far = m5_far + dg[0, j] * cs[0, 0, j] * far[0][j] * q[2, 1, j + 1]
        m5_far = m5_far + dg[7, j] * cs[1, 7, j] * far[1][j] * q[2, 8, j + 1]
        m5_far = m5_far + dg[j, 0] * cs[2, j, 0] * far[2][j] * q[2, j + 1, 1]
        m5_far = m5_far + dg[j, 7] * cs[3, j, 7] * far[3][j] * q[2, j + 1, 8]

    moments = [m0, m1, m2, m3, m4, m5 - m5_far]
    lanes = lax.broadcasted_iota(jnp.int32, (1, 128), 1)
    row = jnp.zeros((1, 128), F32)
    for k in range(6):
        line = jnp.sum(moments[k], axis=0, keepdims=True)
        line = jnp.sum(line[:, :128] + line[:, 128:], axis=1, keepdims=True)
        row = jnp.where(lanes == k, line, row)
    a1s[...] = row
    for i in range(1, n_grp):
        to_grp(0, a1s, a1r.at[i], i).start()

    q[2, 0, 1:9] += far[0]
    q[2, 9, 1:9] += far[1]
    q[2, 1:9, 0] += far[2]
    q[2, 1:9, 9] += far[3]
    for j in range(8):
        sx[1] -= hd[0, j] * far[0][j]
        sx[8] += hd[7, j] * far[1][j]
        fy[1, j] -= hd[j, 0] * far[2][j]
        fy[2, j] += hd[j, 7] * far[3][j]
    flux_finish(3)
    send_columns(3)

    partial = a1s[...]
    for i in range(1, n_grp):
        to_grp(0, a1s, a1r.at[i], i).wait_recv()
        partial = partial + a1r[i]
    a2s[...] = partial

    @pl.loop(1, n_dev)
    def _(i):
        sum_copy(i).start()

    @pl.loop(1, n_dev)
    def _(i):
        ids_copy(i).wait_recv()

    marks = jnp.concatenate([spread(idr[i], 8) for i in range(n_dev)], axis=0)
    mark_lane = lax.broadcasted_iota(jnp.int32, (rows, 128), 1)
    mark_row = lax.broadcasted_iota(jnp.int32, (rows, 128), 0) % 8
    first_mark = jnp.sum(jnp.where(mark_lane == mark_row, marks, 0.0), axis=1, keepdims=True)
    second_mark = jnp.sum(
        jnp.where(mark_lane == mark_row + 8, marks, 0.0), axis=1, keepdims=True
    )
    lane_b = lax.broadcasted_iota(jnp.int32, (rows, BLOCKS), 1).astype(F32)
    first_hot = hot_of(first_mark == lane_b)
    second_hot = hot_of(second_mark == lane_b)

    def image_copy(which, i):
        return to_grp(1 + which, pix.at[which, lax.rem(g + i, n_grp)], imr.at[which, i], i)

    def send_pixels(which):
        got = parts(dar[which].reshape(rows, 128).T)
        image = joined(jnp.dot(got, first_hot, preferred_element_type=F32))[:64]
        image = image + joined(jnp.dot(got, second_hot, preferred_element_type=F32))[64:]
        pix[which] = image.reshape(8, 8, BLOCKS)
        for i in range(1, n_grp):
            image_copy(which, i).start()

    @pl.loop(1, n_dev)
    def _(i):
        ids_copy(i).wait_send()
        for which in range(3):
            data_copy(which, i).wait_send()
            data_copy(which, i).wait_recv()

    for which in range(3):
        send_pixels(which)

    @pl.loop(1, n_dev)
    def _(i):
        data_copy(3, i).wait_recv()

    send_pixels(3)

    @pl.loop(1, n_dev)
    def _(i):
        sum_copy(i).wait_recv()

    whole = partial
    for i in range(1, n_dev):
        whole = whole + a2r[i]
    m = [
        jnp.broadcast_to(
            jnp.sum(jnp.where(lanes == k, whole, 0.0), axis=1, keepdims=True), (1, 128)
        )
        for k in range(6)
    ]
    l10 = m[2] / m[1]
    l20 = m[3] / m[1]
    d1 = m[3] - l10 * m[2]
    t21 = m[4] - l20 * m[2]
    l21 = t21 / d1
    d2 = m[5] - l20 * m[3] - l21 * t21
    y1 = m[1] - l10 * m[0]
    y2 = m[2] - l20 * m[0] - l21 * y1
    c2 = y2 / d2
    c1 = y1 / d1 - l21 * c2
    c0 = m[0] / m[1] - l10 * c1 - l20 * c2
    coefs = [jnp.concatenate([spread(c, 8), spread(c, 8)], axis=1) for c in (c0, c1, c2)]
    def mixed(read):
        return coefs[0] * read(0) + coefs[1] * read(1) + coefs[2] * read(2)

    @pl.loop(0, 8)
    def _(i):
        pp[0, i + 1] = mixed(lambda k: q[k, 0, i + 1])
        pp[9, i + 1] = mixed(lambda k: q[k, 9, i + 1])
        zf[0, i] = mixed(lambda k: zf[2 * k, i])
        zf[1, i] = mixed(lambda k: zf[2 * k + 1, i])
        for j in range(10):
            pp[i + 1, j] = mixed(lambda k: q[k, i + 1, j])

    @pl.loop(0, 8)
    def _(i):
        for j in range(8):
            c = pp[i + 1, j + 1]
            low, high = beside_z(c, zf[0, i, j : j + 1], zf[1, i, j : j + 1])
            half = 0.5 * wp[i + 1, j + 1]
            newv[0, i, j] = vx[i + 1, j] - half * (pp[i + 2, j + 1] - pp[i, j + 1])
            newv[1, i, j] = vy[i, j + 1] - half * (pp[i + 1, j + 2] - pp[i + 1, j])
            newv[2, i, j] = vz[i, j] - half * (high - low)

    for number in range(8):
        for face in range(4):

            @pl.when(sends[face])
            def _():
                halo(number, face).wait_send()

    for i in range(1, n_grp):
        to_grp(0, a1s, a1r.at[i], i).wait_send()

    @pl.loop(1, n_dev)
    def _(i):
        sum_copy(i).wait_send()
        data_copy(3, i).wait_send()

    optical = zero
    for which in range(4):
        layer_sum = pix[which, g]
        for i in range(1, n_grp):
            image_copy(which, i).wait_recv()
            layer_sum = layer_sum + imr[which, i]
        optical = optical + (layer_sum if which == 0 else coefs[which - 1] * layer_sum)
    shade = 1.0 - jnp.exp(-optical)
    for row in range(8):
        rendered[:, BLOCKS * row : BLOCKS * (row + 1)] = shade[row : row + 1]
    for which in range(4):
        for i in range(1, n_grp):
            image_copy(which, i).wait_send()


def solution(mesh):
    n_grp, n_dev = mesh.shape["grp"], mesh.shape["dev"]

    def step(
        velocity, density, inverse_density, neighbours, leaf_layer, leaf_tile, leaf_block, samples
    ):
        vmem = pl.BlockSpec(memory_space=pltpu.VMEM)
        anywhere = pl.BlockSpec(memory_space=pl.ANY)
        smem = pl.BlockSpec(memory_space=pltpu.SMEM)
        new_velocity, rendered = pl.pallas_call(
            functools.partial(kernel, n_grp, n_dev),
            out_shape=(
                pltpu.VMEM((3, 8, 8, 8, L), F32),
                pltpu.VMEM((1, 8 * BLOCKS), F32),
            ),
            in_specs=[anywhere] * 7 + [smem],
            out_specs=(vmem, vmem),
            scratch_shapes=[
                pltpu.VMEM((6, L), jnp.int32),
                pltpu.VMEM((3, 1, L), jnp.int32),
                pltpu.VMEM((10, 10, 8, L), F32),
                pltpu.VMEM((10, 8, 8, L), F32),
                pltpu.VMEM((8, 10, 8, L), F32),
                pltpu.VMEM((8, 8, 8, L), F32),
                pltpu.VMEM((8, 8, 8, L), F32),
                pltpu.VMEM((8, 8, 8, L), F32),
                pltpu.VMEM((4, 10, 10, 8, L), F32),
                pltpu.VMEM((6, 8, 8, L), F32),
                pltpu.VMEM((2, 8, 8, L), F32),
                pltpu.VMEM((6, 8, 8, 8, L), F32),
                pltpu.VMEM((8, 8, 8, L), F32),
                pltpu.VMEM((10, 10, 8, L), F32),
                pltpu.VMEM((6, L, L), BF16),
                pltpu.VMEM((4, 2, 2 * FACE, L), BF16),
                pltpu.VMEM((4, 2, 2 * FACE, L), BF16),
                pltpu.VMEM((4, 4, 8, 8, L), F32),
                pltpu.VMEM((7, 4, FACE // 2, 128), F32),
                pltpu.VMEM((7, 4, FACE // 2, 128), F32),
                pltpu.VMEM((4, FACE, 128), F32),
                pltpu.VMEM((4, FACE, 128), F32),
                pltpu.VMEM((1, 128), F32),
                pltpu.VMEM((n_grp, 1, 128), F32),
                pltpu.VMEM((1, 128), F32),
                pltpu.VMEM((n_dev, 1, 128), F32),
                pltpu.VMEM((n_dev, 1, 128), F32),
                pltpu.VMEM((n_dev, 1, 128), F32),
                pltpu.VMEM((4, n_dev, 8, 128), F32),
                pltpu.VMEM((4, n_dev, 8, 128), F32),
                pltpu.VMEM((4, 8, 8, BLOCKS), F32),
                pltpu.VMEM((4, n_grp, 8, BLOCKS), F32),
                pltpu.VMEM((10, 8, L), F32),
                pltpu.VMEM((4, 8, 8, L), F32),
                pltpu.VMEM((8, 8, L), F32),
                pltpu.VMEM((8, 8, L), F32),
                pltpu.VMEM((64, L), F32),
                pltpu.SemaphoreType.DMA((9,)),
                pltpu.SemaphoreType.DMA((8, 4)),
                pltpu.SemaphoreType.DMA((8, 4)),
                pltpu.SemaphoreType.DMA((5, n_grp)),
                pltpu.SemaphoreType.DMA((5, n_grp)),
                pltpu.SemaphoreType.DMA((6, n_dev)),
                pltpu.SemaphoreType.DMA((6, n_dev)),
                pltpu.SemaphoreType.REGULAR((2,)),
            ],
            compiler_params=pltpu.CompilerParams(
                collective_id=0, has_side_effects=True, vmem_limit_bytes=(64 * 1024 - 2048) * 1024
            ),
        )(
            velocity.reshape(3, 8, 8, 8, L),
            density.reshape(8, 8, 8, L),
            inverse_density.reshape(8, 8, 8, L),
            neighbours,
            leaf_layer.reshape(1, L),
            leaf_tile.reshape(1, L),
            leaf_block.reshape(1, L),
            samples,
        )
        return new_velocity.reshape(3, 512, L), rendered

    return jax.shard_map(
        step,
        mesh=mesh,
        in_specs=(
            P(None, None, ("grp", "dev")),
            P(None, ("grp", "dev")),
            P(None, ("grp", "dev")),
            P(None, ("grp", "dev")),
            P(("grp", "dev")),
            P(("grp", "dev"), None),
            P(("grp", "dev")),
            P(),
        ),
        out_specs=(P(None, None, ("grp", "dev")), P("dev", "grp")),
        check_vma=False,
    )
```

```python
import functools

import jax
import jax.numpy as jnp
from jax import lax
from jax.experimental import pallas as pl
from jax.experimental.pallas import tpu as pltpu
from jax.sharding import PartitionSpec as P

BLOCKS = 256
advect_step = 0.2
ray_step = 0.03
L = 256
FACE = 64
CAP = 16
F32 = jnp.float32
BF16 = jnp.bfloat16
MESH = pl.DeviceIdType.MESH


def parts(x):
    hi = x.astype(BF16)
    rest = x - hi.astype(F32)
    mid = rest.astype(BF16)
    low = (rest - mid.astype(F32)).astype(BF16)
    return jnp.concatenate([hi, mid, low], axis=0)


def joined(y):
    rows = y.shape[0] // 3
    return y[:rows] + y[rows : 2 * rows] + y[2 * rows :]


def pick(x, hot):
    return joined(jnp.dot(parts(x), hot, preferred_element_type=F32))


def pick_t(x, hot):
    return joined(
        lax.dot_general(parts(x), hot, (((1,), (1,)), ((), ())), preferred_element_type=F32)
    )


def spread(row, rows):
    return jnp.broadcast_to(row, (rows, row.shape[1]))


def hot_of(condition):
    return jnp.where(condition, 1.0, 0.0).astype(BF16)


def kernel(
    n_grp,
    n_dev,
    vel,
    dens,
    inv,
    nbr_any,
    layer_any,
    tile_any,
    block_any,
    samples,
    newv,
    rendered,
    nbr,
    rows_in,
    wp,
    vx,
    vy,
    vz,
    dn,
    hd,
    q,
    zf,
    zt,
    cs,
    dg,
    pp,
    gl,
    cp,
    er,
    rf,
    sb,
    rb,
    sbw,
    rbw,
    a1s,
    a1r,
    a2s,
    a2r,
    ids,
    idr,
    das,
    dar,
    pix,
    imr,
    sx,
    fy,
    sz,
    sd,
    col,
    in_sem,
    hs_sem,
    hr_sem,
    gs_sem,
    gr_sem,
    ds_sem,
    dr_sem,
    relay_sem,
):
    g = lax.axis_index("grp")
    d = lax.axis_index("dev")
    me = g * n_dev + d

    def grp_at(step):
        return (lax.rem(g + step, n_grp), d)

    def dev_at(step):
        return (g, lax.rem(d + step, n_dev))

    def torus_at(step_x, step_z):
        x = lax.rem(d // 8 + step_x, n_dev // 8)
        return (g, x * 8 + lax.rem(lax.rem(d, 8) + step_z, 8))

    two_away = [torus_at(0, 2), torus_at(0, 6), torus_at(2, 0)] + [
        torus_at(x, z) for x in (1, n_dev // 8 - 1) for z in (1, 7)
    ]
    greeted = [torus_at(0, 1), torus_at(0, 7), torus_at(1, 0), torus_at(n_dev // 8 - 1, 0)]
    greeted = [grp_at(i) for i in range(1, n_grp)] + greeted + two_away
    barrier = pltpu.get_barrier_semaphore()
    for who in greeted:
        pl.semaphore_signal(barrier, inc=1, device_id=who, device_id_type=MESH)

    def relay(number):
        for who in two_away:
            pl.semaphore_signal(
                relay_sem.at[number], inc=1, device_id=who, device_id_type=MESH
            )

    small = [
        pltpu.make_async_copy(nbr_any, nbr, in_sem.at[5]),
        pltpu.make_async_copy(tile_any, rows_in.at[0], in_sem.at[6]),
        pltpu.make_async_copy(block_any, rows_in.at[1], in_sem.at[7]),
        pltpu.make_async_copy(layer_any, rows_in.at[2], in_sem.at[8]),
    ]
    loads = [
        pltpu.make_async_copy(inv, wp.at[pl.ds(1, 8), pl.ds(1, 8)], in_sem.at[0]),
        pltpu.make_async_copy(vel.at[0], vx.at[pl.ds(1, 8)], in_sem.at[1]),
        pltpu.make_async_copy(vel.at[1], vy.at[:, pl.ds(1, 8)], in_sem.at[2]),
        pltpu.make_async_copy(dens, dn, in_sem.at[3]),
        pltpu.make_async_copy(vel.at[2], vz, in_sem.at[4]),
    ]
    for load in small + loads:
        load.start()

    to = [dev_at(1), dev_at(n_dev - 1), grp_at(1), grp_at(n_grp - 1)]
    sends = [d < n_dev - 1, d > 0, g < n_grp - 1, g > 0]
    takes = [d > 0, d < n_dev - 1, g > 0, g < n_grp - 1]

    for face in range(4):

        @pl.when(jnp.logical_not(takes[face]))
        def _():
            rb[:, face] = jnp.zeros((7, FACE // 2, 128), F32)
            rbw[face] = jnp.zeros((FACE, 128), F32)

    for load in small:
        load.wait()

    table = nbr[...]
    present = table >= 0
    local = present & ((table // L) == me)
    remote = present & ((table // L) != me)
    slot = table % L
    local_slot = jnp.where(local, slot, -1)
    remote_slot = jnp.where(remote, slot, -1)
    sub = lax.broadcasted_iota(jnp.int32, (L, L), 0)
    lane = lax.broadcasted_iota(jnp.int32, (L, L), 1)
    upper = hot_of(sub < lane)
    sub128 = lax.broadcasted_iota(jnp.int32, (2 * FACE, L), 0)
    tile_row = rows_in[0]
    tile_hot = hot_of(
        lax.broadcasted_iota(jnp.int32, (n_dev, L), 0) == spread(tile_row, n_dev)
    )
    before = jnp.dot(
        jnp.concatenate([tile_hot, hot_of(remote), jnp.zeros((10, L), BF16)], axis=0),
        upper,
        preferred_element_type=F32,
    )
    for face in range(4):
        out_face = face ^ 1
        place = before[n_dev + out_face : n_dev + out_face + 1].astype(jnp.int32)
        place = jnp.where(remote_slot[out_face : out_face + 1] >= 0, place, -1000)
        cp[face, 0] = hot_of(sub128 == spread(place, 2 * FACE))
        cp[face, 1] = hot_of(sub128 == spread(place + FACE, 2 * FACE))

    for load in loads[:4]:
        load.wait()

    def flat(x):
        return x.reshape(FACE, L)

    def cube(x):
        return x.reshape(8, 8, L)

    def halo(number, face):
        wide = number == 7
        return pltpu.make_async_remote_copy(
            src_ref=sbw.at[face] if wide else sb.at[number, face],
            dst_ref=rbw.at[face] if wide else rb.at[number, face],
            send_sem=hs_sem.at[number, face],
            recv_sem=hr_sem.at[number, face],
            device_id=to[face],
            device_id_type=MESH,
        )

    def start_faces(number):
        for face in range(4):

            @pl.when(sends[face])
            def _():
                halo(number, face).start()

    def pack_faces(number, layers):
        for face in range(4):
            rows_64 = flat(layers[face])
            sb[number, face] = pick_t(rows_64[:32], cp[face, 0]) + pick_t(
                rows_64[32:], cp[face, 1]
            )

    def take_faces(number):
        for face in range(4):

            @pl.when(takes[face])
            def _():
                halo(number, face).wait_recv()

    def unpacked(number, face):
        got = parts(rb[number, face])
        top = joined(jnp.dot(got, er[face, 0], preferred_element_type=F32))
        bottom = joined(jnp.dot(got, er[face, 1], preferred_element_type=F32))
        return cube(jnp.concatenate([top, bottom], axis=0))

    first = [wp[8, 1:9], wp[1, 1:9], wp[1:9, 8], wp[1:9, 1]]
    second = [vx[8], vx[1], vy[:, 8], vy[:, 1]]
    for face in range(4):
        sbw[face] = pick_t(flat(first[face]), cp[face, 0]) + pick_t(
            flat(second[face]), cp[face, 1]
        )

    pl.semaphore_wait(barrier, len(greeted))
    start_faces(7)
    relay(0)
    pack_faces(6, [dn[7], dn[0], dn[:, 7], dn[:, 0]])
    start_faces(6)

    for face in range(6):
        gl[face] = hot_of(sub == spread(local_slot[face : face + 1], L))
    for face in range(4):
        mine = remote_slot[face : face + 1]
        occupied = jnp.sum(
            jnp.where(sub == spread(mine, L), 1.0, 0.0), axis=1, keepdims=True
        )
        rank = jnp.sum(
            jnp.where(sub < spread(mine, L), occupied, 0.0), axis=0, keepdims=True
        ).astype(jnp.int32)
        rank = jnp.where(mine >= 0, rank, -1000)
        er[face, 0] = hot_of(sub128 == spread(rank, 2 * FACE))
        er[face, 1] = hot_of(sub128 == spread(rank + FACE, 2 * FACE))

    rank = jnp.sum(
        jnp.where(tile_hot > 0, before[:n_dev], 0.0), axis=0, keepdims=True
    ).astype(jnp.int32)
    rows = n_dev * 8
    sub_key = lax.broadcasted_iota(jnp.int32, (rows, L), 0)
    first_key = jnp.where(rank < 8, tile_row * 8 + rank, -1)
    second_key = jnp.where(rank >= 8, tile_row * 8 + rank - 8, -1)
    slot_hot = jnp.concatenate(
        [hot_of(sub_key == spread(first_key, rows)), hot_of(sub_key == spread(second_key, rows))],
        axis=1,
    )

    def into_slots(values):
        empty = jnp.zeros_like(values)
        packed = jnp.concatenate(
            [
                jnp.concatenate([values, empty], axis=1),
                jnp.concatenate([empty, values], axis=1),
            ],
            axis=0,
        )
        return lax.dot_general(
            slot_hot, packed, (((1,), (1,)), ((), ())), preferred_element_type=F32
        )

    def to_dev(number, src, dst, i):
        return pltpu.make_async_remote_copy(
            src_ref=src,
            dst_ref=dst,
            send_sem=ds_sem.at[number],
            recv_sem=dr_sem.at[number],
            device_id=dev_at(i),
            device_id_type=MESH,
        )

    def to_grp(number, src, dst, i):
        return pltpu.make_async_remote_copy(
            src_ref=src,
            dst_ref=dst,
            send_sem=gs_sem.at[number],
            recv_sem=gr_sem.at[number],
            device_id=grp_at(i),
            device_id_type=MESH,
        )

    def all_dev(number):
        got = [idr, a2r, dar.at[0], dar.at[1], dar.at[2], dar.at[3]][number]
        got = got.at[pl.ds(1, n_dev - 1)]
        return to_dev(number, got, got, 1)

    def all_grp(number):
        got = [a1r, imr.at[0], imr.at[1], imr.at[2], imr.at[3]][number]
        got = got.at[pl.ds(1, n_grp - 1)]
        return to_grp(number, got, got, 1)

    def ids_copy(i):
        return to_dev(0, ids.at[lax.rem(d + i, n_dev)], idr.at[i], i)

    def sum_copy(i):
        return to_dev(1, a2s, a2r.at[i], i)

    def data_copy(which, i):
        return to_dev(2 + which, das.at[which, lax.rem(d + i, n_dev)], dar.at[which, i], i)

    marked = jnp.where(
        lax.broadcasted_iota(jnp.int32, (128, L), 0) == spread(rank, 128),
        spread(rows_in[1], 128),
        0,
    )
    marked = lax.dot_general(
        tile_hot,
        marked.astype(F32).astype(BF16),
        (((1,), (1,)), ((), ())),
        preferred_element_type=F32,
    )
    for t in range(n_dev):
        ids[t] = marked[t : t + 1]

    idr[0] = ids[d]
    limit = jnp.zeros((1, L), jnp.int32)
    for t in range(n_dev):
        limit = jnp.where(tile_row == t, samples[t], limit)
    marched = jnp.where(rows_in[2] < limit, ray_step, 0.0)

    loads[4].wait()

    def fill_z_tables(read):
        @pl.loop(0, 8)
        def _(i):
            for j in range(8):
                c = read(i, j)
                zt[0, i, j : j + 1, :] = c[7:8]
                zt[1, i, j : j + 1, :] = c[0:1]

    def local_faces(k):
        q[k, 0, 1:9] = cube(pick(flat(q[k, 8, 1:9]), gl[0]))
        q[k, 9, 1:9] = cube(pick(flat(q[k, 1, 1:9]), gl[1]))
        q[k, 1:9, 0] = cube(pick(flat(q[k, 1:9, 8]), gl[2]))
        q[k, 1:9, 9] = cube(pick(flat(q[k, 1:9, 1]), gl[3]))
        zf[2 * k] = cube(pick(flat(zt[0]), gl[4]))
        zf[2 * k + 1] = cube(pick(flat(zt[1]), gl[5]))

    fill_z_tables(lambda i, j: vz[i, j])
    zf[2] = cube(pick(flat(zt[0]), gl[4]))
    zf[3] = cube(pick(flat(zt[1]), gl[5]))
    fill_z_tables(lambda i, j: wp[i + 1, j + 1])
    absent = [jnp.where(present[face : face + 1], 0.0, 1.0) for face in range(6)]
    zf[0] = cube(pick(flat(zt[0]), gl[4]))
    zf[1] = cube(pick(flat(zt[1]), gl[5]))

    def both(first, second, face):
        return pick(jnp.concatenate([flat(first), flat(second)], axis=0), gl[face])

    near_local = [
        both(wp[8, 1:9], vx[8], 0),
        both(wp[1, 1:9], vx[1], 1),
        both(wp[1:9, 8], vy[:, 8], 2),
        both(wp[1:9, 1], vy[:, 1], 3),
    ]
    k_id = lax.broadcasted_iota(jnp.int32, (8, L), 0)
    at_low = k_id == 0
    at_high = k_id == 7
    zero = jnp.zeros((8, L), F32)

    def beside_z(c, low, high):
        return (
            jnp.where(at_low, low, pltpu.roll(c, 1, 0)),
            jnp.where(at_high, high, pltpu.roll(c, 7, 0)),
        )

    def start(i, columns):
        for j in columns:
            c = wp[i + 1, j + 1]
            low, high = beside_z(
                c,
                zf[0, i, j : j + 1] + absent[4] * c[0:1],
                zf[1, i, j : j + 1] + absent[5] * c[7:8],
            )
            near = [wp[i, j + 1], wp[i + 2, j + 1], wp[i + 1, j], wp[i + 1, j + 2], low, high]
            coupling = [0.5 * (c + value) for value in near]
            diagonal = (
                coupling[0] + coupling[1] + coupling[2] + coupling[3] + coupling[4] + coupling[5]
            )
            inverse = 1.0 / diagonal
            dg[i, j] = diagonal
            for face in range(6):
                cs[face, i, j] = coupling[face] * inverse
            v = vz[i, j]
            low, high = beside_z(v, zf[2, i, j : j + 1], zf[3, i, j : j + 1])
            source = -0.5 * (
                (vx[i + 2, j] - vx[i, j]) + (vy[i, j + 2] - vy[i, j]) + (high - low)
            )
            q[0, i + 1, j + 1] = source * inverse

    @pl.loop(1, 7)
    def _(i):
        start(i, range(1, 7))

    take_faces(7)
    pl.semaphore_wait(relay_sem.at[0], len(two_away))
    relay(1)
    for face in range(4):
        got = parts(rbw[face])
        w_far = joined(jnp.dot(got, er[face, 0], preferred_element_type=F32))
        v_far = joined(jnp.dot(got, er[face, 1], preferred_element_type=F32))
        rf[face, 0] = cube(w_far)
        rf[face, 1] = cube(v_far)
        w_near = cube(near_local[face][:FACE] + w_far)
        v_near = cube(near_local[face][FACE:] + v_far)
        if face == 0:
            wp[0, 1:9] = w_near + absent[face] * wp[1, 1:9]
            vx[0] = v_near
        elif face == 1:
            wp[9, 1:9] = w_near + absent[face] * wp[8, 1:9]
            vx[9] = v_near
        elif face == 2:
            wp[1:9, 0] = w_near + absent[face] * wp[1:9, 1]
            vy[:, 0] = v_near
        else:
            wp[1:9, 9] = w_near + absent[face] * wp[1:9, 8]
            vy[:, 9] = v_near

    for i in (0, 7):
        start(i, range(8))

    @pl.loop(1, 7)
    def _(i):
        start(i, (0, 7))

    def send_field(k):
        pack_faces(k, [q[k, 8, 1:9], q[k, 1, 1:9], q[k, 1:9, 8], q[k, 1:9, 1]])
        start_faces(k)

    def send_deep(k):
        pack_faces(3 + k, [q[k, 7, 1:9], q[k, 2, 1:9], q[k, 1:9, 7], q[k, 1:9, 2]])
        start_faces(3 + k)

    send_field(0)

    def apply_local(k):
        @pl.loop(0, 8)
        def _(i):
            for j in range(8):
                c = q[k, i + 1, j + 1]
                low, high = beside_z(c, zf[2 * k, i, j : j + 1], zf[2 * k + 1, i, j : j + 1])
                near = [
                    q[k, i, j + 1],
                    q[k, i + 2, j + 1],
                    q[k, i + 1, j],
                    q[k, i + 1, j + 2],
                    low,
                    high,
                ]
                value = c
                for face in range(6):
                    value = value - cs[face, i, j] * near[face]
                q[k + 1, i + 1, j + 1] = value

    def add_far(k):
        far = [unpacked(k, face) for face in range(4)]
        q[k, 0, 1:9] += far[0]
        q[k, 9, 1:9] += far[1]
        q[k, 1:9, 0] += far[2]
        q[k, 1:9, 9] += far[3]
        q[k + 1, 1, 1:9] -= cs[0, 0] * far[0]
        q[k + 1, 8, 1:9] -= cs[1, 7] * far[1]
        q[k + 1, 1:9, 1] -= cs[2, :, 0] * far[2]
        q[k + 1, 1:9, 8] -= cs[3, :, 7] * far[3]

    def products(k):
        def body(i, totals):
            even, odd = totals
            for j in range(8):
                c = q[k, i + 1, j + 1]
                scaled = dg[i, j] * c
                even = even + c * scaled
                odd = odd + q[k + 1, i + 1, j + 1] * scaled
            return even, odd

        return lax.fori_loop(0, 8, body, (zero, zero))

    def read_z(k):
        return lambda i, j: q[k, i + 1, j + 1]

    def flux_local(which):
        base = which == 0
        k = which - 1

        @pl.loop(0, 8)
        def _(i):
            sum_x = zero
            sum_z = zero
            sum_d = zero
            for j in range(8):
                if base:
                    smoke = dn[i, j]
                    sum_x = sum_x + smoke * vx[i + 1, j]
                    sum_z = sum_z + smoke * vz[i, j]
                    sum_d = sum_d + smoke
                    if j == 0:
                        fy[1, i] = smoke * vy[i, 1]
                    if j == 7:
                        fy[2, i] = smoke * vy[i, 8]
                else:
                    half = hd[i, j]
                    low, high = beside_z(
                        q[k, i + 1, j + 1], zf[2 * k, i, j : j + 1], zf[2 * k + 1, i, j : j + 1]
                    )
                    sum_x = sum_x + half * (q[k, i + 2, j + 1] - q[k, i, j + 1])
                    sum_z = sum_z + half * (high - low)
                    if j == 0:
                        fy[1, i] = half * (q[k, i + 1, 2] - q[k, i + 1, 0])
                    if j == 7:
                        fy[2, i] = half * (q[k, i + 1, 9] - q[k, i + 1, 7])
            sx[i + 1] = sum_x
            sz[i] = sum_z
            if base:
                sd[i] = sum_d
            zt[0, 0, pl.ds(i, 1), :] = sum_z[7:8]
            zt[1, 0, pl.ds(i, 1), :] = sum_z[0:1]

        def pick_8(x, hot):
            return pick(jnp.concatenate([x, x], axis=0), hot)[:8]

        sx[0] = pick_8(sx[8], gl[0])
        sx[9] = pick_8(sx[1], gl[1])
        fy[0] = cube(pick(flat(fy[2]), gl[2]))
        fy[3] = cube(pick(flat(fy[1]), gl[3]))
        z_low = pick_8(zt[0, 0], gl[4])
        z_high = pick_8(zt[1, 0], gl[5])
        for i in range(8):
            low, high = beside_z(sz[i], z_low[i : i + 1], z_high[i : i + 1])
            sz[i] = high - low

    def flux_finish(which):
        base = which == 0
        k = which - 1

        def far(face):
            if base:
                return rf[face, 2] * rf[face, 1]
            deep = unpacked(3 + k, face)
            change = [
                lambda: q[k, 1, 1:9] - deep,
                lambda: deep - q[k, 8, 1:9],
                lambda: q[k, 1:9, 1] - deep,
                lambda: deep - q[k, 1:9, 8],
            ][face]()
            return rf[face, 3] * change

        if not base:
            take_faces(3 + k)
        sx[0] += jnp.sum(far(0), axis=0)
        sx[9] += jnp.sum(far(1), axis=0)
        fy[0] += far(2)
        fy[3] += far(3)

        for i in range(8):
            change = (
                (sx[i + 2] - sx[i])
                + ((fy[3, i] + fy[2, i]) - (fy[1, i] + fy[0, i]))
                + sz[i]
            )
            change = (0.5 * advect_step) * change
            col[8 * i : 8 * i + 8] = marched * (sd[i] - change if base else change)
        columns = parts(col[...])
        total = into_slots(columns[:64]) + into_slots(columns[64:128]) + into_slots(columns[128:])
        das[which] = total.reshape(n_dev, 8, 128)
        dar[which, 0] = das[which, d]

    def send_columns(which):
        @pl.loop(1, n_dev)
        def _(i):
            data_copy(which, i).start()

    def flux_columns(which):
        flux_local(which)
        flux_finish(which)

    send_deep(0)
    fill_z_tables(read_z(0))
    local_faces(0)
    apply_local(0)
    take_faces(6)
    for face in range(4):
        smoke_far = unpacked(6, face)
        rf[face, 2] = smoke_far
        rf[face, 3] = 0.5 * smoke_far * rf[face, 0]

    @pl.loop(0, 8)
    def _(i):
        for j in range(8):
            hd[i, j] = 0.5 * dn[i, j] * wp[i + 1, j + 1]

    flux_columns(0)
    pl.semaphore_wait(relay_sem.at[1], len(two_away))

    @pl.loop(1, n_dev)
    def _(i):
        ids_copy(i).start()

    send_columns(0)
    take_faces(0)
    add_far(0)
    send_field(1)

    send_deep(1)
    flux_columns(1)
    send_columns(1)
    fill_z_tables(read_z(1))
    local_faces(1)
    apply_local(1)
    m0, m1 = products(0)
    take_faces(1)
    add_far(1)
    send_field(2)

    send_deep(2)
    flux_columns(2)
    send_columns(2)
    fill_z_tables(read_z(2))
    local_faces(2)
    apply_local(2)
    m2, m3 = products(1)
    m4, m5 = products(2)
    flux_local(3)

    take_faces(2)
    far = [unpacked(2, face) for face in range(4)]
    for j in range(8):
        sx[1] -= hd[0, j] * far[0][j]
        sx[8] += hd[7, j] * far[1][j]
        fy[1, j] -= hd[j, 0] * far[2][j]
        fy[2, j] += hd[j, 7] * far[3][j]
    flux_finish(3)
    send_columns(3)

    m5_far = zero
    for j in range(8):
        m5_far = m5_far + dg[0, j] * cs[0, 0, j] * far[0][j] * q[2, 1, j + 1]
        m5_far = m5_far + dg[7, j] * cs[1, 7, j] * far[1][j] * q[2, 8, j + 1]
        m5_far = m5_far + dg[j, 0] * cs[2, j, 0] * far[2][j] * q[2, j + 1, 1]
        m5_far = m5_far + dg[j, 7] * cs[3, j, 7] * far[3][j] * q[2, j + 1, 8]

    moments = [m0, m1, m2, m3, m4, m5 - m5_far]
    lanes = lax.broadcasted_iota(jnp.int32, (1, 128), 1)
    row = jnp.zeros((1, 128), F32)
    for k in range(6):
        line = jnp.sum(moments[k], axis=0, keepdims=True)
        line = jnp.sum(line[:, :128] + line[:, 128:], axis=1, keepdims=True)
        row = jnp.where(lanes == k, line, row)
    a1s[...] = row
    for i in range(1, n_grp):
        to_grp(0, a1s, a1r.at[i], i).start()

    q[2, 0, 1:9] += far[0]
    q[2, 9, 1:9] += far[1]
    q[2, 1:9, 0] += far[2]
    q[2, 1:9, 9] += far[3]
    partial = a1s[...]
    all_grp(0).wait_recv()
    for i in range(1, n_grp):
        partial = partial + a1r[i]
    a2s[...] = partial

    @pl.loop(1, n_dev)
    def _(i):
        sum_copy(i).start()

    all_dev(0).wait_recv()

    marks = jnp.concatenate([spread(idr[i], 8) for i in range(n_dev)], axis=0)
    mark_lane = lax.broadcasted_iota(jnp.int32, (rows, 128), 1)
    mark_row = lax.broadcasted_iota(jnp.int32, (rows, 128), 0) % 8
    first_mark = jnp.sum(jnp.where(mark_lane == mark_row, marks, 0.0), axis=1, keepdims=True)
    second_mark = jnp.sum(
        jnp.where(mark_lane == mark_row + 8, marks, 0.0), axis=1, keepdims=True
    )
    lane_b = lax.broadcasted_iota(jnp.int32, (rows, BLOCKS), 1).astype(F32)
    first_hot = hot_of(first_mark == lane_b)
    second_hot = hot_of(second_mark == lane_b)

    def image_copy(which, i):
        return to_grp(1 + which, pix.at[which, lax.rem(g + i, n_grp)], imr.at[which, i], i)

    def send_pixels(which):
        got = parts(dar[which].reshape(rows, 128).T)
        image = joined(jnp.dot(got, first_hot, preferred_element_type=F32))[:64]
        image = image + joined(jnp.dot(got, second_hot, preferred_element_type=F32))[64:]
        pix[which] = image.reshape(8, 8, BLOCKS)
        for i in range(1, n_grp):
            image_copy(which, i).start()

    for which in range(3):
        all_dev(2 + which).wait_recv()
        send_pixels(which)

    all_dev(5).wait_recv()

    send_pixels(3)

    all_dev(1).wait_recv()

    whole = partial
    for i in range(1, n_dev):
        whole = whole + a2r[i]
    m = [
        jnp.broadcast_to(
            jnp.sum(jnp.where(lanes == k, whole, 0.0), axis=1, keepdims=True), (1, 128)
        )
        for k in range(6)
    ]
    l10 = m[2] / m[1]
    l20 = m[3] / m[1]
    d1 = m[3] - l10 * m[2]
    t21 = m[4] - l20 * m[2]
    l21 = t21 / d1
    d2 = m[5] - l20 * m[3] - l21 * t21
    y1 = m[1] - l10 * m[0]
    y2 = m[2] - l20 * m[0] - l21 * y1
    c2 = y2 / d2
    c1 = y1 / d1 - l21 * c2
    c0 = m[0] / m[1] - l10 * c1 - l20 * c2
    coefs = [jnp.concatenate([spread(c, 8), spread(c, 8)], axis=1) for c in (c0, c1, c2)]
    def mixed(read):
        return coefs[0] * read(0) + coefs[1] * read(1) + coefs[2] * read(2)

    @pl.loop(0, 8)
    def _(i):
        pp[0, i + 1] = mixed(lambda k: q[k, 0, i + 1])
        pp[9, i + 1] = mixed(lambda k: q[k, 9, i + 1])
        zf[0, i] = mixed(lambda k: zf[2 * k, i])
        zf[1, i] = mixed(lambda k: zf[2 * k + 1, i])
        for j in range(10):
            pp[i + 1, j] = mixed(lambda k: q[k, i + 1, j])

    @pl.loop(0, 8)
    def _(i):
        for j in range(8):
            c = pp[i + 1, j + 1]
            low, high = beside_z(c, zf[0, i, j : j + 1], zf[1, i, j : j + 1])
            half = 0.5 * wp[i + 1, j + 1]
            newv[0, i, j] = vx[i + 1, j] - half * (pp[i + 2, j + 1] - pp[i, j + 1])
            newv[1, i, j] = vy[i, j + 1] - half * (pp[i + 1, j + 2] - pp[i + 1, j])
            newv[2, i, j] = vz[i, j] - half * (high - low)

    for number in range(8):
        for face in range(4):

            @pl.when(sends[face])
            def _():
                halo(number, face).wait_send()

    all_grp(0).wait_send()

    for number in range(6):
        all_dev(number).wait_send()

    optical = zero
    for which in range(4):
        layer_sum = pix[which, g]
        all_grp(1 + which).wait_recv()
        for i in range(1, n_grp):
            layer_sum = layer_sum + imr[which, i]
        optical = optical + (layer_sum if which == 0 else coefs[which - 1] * layer_sum)
    shade = 1.0 - jnp.exp(-optical)
    for row in range(8):
        rendered[:, BLOCKS * row : BLOCKS * (row + 1)] = shade[row : row + 1]
    for which in range(4):
        all_grp(1 + which).wait_send()


def solution(mesh):
    n_grp, n_dev = mesh.shape["grp"], mesh.shape["dev"]

    def step(
        velocity, density, inverse_density, neighbours, leaf_layer, leaf_tile, leaf_block, samples
    ):
        vmem = pl.BlockSpec(memory_space=pltpu.VMEM)
        anywhere = pl.BlockSpec(memory_space=pl.ANY)
        smem = pl.BlockSpec(memory_space=pltpu.SMEM)
        new_velocity, rendered = pl.pallas_call(
            functools.partial(kernel, n_grp, n_dev),
            out_shape=(
                pltpu.VMEM((3, 8, 8, 8, L), F32),
                pltpu.VMEM((1, 8 * BLOCKS), F32),
            ),
            in_specs=[anywhere] * 7 + [smem],
            out_specs=(vmem, vmem),
            scratch_shapes=[
                pltpu.VMEM((6, L), jnp.int32),
                pltpu.VMEM((3, 1, L), jnp.int32),
                pltpu.VMEM((10, 10, 8, L), F32),
                pltpu.VMEM((10, 8, 8, L), F32),
                pltpu.VMEM((8, 10, 8, L), F32),
                pltpu.VMEM((8, 8, 8, L), F32),
                pltpu.VMEM((8, 8, 8, L), F32),
                pltpu.VMEM((8, 8, 8, L), F32),
                pltpu.VMEM((4, 10, 10, 8, L), F32),
                pltpu.VMEM((6, 8, 8, L), F32),
                pltpu.VMEM((2, 8, 8, L), F32),
                pltpu.VMEM((6, 8, 8, 8, L), F32),
                pltpu.VMEM((8, 8, 8, L), F32),
                pltpu.VMEM((10, 10, 8, L), F32),
                pltpu.VMEM((6, L, L), BF16),
                pltpu.VMEM((4, 2, 2 * FACE, L), BF16),
                pltpu.VMEM((4, 2, 2 * FACE, L), BF16),
                pltpu.VMEM((4, 4, 8, 8, L), F32),
                pltpu.VMEM((7, 4, FACE // 2, 128), F32),
                pltpu.VMEM((7, 4, FACE // 2, 128), F32),
                pltpu.VMEM((4, FACE, 128), F32),
                pltpu.VMEM((4, FACE, 128), F32),
                pltpu.VMEM((1, 128), F32),
                pltpu.VMEM((n_grp, 1, 128), F32),
                pltpu.VMEM((1, 128), F32),
                pltpu.VMEM((n_dev, 1, 128), F32),
                pltpu.VMEM((n_dev, 1, 128), F32),
                pltpu.VMEM((n_dev, 1, 128), F32),
                pltpu.VMEM((4, n_dev, 8, 128), F32),
                pltpu.VMEM((4, n_dev, 8, 128), F32),
                pltpu.VMEM((4, 8, 8, BLOCKS), F32),
                pltpu.VMEM((4, n_grp, 8, BLOCKS), F32),
                pltpu.VMEM((10, 8, L), F32),
                pltpu.VMEM((4, 8, 8, L), F32),
                pltpu.VMEM((8, 8, L), F32),
                pltpu.VMEM((8, 8, L), F32),
                pltpu.VMEM((64, L), F32),
                pltpu.SemaphoreType.DMA((9,)),
                pltpu.SemaphoreType.DMA((8, 4)),
                pltpu.SemaphoreType.DMA((8, 4)),
                pltpu.SemaphoreType.DMA((5,)),
                pltpu.SemaphoreType.DMA((5,)),
                pltpu.SemaphoreType.DMA((6,)),
                pltpu.SemaphoreType.DMA((6,)),
                pltpu.SemaphoreType.REGULAR((2,)),
            ],
            compiler_params=pltpu.CompilerParams(
                collective_id=0, has_side_effects=True, vmem_limit_bytes=(64 * 1024 - 2048) * 1024
            ),
        )(
            velocity.reshape(3, 8, 8, 8, L),
            density.reshape(8, 8, 8, L),
            inverse_density.reshape(8, 8, 8, L),
            neighbours,
            leaf_layer.reshape(1, L),
            leaf_tile.reshape(1, L),
            leaf_block.reshape(1, L),
            samples,
        )
        return new_velocity.reshape(3, 512, L), rendered

    return jax.shard_map(
        step,
        mesh=mesh,
        in_specs=(
            P(None, None, ("grp", "dev")),
            P(None, ("grp", "dev")),
            P(None, ("grp", "dev")),
            P(None, ("grp", "dev")),
            P(("grp", "dev")),
            P(("grp", "dev"), None),
            P(("grp", "dev")),
            P(),
        ),
        out_specs=(P(None, None, ("grp", "dev")), P("dev", "grp")),
        check_vma=False,
    )
```

```python
import functools

import jax
import jax.numpy as jnp
from jax import lax
from jax.experimental import pallas as pl
from jax.experimental.pallas import tpu as pltpu
from jax.sharding import PartitionSpec as P

BLOCKS = 256
advect_step = 0.2
ray_step = 0.03
L = 256
FACE = 64
CAP = 16
F32 = jnp.float32
BF16 = jnp.bfloat16
MESH = pl.DeviceIdType.MESH


def parts(x):
    hi = x.astype(BF16)
    rest = x - hi.astype(F32)
    mid = rest.astype(BF16)
    low = (rest - mid.astype(F32)).astype(BF16)
    return jnp.concatenate([hi, mid, low], axis=0)


def joined(y):
    rows = y.shape[0] // 3
    return y[:rows] + y[rows : 2 * rows] + y[2 * rows :]


def pick(x, hot):
    return joined(jnp.dot(parts(x), hot, preferred_element_type=F32))


def pick_t(x, hot):
    return joined(
        lax.dot_general(parts(x), hot, (((1,), (1,)), ((), ())), preferred_element_type=F32)
    )


def spread(row, rows):
    return jnp.broadcast_to(row, (rows, row.shape[1]))


def hot_of(condition):
    return jnp.where(condition, 1.0, 0.0).astype(BF16)


def kernel(
    n_grp,
    n_dev,
    vel,
    dens,
    inv,
    nbr_any,
    layer_any,
    tile_any,
    block_any,
    samples,
    newv,
    rendered,
    nbr,
    rows_in,
    wp,
    vx,
    vy,
    vz,
    dn,
    hd,
    q,
    zf,
    zt,
    cs,
    dg,
    pp,
    gl,
    cp,
    er,
    rf,
    sb,
    rb,
    sbw,
    rbw,
    a1s,
    a1r,
    a2s,
    a2r,
    ids,
    idr,
    das,
    dar,
    pix,
    imr,
    sx,
    fy,
    sz,
    sd,
    col,
    in_sem,
    hs_sem,
    hr_sem,
    gs_sem,
    gr_sem,
    ds_sem,
    dr_sem,
    relay_sem,
):
    g = lax.axis_index("grp")
    d = lax.axis_index("dev")
    me = g * n_dev + d

    def grp_at(step):
        return (lax.rem(g + step, n_grp), d)

    def dev_at(step):
        return (g, lax.rem(d + step, n_dev))

    def torus_at(step_x, step_z):
        x = lax.rem(d // 8 + step_x, n_dev // 8)
        return (g, x * 8 + lax.rem(lax.rem(d, 8) + step_z, 8))

    two_away = [torus_at(0, 2), torus_at(0, 6), torus_at(2, 0)] + [
        torus_at(x, z) for x in (1, n_dev // 8 - 1) for z in (1, 7)
    ]
    greeted = [torus_at(0, 1), torus_at(0, 7), torus_at(1, 0), torus_at(n_dev // 8 - 1, 0)]
    greeted = [grp_at(i) for i in range(1, n_grp)] + greeted + two_away
    barrier = pltpu.get_barrier_semaphore()
    for who in greeted:
        pl.semaphore_signal(barrier, inc=1, device_id=who, device_id_type=MESH)

    def relay(number):
        for who in two_away:
            pl.semaphore_signal(
                relay_sem.at[number], inc=1, device_id=who, device_id_type=MESH
            )

    small = [
        pltpu.make_async_copy(nbr_any, nbr, in_sem.at[5]),
        pltpu.make_async_copy(tile_any, rows_in.at[0], in_sem.at[6]),
        pltpu.make_async_copy(block_any, rows_in.at[1], in_sem.at[7]),
        pltpu.make_async_copy(layer_any, rows_in.at[2], in_sem.at[8]),
    ]
    loads = [
        pltpu.make_async_copy(inv, wp.at[pl.ds(1, 8), pl.ds(1, 8)], in_sem.at[0]),
        pltpu.make_async_copy(vel.at[0], vx.at[pl.ds(1, 8)], in_sem.at[1]),
        pltpu.make_async_copy(vel.at[1], vy.at[:, pl.ds(1, 8)], in_sem.at[2]),
        pltpu.make_async_copy(dens, dn, in_sem.at[3]),
        pltpu.make_async_copy(vel.at[2], vz, in_sem.at[4]),
    ]
    for load in small + loads:
        load.start()

    to = [dev_at(1), dev_at(n_dev - 1), grp_at(1), grp_at(n_grp - 1)]
    sends = [d < n_dev - 1, d > 0, g < n_grp - 1, g > 0]
    takes = [d > 0, d < n_dev - 1, g > 0, g < n_grp - 1]

    for face in range(4):

        @pl.when(jnp.logical_not(takes[face]))
        def _():
            rb[:, face] = jnp.zeros((7, FACE // 2, 128), F32)
            rbw[face] = jnp.zeros((FACE, 128), F32)

    for load in small:
        load.wait()

    table = nbr[...]
    present = table >= 0
    local = present & ((table // L) == me)
    remote = present & ((table // L) != me)
    slot = table % L
    local_slot = jnp.where(local, slot, -1)
    remote_slot = jnp.where(remote, slot, -1)
    sub = lax.broadcasted_iota(jnp.int32, (L, L), 0)
    lane = lax.broadcasted_iota(jnp.int32, (L, L), 1)
    upper = hot_of(sub < lane)
    sub128 = lax.broadcasted_iota(jnp.int32, (2 * FACE, L), 0)
    tile_row = rows_in[0]
    tile_hot = hot_of(
        lax.broadcasted_iota(jnp.int32, (n_dev, L), 0) == spread(tile_row, n_dev)
    )
    before = jnp.dot(
        jnp.concatenate([tile_hot, hot_of(remote), jnp.zeros((10, L), BF16)], axis=0),
        upper,
        preferred_element_type=F32,
    )
    for face in range(4):
        out_face = face ^ 1
        place = before[n_dev + out_face : n_dev + out_face + 1].astype(jnp.int32)
        place = jnp.where(remote_slot[out_face : out_face + 1] >= 0, place, -1000)
        cp[face, 0] = hot_of(sub128 == spread(place, 2 * FACE))
        cp[face, 1] = hot_of(sub128 == spread(place + FACE, 2 * FACE))

    for load in loads[:4]:
        load.wait()

    def flat(x):
        return x.reshape(FACE, L)

    def cube(x):
        return x.reshape(8, 8, L)

    def halo(number, face):
        wide = number == 7
        return pltpu.make_async_remote_copy(
            src_ref=sbw.at[face] if wide else sb.at[number, face],
            dst_ref=rbw.at[face] if wide else rb.at[number, face],
            send_sem=hs_sem.at[1 if wide else 0, face],
            recv_sem=hr_sem.at[number, face],
            device_id=to[face],
            device_id_type=MESH,
        )

    def start_faces(number):
        for face in range(4):

            @pl.when(sends[face])
            def _():
                halo(number, face).start()

    def pack_faces(number, layers):
        for face in range(4):
            rows_64 = flat(layers[face])
            sb[number, face] = pick_t(rows_64[:32], cp[face, 0]) + pick_t(
                rows_64[32:], cp[face, 1]
            )

    def take_faces(number):
        for face in range(4):

            @pl.when(takes[face])
            def _():
                halo(number, face).wait_recv()

    def unpacked(number, face):
        got = parts(rb[number, face])
        top = joined(jnp.dot(got, er[face, 0], preferred_element_type=F32))
        bottom = joined(jnp.dot(got, er[face, 1], preferred_element_type=F32))
        return cube(jnp.concatenate([top, bottom], axis=0))

    first = [wp[8, 1:9], wp[1, 1:9], wp[1:9, 8], wp[1:9, 1]]
    second = [vx[8], vx[1], vy[:, 8], vy[:, 1]]
    for face in range(4):
        sbw[face] = pick_t(flat(first[face]), cp[face, 0]) + pick_t(
            flat(second[face]), cp[face, 1]
        )

    pl.semaphore_wait(barrier, len(greeted))
    start_faces(7)
    relay(0)
    pack_faces(6, [dn[7], dn[0], dn[:, 7], dn[:, 0]])
    start_faces(6)

    for face in range(6):
        gl[face] = hot_of(sub == spread(local_slot[face : face + 1], L))
    for face in range(4):
        mine = remote_slot[face : face + 1]
        occupied = jnp.sum(
            jnp.where(sub == spread(mine, L), 1.0, 0.0), axis=1, keepdims=True
        )
        rank = jnp.sum(
            jnp.where(sub < spread(mine, L), occupied, 0.0), axis=0, keepdims=True
        ).astype(jnp.int32)
        rank = jnp.where(mine >= 0, rank, -1000)
        er[face, 0] = hot_of(sub128 == spread(rank, 2 * FACE))
        er[face, 1] = hot_of(sub128 == spread(rank + FACE, 2 * FACE))

    rank = jnp.sum(
        jnp.where(tile_hot > 0, before[:n_dev], 0.0), axis=0, keepdims=True
    ).astype(jnp.int32)
    rows = n_dev * 8
    sub_key = lax.broadcasted_iota(jnp.int32, (rows, L), 0)
    first_key = jnp.where(rank < 8, tile_row * 8 + rank, -1)
    second_key = jnp.where(rank >= 8, tile_row * 8 + rank - 8, -1)
    slot_hot = jnp.concatenate(
        [hot_of(sub_key == spread(first_key, rows)), hot_of(sub_key == spread(second_key, rows))],
        axis=1,
    )

    def into_slots(values):
        empty = jnp.zeros_like(values)
        packed = jnp.concatenate(
            [
                jnp.concatenate([values, empty], axis=1),
                jnp.concatenate([empty, values], axis=1),
            ],
            axis=0,
        )
        return lax.dot_general(
            slot_hot, packed, (((1,), (1,)), ((), ())), preferred_element_type=F32
        )

    def to_dev(number, src, dst, i):
        return pltpu.make_async_remote_copy(
            src_ref=src,
            dst_ref=dst,
            send_sem=ds_sem.at[number],
            recv_sem=dr_sem.at[number],
            device_id=dev_at(i),
            device_id_type=MESH,
        )

    def to_grp(number, src, dst, i):
        return pltpu.make_async_remote_copy(
            src_ref=src,
            dst_ref=dst,
            send_sem=gs_sem.at[number],
            recv_sem=gr_sem.at[number],
            device_id=grp_at(i),
            device_id_type=MESH,
        )

    def all_dev(number):
        got = [idr, a2r, dar.at[0], dar.at[1], dar.at[2], dar.at[3]][number]
        got = got.at[pl.ds(1, n_dev - 1)]
        return to_dev(number, got, got, 1)

    def all_grp(number):
        got = [a1r, imr.at[0], imr.at[1], imr.at[2], imr.at[3]][number]
        got = got.at[pl.ds(1, n_grp - 1)]
        return to_grp(number, got, got, 1)

    def ids_copy(i):
        return to_dev(0, ids.at[lax.rem(d + i, n_dev)], idr.at[i], i)

    def sum_copy(i):
        return to_dev(1, a2s, a2r.at[i], i)

    def data_copy(which, i):
        return to_dev(2 + which, das.at[which, lax.rem(d + i, n_dev)], dar.at[which, i], i)

    marked = jnp.where(
        lax.broadcasted_iota(jnp.int32, (128, L), 0) == spread(rank, 128),
        spread(rows_in[1], 128),
        0,
    )
    marked = lax.dot_general(
        tile_hot,
        marked.astype(F32).astype(BF16),
        (((1,), (1,)), ((), ())),
        preferred_element_type=F32,
    )
    for t in range(n_dev):
        ids[t] = marked[t : t + 1]

    idr[0] = ids[d]
    limit = jnp.zeros((1, L), jnp.int32)
    for t in range(n_dev):
        limit = jnp.where(tile_row == t, samples[t], limit)
    marched = jnp.where(rows_in[2] < limit, ray_step, 0.0)

    loads[4].wait()

    def fill_z_tables(read):
        @pl.loop(0, 8)
        def _(i):
            for j in range(8):
                c = read(i, j)
                zt[0, i, j : j + 1, :] = c[7:8]
                zt[1, i, j : j + 1, :] = c[0:1]

    def local_faces(k):
        q[k, 0, 1:9] = cube(pick(flat(q[k, 8, 1:9]), gl[0]))
        q[k, 9, 1:9] = cube(pick(flat(q[k, 1, 1:9]), gl[1]))
        q[k, 1:9, 0] = cube(pick(flat(q[k, 1:9, 8]), gl[2]))
        q[k, 1:9, 9] = cube(pick(flat(q[k, 1:9, 1]), gl[3]))
        zf[2 * k] = cube(pick(flat(zt[0]), gl[4]))
        zf[2 * k + 1] = cube(pick(flat(zt[1]), gl[5]))

    fill_z_tables(lambda i, j: vz[i, j])
    zf[2] = cube(pick(flat(zt[0]), gl[4]))
    zf[3] = cube(pick(flat(zt[1]), gl[5]))
    fill_z_tables(lambda i, j: wp[i + 1, j + 1])
    absent = [jnp.where(present[face : face + 1], 0.0, 1.0) for face in range(6)]
    zf[0] = cube(pick(flat(zt[0]), gl[4]))
    zf[1] = cube(pick(flat(zt[1]), gl[5]))

    def both(first, second, face):
        return pick(jnp.concatenate([flat(first), flat(second)], axis=0), gl[face])

    near_local = [
        both(wp[8, 1:9], vx[8], 0),
        both(wp[1, 1:9], vx[1], 1),
        both(wp[1:9, 8], vy[:, 8], 2),
        both(wp[1:9, 1], vy[:, 1], 3),
    ]
    k_id = lax.broadcasted_iota(jnp.int32, (8, L), 0)
    at_low = k_id == 0
    at_high = k_id == 7
    zero = jnp.zeros((8, L), F32)

    def beside_z(c, low, high):
        return (
            jnp.where(at_low, low, pltpu.roll(c, 1, 0)),
            jnp.where(at_high, high, pltpu.roll(c, 7, 0)),
        )

    def start(i, columns):
        for j in columns:
            c = wp[i + 1, j + 1]
            low, high = beside_z(
                c,
                zf[0, i, j : j + 1] + absent[4] * c[0:1],
                zf[1, i, j : j + 1] + absent[5] * c[7:8],
            )
            near = [wp[i, j + 1], wp[i + 2, j + 1], wp[i + 1, j], wp[i + 1, j + 2], low, high]
            coupling = [0.5 * (c + value) for value in near]
            diagonal = (
                coupling[0] + coupling[1] + coupling[2] + coupling[3] + coupling[4] + coupling[5]
            )
            inverse = 1.0 / diagonal
            dg[i, j] = diagonal
            for face in range(6):
                cs[face, i, j] = coupling[face] * inverse
            v = vz[i, j]
            low, high = beside_z(v, zf[2, i, j : j + 1], zf[3, i, j : j + 1])
            source = -0.5 * (
                (vx[i + 2, j] - vx[i, j]) + (vy[i, j + 2] - vy[i, j]) + (high - low)
            )
            q[0, i + 1, j + 1] = source * inverse

    @pl.loop(1, 7)
    def _(i):
        start(i, range(1, 7))

    take_faces(7)
    pl.semaphore_wait(relay_sem.at[0], len(two_away))
    relay(1)
    for face in range(4):
        got = parts(rbw[face])
        w_far = joined(jnp.dot(got, er[face, 0], preferred_element_type=F32))
        v_far = joined(jnp.dot(got, er[face, 1], preferred_element_type=F32))
        rf[face, 0] = cube(w_far)
        rf[face, 1] = cube(v_far)
        w_near = cube(near_local[face][:FACE] + w_far)
        v_near = cube(near_local[face][FACE:] + v_far)
        if face == 0:
            wp[0, 1:9] = w_near + absent[face] * wp[1, 1:9]
            vx[0] = v_near
        elif face == 1:
            wp[9, 1:9] = w_near + absent[face] * wp[8, 1:9]
            vx[9] = v_near
        elif face == 2:
            wp[1:9, 0] = w_near + absent[face] * wp[1:9, 1]
            vy[:, 0] = v_near
        else:
            wp[1:9, 9] = w_near + absent[face] * wp[1:9, 8]
            vy[:, 9] = v_near

    for i in (0, 7):
        start(i, range(8))

    @pl.loop(1, 7)
    def _(i):
        start(i, (0, 7))

    def send_field(k):
        pack_faces(k, [q[k, 8, 1:9], q[k, 1, 1:9], q[k, 1:9, 8], q[k, 1:9, 1]])
        start_faces(k)

    def send_deep(k):
        pack_faces(3 + k, [q[k, 7, 1:9], q[k, 2, 1:9], q[k, 1:9, 7], q[k, 1:9, 2]])
        start_faces(3 + k)

    send_field(0)

    def apply_local(k):
        @pl.loop(0, 8)
        def _(i):
            for j in range(8):
                c = q[k, i + 1, j + 1]
                low, high = beside_z(c, zf[2 * k, i, j : j + 1], zf[2 * k + 1, i, j : j + 1])
                near = [
                    q[k, i, j + 1],
                    q[k, i + 2, j + 1],
                    q[k, i + 1, j],
                    q[k, i + 1, j + 2],
                    low,
                    high,
                ]
                value = c
                for face in range(6):
                    value = value - cs[face, i, j] * near[face]
                q[k + 1, i + 1, j + 1] = value

    def add_far(k):
        far = [unpacked(k, face) for face in range(4)]
        q[k, 0, 1:9] += far[0]
        q[k, 9, 1:9] += far[1]
        q[k, 1:9, 0] += far[2]
        q[k, 1:9, 9] += far[3]
        q[k + 1, 1, 1:9] -= cs[0, 0] * far[0]
        q[k + 1, 8, 1:9] -= cs[1, 7] * far[1]
        q[k + 1, 1:9, 1] -= cs[2, :, 0] * far[2]
        q[k + 1, 1:9, 8] -= cs[3, :, 7] * far[3]

    def products(k):
        def body(i, totals):
            even, odd = totals
            for j in range(8):
                c = q[k, i + 1, j + 1]
                scaled = dg[i, j] * c
                even = even + c * scaled
                odd = odd + q[k + 1, i + 1, j + 1] * scaled
            return even, odd

        return lax.fori_loop(0, 8, body, (zero, zero))

    def read_z(k):
        return lambda i, j: q[k, i + 1, j + 1]

    def flux_local(which):
        base = which == 0
        k = which - 1

        @pl.loop(0, 8)
        def _(i):
            sum_x = zero
            sum_z = zero
            sum_d = zero
            for j in range(8):
                if base:
                    smoke = dn[i, j]
                    sum_x = sum_x + smoke * vx[i + 1, j]
                    sum_z = sum_z + smoke * vz[i, j]
                    sum_d = sum_d + smoke
                    if j == 0:
                        fy[1, i] = smoke * vy[i, 1]
                    if j == 7:
                        fy[2, i] = smoke * vy[i, 8]
                else:
                    half = hd[i, j]
                    low, high = beside_z(
                        q[k, i + 1, j + 1], zf[2 * k, i, j : j + 1], zf[2 * k + 1, i, j : j + 1]
                    )
                    sum_x = sum_x + half * (q[k, i + 2, j + 1] - q[k, i, j + 1])
                    sum_z = sum_z + half * (high - low)
                    if j == 0:
                        fy[1, i] = half * (q[k, i + 1, 2] - q[k, i + 1, 0])
                    if j == 7:
                        fy[2, i] = half * (q[k, i + 1, 9] - q[k, i + 1, 7])
            sx[i + 1] = sum_x
            sz[i] = sum_z
            if base:
                sd[i] = sum_d
            zt[0, 0, pl.ds(i, 1), :] = sum_z[7:8]
            zt[1, 0, pl.ds(i, 1), :] = sum_z[0:1]

        def pick_8(x, hot):
            return pick(jnp.concatenate([x, x], axis=0), hot)[:8]

        sx[0] = pick_8(sx[8], gl[0])
        sx[9] = pick_8(sx[1], gl[1])
        fy[0] = cube(pick(flat(fy[2]), gl[2]))
        fy[3] = cube(pick(flat(fy[1]), gl[3]))
        z_low = pick_8(zt[0, 0], gl[4])
        z_high = pick_8(zt[1, 0], gl[5])
        for i in range(8):
            low, high = beside_z(sz[i], z_low[i : i + 1], z_high[i : i + 1])
            sz[i] = high - low

    def flux_finish(which):
        base = which == 0
        k = which - 1

        def far(face):
            if base:
                return rf[face, 2] * rf[face, 1]
            deep = unpacked(3 + k, face)
            change = [
                lambda: q[k, 1, 1:9] - deep,
                lambda: deep - q[k, 8, 1:9],
                lambda: q[k, 1:9, 1] - deep,
                lambda: deep - q[k, 1:9, 8],
            ][face]()
            return rf[face, 3] * change

        if not base:
            take_faces(3 + k)
        sx[0] += jnp.sum(far(0), axis=0)
        sx[9] += jnp.sum(far(1), axis=0)
        fy[0] += far(2)
        fy[3] += far(3)

        for i in range(8):
            change = (
                (sx[i + 2] - sx[i])
                + ((fy[3, i] + fy[2, i]) - (fy[1, i] + fy[0, i]))
                + sz[i]
            )
            change = (0.5 * advect_step) * change
            col[8 * i : 8 * i + 8] = marched * (sd[i] - change if base else change)
        columns = parts(col[...])
        total = into_slots(columns[:64]) + into_slots(columns[64:128]) + into_slots(columns[128:])
        das[which] = total.reshape(n_dev, 8, 128)
        dar[which, 0] = das[which, d]

    def send_columns(which):
        @pl.loop(1, n_dev, unroll=True)
        def _(i):
            data_copy(which, i).start()

    def flux_columns(which):
        flux_local(which)
        flux_finish(which)

    send_deep(0)
    fill_z_tables(read_z(0))
    local_faces(0)
    apply_local(0)
    take_faces(6)
    for face in range(4):
        smoke_far = unpacked(6, face)
        rf[face, 2] = smoke_far
        rf[face, 3] = 0.5 * smoke_far * rf[face, 0]

    @pl.loop(0, 8)
    def _(i):
        for j in range(8):
            hd[i, j] = 0.5 * dn[i, j] * wp[i + 1, j + 1]

    flux_columns(0)
    pl.semaphore_wait(relay_sem.at[1], len(two_away))

    @pl.loop(1, n_dev, unroll=True)
    def _(i):
        ids_copy(i).start()

    send_columns(0)
    take_faces(0)
    add_far(0)
    send_field(1)

    send_deep(1)
    flux_columns(1)
    send_columns(1)
    fill_z_tables(read_z(1))
    local_faces(1)
    apply_local(1)
    m0, m1 = products(0)
    take_faces(1)
    add_far(1)
    send_field(2)

    send_deep(2)
    flux_columns(2)
    send_columns(2)
    fill_z_tables(read_z(2))
    local_faces(2)
    apply_local(2)
    m2, m3 = products(1)
    m4, m5 = products(2)
    flux_local(3)

    take_faces(2)
    far = [unpacked(2, face) for face in range(4)]
    for j in range(8):
        sx[1] -= hd[0, j] * far[0][j]
        sx[8] += hd[7, j] * far[1][j]
        fy[1, j] -= hd[j, 0] * far[2][j]
        fy[2, j] += hd[j, 7] * far[3][j]
    flux_finish(3)
    send_columns(3)

    m5_far = zero
    for j in range(8):
        m5_far = m5_far + dg[0, j] * cs[0, 0, j] * far[0][j] * q[2, 1, j + 1]
        m5_far = m5_far + dg[7, j] * cs[1, 7, j] * far[1][j] * q[2, 8, j + 1]
        m5_far = m5_far + dg[j, 0] * cs[2, j, 0] * far[2][j] * q[2, j + 1, 1]
        m5_far = m5_far + dg[j, 7] * cs[3, j, 7] * far[3][j] * q[2, j + 1, 8]

    moments = [m0, m1, m2, m3, m4, m5 - m5_far]
    lanes = lax.broadcasted_iota(jnp.int32, (1, 128), 1)
    row = jnp.zeros((1, 128), F32)
    for k in range(6):
        line = jnp.sum(moments[k], axis=0, keepdims=True)
        line = jnp.sum(line[:, :128] + line[:, 128:], axis=1, keepdims=True)
        row = jnp.where(lanes == k, line, row)
    a1s[...] = row
    for i in range(1, n_grp):
        to_grp(0, a1s, a1r.at[i], i).start()

    q[2, 0, 1:9] += far[0]
    q[2, 9, 1:9] += far[1]
    q[2, 1:9, 0] += far[2]
    q[2, 1:9, 9] += far[3]
    partial = a1s[...]
    all_grp(0).wait_recv()
    for i in range(1, n_grp):
        partial = partial + a1r[i]
    a2s[...] = partial

    @pl.loop(1, n_dev, unroll=True)
    def _(i):
        sum_copy(i).start()

    all_dev(0).wait_recv()

    marks = jnp.concatenate([spread(idr[i], 8) for i in range(n_dev)], axis=0)
    mark_lane = lax.broadcasted_iota(jnp.int32, (rows, 128), 1)
    mark_row = lax.broadcasted_iota(jnp.int32, (rows, 128), 0) % 8
    first_mark = jnp.sum(jnp.where(mark_lane == mark_row, marks, 0.0), axis=1, keepdims=True)
    second_mark = jnp.sum(
        jnp.where(mark_lane == mark_row + 8, marks, 0.0), axis=1, keepdims=True
    )
    lane_b = lax.broadcasted_iota(jnp.int32, (rows, BLOCKS), 1).astype(F32)
    first_hot = hot_of(first_mark == lane_b)
    second_hot = hot_of(second_mark == lane_b)

    def image_copy(which, i):
        return to_grp(1 + which, pix.at[which, lax.rem(g + i, n_grp)], imr.at[which, i], i)

    def send_pixels(which):
        got = parts(dar[which].reshape(rows, 128).T)
        image = joined(jnp.dot(got, first_hot, preferred_element_type=F32))[:64]
        image = image + joined(jnp.dot(got, second_hot, preferred_element_type=F32))[64:]
        pix[which] = image.reshape(8, 8, BLOCKS)
        for i in range(1, n_grp):
            image_copy(which, i).start()

    for which in range(3):
        all_dev(2 + which).wait_recv()
        send_pixels(which)

    all_dev(5).wait_recv()

    send_pixels(3)

    all_dev(1).wait_recv()

    whole = partial
    for i in range(1, n_dev):
        whole = whole + a2r[i]
    m = [
        jnp.broadcast_to(
            jnp.sum(jnp.where(lanes == k, whole, 0.0), axis=1, keepdims=True), (1, 128)
        )
        for k in range(6)
    ]
    l10 = m[2] / m[1]
    l20 = m[3] / m[1]
    d1 = m[3] - l10 * m[2]
    t21 = m[4] - l20 * m[2]
    l21 = t21 / d1
    d2 = m[5] - l20 * m[3] - l21 * t21
    y1 = m[1] - l10 * m[0]
    y2 = m[2] - l20 * m[0] - l21 * y1
    c2 = y2 / d2
    c1 = y1 / d1 - l21 * c2
    c0 = m[0] / m[1] - l10 * c1 - l20 * c2
    coefs = [jnp.concatenate([spread(c, 8), spread(c, 8)], axis=1) for c in (c0, c1, c2)]
    def mixed(read):
        return coefs[0] * read(0) + coefs[1] * read(1) + coefs[2] * read(2)

    @pl.loop(0, 8)
    def _(i):
        pp[0, i + 1] = mixed(lambda k: q[k, 0, i + 1])
        pp[9, i + 1] = mixed(lambda k: q[k, 9, i + 1])
        zf[0, i] = mixed(lambda k: zf[2 * k, i])
        zf[1, i] = mixed(lambda k: zf[2 * k + 1, i])
        for j in range(10):
            pp[i + 1, j] = mixed(lambda k: q[k, i + 1, j])

    @pl.loop(0, 8)
    def _(i):
        for j in range(8):
            c = pp[i + 1, j + 1]
            low, high = beside_z(c, zf[0, i, j : j + 1], zf[1, i, j : j + 1])
            half = 0.5 * wp[i + 1, j + 1]
            newv[0, i, j] = vx[i + 1, j] - half * (pp[i + 2, j + 1] - pp[i, j + 1])
            newv[1, i, j] = vy[i, j + 1] - half * (pp[i + 1, j + 2] - pp[i + 1, j])
            newv[2, i, j] = vz[i, j] - half * (high - low)

    for face in range(4):

        @pl.when(sends[face])
        def _():
            halo(7, face).wait_send()
            pltpu.make_async_remote_copy(
                src_ref=sb.at[:, face],
                dst_ref=rb.at[:, face],
                send_sem=hs_sem.at[0, face],
                recv_sem=hr_sem.at[0, face],
                device_id=to[face],
                device_id_type=MESH,
            ).wait_send()

    all_grp(0).wait_send()

    for number in range(6):
        all_dev(number).wait_send()

    optical = zero
    for which in range(4):
        layer_sum = pix[which, g]
        all_grp(1 + which).wait_recv()
        for i in range(1, n_grp):
            layer_sum = layer_sum + imr[which, i]
        optical = optical + (layer_sum if which == 0 else coefs[which - 1] * layer_sum)
    shade = 1.0 - jnp.exp(-optical)
    for row in range(8):
        rendered[:, BLOCKS * row : BLOCKS * (row + 1)] = shade[row : row + 1]
    for which in range(4):
        all_grp(1 + which).wait_send()


def solution(mesh):
    n_grp, n_dev = mesh.shape["grp"], mesh.shape["dev"]

    def step(
        velocity, density, inverse_density, neighbours, leaf_layer, leaf_tile, leaf_block, samples
    ):
        vmem = pl.BlockSpec(memory_space=pltpu.VMEM)
        anywhere = pl.BlockSpec(memory_space=pl.ANY)
        smem = pl.BlockSpec(memory_space=pltpu.SMEM)
        new_velocity, rendered = pl.pallas_call(
            functools.partial(kernel, n_grp, n_dev),
            out_shape=(
                pltpu.VMEM((3, 8, 8, 8, L), F32),
                pltpu.VMEM((1, 8 * BLOCKS), F32),
            ),
            in_specs=[anywhere] * 7 + [smem],
            out_specs=(vmem, vmem),
            scratch_shapes=[
                pltpu.VMEM((6, L), jnp.int32),
                pltpu.VMEM((3, 1, L), jnp.int32),
                pltpu.VMEM((10, 10, 8, L), F32),
                pltpu.VMEM((10, 8, 8, L), F32),
                pltpu.VMEM((8, 10, 8, L), F32),
                pltpu.VMEM((8, 8, 8, L), F32),
                pltpu.VMEM((8, 8, 8, L), F32),
                pltpu.VMEM((8, 8, 8, L), F32),
                pltpu.VMEM((4, 10, 10, 8, L), F32),
                pltpu.VMEM((6, 8, 8, L), F32),
                pltpu.VMEM((2, 8, 8, L), F32),
                pltpu.VMEM((6, 8, 8, 8, L), F32),
                pltpu.VMEM((8, 8, 8, L), F32),
                pltpu.VMEM((10, 10, 8, L), F32),
                pltpu.VMEM((6, L, L), BF16),
                pltpu.VMEM((4, 2, 2 * FACE, L), BF16),
                pltpu.VMEM((4, 2, 2 * FACE, L), BF16),
                pltpu.VMEM((4, 4, 8, 8, L), F32),
                pltpu.VMEM((7, 4, FACE // 2, 128), F32),
                pltpu.VMEM((7, 4, FACE // 2, 128), F32),
                pltpu.VMEM((4, FACE, 128), F32),
                pltpu.VMEM((4, FACE, 128), F32),
                pltpu.VMEM((1, 128), F32),
                pltpu.VMEM((n_grp, 1, 128), F32),
                pltpu.VMEM((1, 128), F32),
                pltpu.VMEM((n_dev, 1, 128), F32),
                pltpu.VMEM((n_dev, 1, 128), F32),
                pltpu.VMEM((n_dev, 1, 128), F32),
                pltpu.VMEM((4, n_dev, 8, 128), F32),
                pltpu.VMEM((4, n_dev, 8, 128), F32),
                pltpu.VMEM((4, 8, 8, BLOCKS), F32),
                pltpu.VMEM((4, n_grp, 8, BLOCKS), F32),
                pltpu.VMEM((10, 8, L), F32),
                pltpu.VMEM((4, 8, 8, L), F32),
                pltpu.VMEM((8, 8, L), F32),
                pltpu.VMEM((8, 8, L), F32),
                pltpu.VMEM((64, L), F32),
                pltpu.SemaphoreType.DMA((9,)),
                pltpu.SemaphoreType.DMA((2, 4)),
                pltpu.SemaphoreType.DMA((8, 4)),
                pltpu.SemaphoreType.DMA((5,)),
                pltpu.SemaphoreType.DMA((5,)),
                pltpu.SemaphoreType.DMA((6,)),
                pltpu.SemaphoreType.DMA((6,)),
                pltpu.SemaphoreType.REGULAR((2,)),
            ],
            compiler_params=pltpu.CompilerParams(
                collective_id=0, has_side_effects=True, vmem_limit_bytes=(64 * 1024 - 2048) * 1024
            ),
        )(
            velocity.reshape(3, 8, 8, 8, L),
            density.reshape(8, 8, 8, L),
            inverse_density.reshape(8, 8, 8, L),
            neighbours,
            leaf_layer.reshape(1, L),
            leaf_tile.reshape(1, L),
            leaf_block.reshape(1, L),
            samples,
        )
        return new_velocity.reshape(3, 512, L), rendered

    return jax.shard_map(
        step,
        mesh=mesh,
        in_specs=(
            P(None, None, ("grp", "dev")),
            P(None, ("grp", "dev")),
            P(None, ("grp", "dev")),
            P(None, ("grp", "dev")),
            P(("grp", "dev")),
            P(("grp", "dev"), None),
            P(("grp", "dev")),
            P(),
        ),
        out_specs=(P(None, None, ("grp", "dev")), P("dev", "grp")),
        check_vma=False,
    )
```
